128 devices in a mesh: section: 2 (over x_hi), dp: 16 (over y, z), tensor: 4 (over x_lo, core).
Axes of the slice: x: 4 (x_hi: 2, x_lo: 2; x = x_hi * 2 + x_lo), y: 4, z: 4, core: 2. Of those that a mesh axis runs over, the one named last changes fastest.
Arguments:
- inputs: bfloat16 [2, 2048, 1536], P(None, ('dp', 'tensor')), may hold values from -6 to 6
- cotangent: bfloat16 [2, 2048, 1536], P(None, ('dp', 'tensor')), may hold values from -6 to 6
- segments: int32 [2, 2048], replicated, may hold values from 0 to 7, as said below
- gain_one: bfloat16 [2, 1536], P('section', ('dp', 'tensor')), may hold values from 0.5 to 1.5
- w_query: bfloat16 [2, 1536, 1536], P('section', 'dp', 'tensor'), may hold values from -0.15625 to 0.15625
- b_query: bfloat16 [2, 1536], P('section', 'tensor'), may hold values from -3 to 3
- w_keyval: bfloat16 [2, 1536, 512], P('section', ('dp', 'tensor')), may hold values from -0.15625 to 0.15625
- b_keyval: bfloat16 [2, 512], P('section', ('dp', 'tensor')), may hold values from -3 to 3
- w_out: bfloat16 [2, 1536, 1536], P('section', 'tensor', 'dp'), may hold values from -1.25 to 1.25
- gain_two: bfloat16 [2, 1536], P('section', ('dp', 'tensor')), may hold values from 0.5 to 1.5
- w_gate: bfloat16 [2, 1536, 8960], P('section', 'dp', 'tensor'), may hold values from -0.15625 to 0.15625
- w_up: bfloat16 [2, 1536, 8960], P('section', 'dp', 'tensor'), may hold values from -0.15625 to 0.15625
- w_down: bfloat16 [2, 8960, 1536], P('section', 'tensor', 'dp'), may hold values from -0.0625 to 0.0625
Outputs:
- section_out: bfloat16 [2, 2, 2048, 1536], P('section', None, ('dp', 'tensor'))
- input_grad: bfloat16 [2, 2, 2048, 1536], P('section', None, ('dp', 'tensor'))
- grad_gain_one: float32 [2, 1536], P('section', ('dp', 'tensor'))
- grad_w_query: float32 [2, 1536, 1536], P('section', 'dp', 'tensor')
- grad_b_query: float32 [2, 1536], P('section', 'tensor')
- grad_w_keyval: float32 [2, 1536, 512], P('section', ('dp', 'tensor'))
- grad_b_keyval: float32 [2, 512], P('section', ('dp', 'tensor'))
- grad_w_out: float32 [2, 1536, 1536], P('section', 'tensor', 'dp')
- grad_gain_two: float32 [2, 1536], P('section', ('dp', 'tensor'))
- grad_w_gate: float32 [2, 1536, 8960], P('section', 'dp', 'tensor')
- grad_w_up: float32 [2, 1536, 8960], P('section', 'dp', 'tensor')
- grad_w_down: float32 [2, 8960, 1536], P('section', 'tensor', 'dp')
The draws below stay inside these ranges and needn't reach their ends.
Inputs may be any that keep to these rules, and one draw needn't show every extreme that they name: `segments`: segment numbers start at 0 and rise by one at each new document. In one micro-batch, drawn from the seed, one document covers the whole sequence; in the others eight documents of 128 to 384 tokens follow one another.
All inputs are finite; a program needn't handle non-finite values.
Results may differ from the reference program's by a relative error of at most 0.025.
Values may be sent and summed in bfloat16 or wider, within the bound.
No kernel may reach another device: no remote copies, remote signals or barrier semaphores. Data moves between devices by JAX's collectives and lax.ppermute only.
A program may use at most 192 MiB of HBM per device.

```python
import jax
import jax.numpy as jnp
from jax import lax

D = 1536
HQ = 12
KVH = 2
HD = 128
FF = 8960
MB = 2
SEQ = 2048
QD = 1536
KVW = 512
LAYERS = 2
N_TENSOR = 4


def draw_segments(key, part):
    key = jax.random.fold_in(key, 7)
    offset_key, whole_key = jax.random.split(key)
    step_len = SEQ // 8
    offsets = jax.random.randint(offset_key, (MB, 7), 0, step_len // 2)
    cuts = (jnp.arange(1, 8, dtype=jnp.int32)[None, :] * step_len + offsets).astype(jnp.int32)
    position = jnp.arange(SEQ, dtype=jnp.int32)
    numbers = jnp.sum((cuts[:, None, :] <= position[None, :, None]).astype(jnp.int32), axis=2)
    whole_batch = jax.random.randint(whole_key, (), 0, MB)
    single = (jnp.arange(MB, dtype=jnp.int32) == whole_batch)[:, None]
    return jnp.where(single, 0, numbers).astype(jnp.int32)


def steps_of(key, shape, pieces, low, high):
    gain = 1.0
    for axis_at, parts in pieces:
        draws = jax.random.uniform(jax.random.fold_in(jax.random.fold_in(key, 6), axis_at), (parts,), jnp.float32, low / len(pieces), high / len(pieces))
        gain = gain * jnp.repeat(jnp.exp(draws), shape[axis_at] // parts).reshape((-1,) + (1,) * (len(shape) - 1 - axis_at))
    return gain


def bell_draw(rng, shape, deviation, limit, cuts=(), kind=jnp.bfloat16):
    values = jax.random.normal(rng, shape, jnp.float32) * deviation
    if len(cuts) > 0:
        values = steps_of(rng, shape, cuts, -0.22, 0.18) * values
    return jnp.clip(values, min=-limit, max=limit).astype(kind)


def setup_inputs(seed: int = 0) -> dict:
    splits = jax.random.split(jax.random.key(seed), 14)
    return {
        "inputs": bell_draw(splits[0], (MB, SEQ, D), 1.0, 6.0, ((1, 64),)),
        "cotangent": bell_draw(splits[1], (MB, SEQ, D), 1.0, 6.0, ((1, 64),)),
        "segments": draw_segments(jax.random.fold_in(splits[13], 71), 0),
        "gain_one": jnp.clip(1.0 + 0.1 * jax.random.normal(splits[3], (LAYERS, D), jnp.float32), 0.5, 1.5).astype(jnp.bfloat16),
        "w_query": bell_draw(splits[4], (LAYERS, D, QD), D ** -0.5, 0.15625, ((0, 2), (1, 16), (2, 4))),
        "b_query": bell_draw(splits[5], (LAYERS, QD), 0.5, 3.0, ((0, 2), (1, 4))),
        "w_keyval": bell_draw(splits[6], (LAYERS, D, KVW), D ** -0.5, 0.15625, ((0, 2), (1, 64))),
        "b_keyval": bell_draw(splits[7], (LAYERS, KVW), 0.5, 3.0, ((0, 2), (1, 64))),
        "w_out": bell_draw(splits[8], (LAYERS, QD, D), (max(QD // 64, 1)) ** -0.5, 1.25, ((0, 2), (1, 4), (2, 16))),
        "gain_two": jnp.clip(1.0 + 0.1 * jax.random.normal(splits[9], (LAYERS, D), jnp.float32), 0.5, 1.5).astype(jnp.bfloat16),
        "w_gate": bell_draw(splits[10], (LAYERS, D, FF), D ** -0.5, 0.15625, ((0, 2), (1, 16), (2, 4))),
        "w_up": bell_draw(splits[11], (LAYERS, D, FF), D ** -0.5, 0.15625, ((0, 2), (1, 16), (2, 4))),
        "w_down": bell_draw(splits[12], (LAYERS, FF, D), FF ** -0.5, 0.0625, ((0, 2), (1, 4), (2, 16))),
    }


EPS = 1e-06
NEG = -1e+30
THETA = 1000000.0

@jax.custom_vjp
def low(v):
    return lax.optimization_barrier(v.astype(jnp.bfloat16)).astype(jnp.float32)

@jax.custom_vjp
def low_back(v):
    return v

def low_keep(v):
    return (low(v), None)

def low_pass(kept, grad):
    return (grad,)

def back_keep(v):
    return (v, None)

def back_low(kept, grad):
    return (low(grad),)
low.defvjp(low_keep, low_pass)
low_back.defvjp(back_keep, back_low)

def high_dot(left_side, right_side):
    return jnp.dot(left_side, right_side, precision=lax.Precision.HIGHEST, preferred_element_type=jnp.float32)

def rms_rows(values):
    return values * lax.rsqrt(lax.optimization_barrier(jnp.mean(values * values, axis=-1, keepdims=True)) + EPS)

def rotate(values, cosine, sine_part):
    halfway = values.shape[-1] // 2
    first_half = values[..., :halfway]
    second_half = values[..., halfway:]
    return jnp.concatenate([first_half * cosine - second_half * sine_part, second_half * cosine + first_half * sine_part], axis=-1)

def attend_block(query_block, pos_block, seg_block, key_copies, value_copies, positions, segments_row):
    scores = jnp.einsum('qjhd,jkd->jhqk', query_block, key_copies, precision=lax.Precision.HIGHEST) * HD ** (-0.5)
    scores = low_back(scores)
    allowed = (segments_row[None, :] == seg_block[:, None]) & (positions[None, :] <= pos_block[:, None])
    scores = jnp.where(allowed[None, None], scores, NEG)
    row_top = lax.optimization_barrier(jnp.max(scores, axis=-1, keepdims=True))
    weights_exp = jnp.exp(scores - row_top)
    probabilities = low(weights_exp / lax.optimization_barrier(jnp.sum(weights_exp, axis=-1, keepdims=True)))
    return jnp.einsum('jhqk,jkd->qjhd', probabilities, value_copies, precision=lax.Precision.HIGHEST)

def run_layer(values, weights, angle_cos, angle_sin, positions, segments_row):
    gain_first, w_query, b_query, w_keyval, b_keyval, w_out, gain_second, w_gate, w_up, w_down = weights
    heads_local = HQ // N_TENSOR
    group_size = HQ // KVH
    normed = low(rms_rows(values) * gain_first)
    query_pre = (high_dot(normed, w_query) + b_query).reshape(SEQ, N_TENSOR, heads_local, HD)
    query_rot = low(rotate(low_back(query_pre), angle_cos[:, None, None, :], angle_sin[:, None, None, :]))
    keyval = high_dot(normed, w_keyval) + b_keyval
    key_pre = keyval[:, :KVH * HD].reshape(SEQ, KVH, HD)
    value_pre = keyval[:, KVH * HD:].reshape(SEQ, KVH, HD)
    key_list = []
    value_list = []
    for member in range(N_TENSOR):
        head_index = member * heads_local // group_size
        key_list.append(low(rotate(low_back(key_pre[:, head_index]), angle_cos, angle_sin)))
        value_list.append(low(low_back(value_pre[:, head_index])))
    key_copies = jnp.stack(key_list)
    value_copies = jnp.stack(value_list)
    block_rows = min(512, SEQ)
    blocks = SEQ // block_rows

    def block_fn(batch_item):
        return attend_block(batch_item[0], batch_item[1], batch_item[2], key_copies, value_copies, positions, segments_row)
    attended = lax.map(jax.checkpoint(block_fn), (query_rot.reshape(blocks, block_rows, N_TENSOR, heads_local, HD), positions.reshape(blocks, block_rows), segments_row.reshape(blocks, block_rows)))
    attended = low(low_back(attended.reshape(SEQ, HQ * HD)))
    mixed_rows = values + low_back(high_dot(attended, w_out))
    second = low(rms_rows(mixed_rows) * gain_second)
    gate_proj = low_back(high_dot(second, w_gate))
    up_proj = low_back(high_dot(second, w_up))
    hidden = low(jax.nn.silu(gate_proj) * up_proj)
    return mixed_rows + high_dot(hidden, w_down)

def forward(params, probe_zero, values, segments_row):
    positions = jnp.arange(SEQ, dtype=jnp.int32)
    inverse_freq = THETA ** (-(jnp.arange(HD // 2, dtype=jnp.float32) * 2.0) / HD)
    angles = positions.astype(jnp.float32)[:, None] * inverse_freq[None, :]
    angle_cos = jnp.cos(angles)
    angle_sin = jnp.sin(angles)
    first_weights = tuple((weight[0] for weight in params))
    second_weights = tuple((weight[1] for weight in params))
    first_out = run_layer(values, first_weights, angle_cos, angle_sin, positions, segments_row)
    passed = low_back(low(first_out)) + probe_zero
    final_out = run_layer(passed, second_weights, angle_cos, angle_sin, positions, segments_row)
    return (final_out, low(first_out))

def reference(inputs, cotangent, segments, gain_one, w_query, b_query, w_keyval, b_keyval, w_out, gain_two, w_gate, w_up, w_down):
    params = tuple((weight.astype(jnp.float32) for weight in (gain_one, w_query, b_query, w_keyval, b_keyval, w_out, gain_two, w_gate, w_up, w_down)))

    def one_batch(totals, batch_item):
        input_row, cot_row, seg_row = batch_item

        def wrapped(weights, probe_zero, values):
            return forward(weights, probe_zero, values, seg_row)
        probe_zero = jnp.zeros((SEQ, D), jnp.float32)
        output, pullback, first_out = jax.vjp(wrapped, params, probe_zero, input_row.astype(jnp.float32), has_aux=True)
        grad_params, grad_probe, grad_input = pullback(cot_row.astype(jnp.float32))
        totals = jax.tree.map(lambda left_side, right_side: left_side + right_side, totals, grad_params)
        return (totals, (first_out, output, grad_input, grad_probe))
    zero_grads = jax.tree.map(jnp.zeros_like, params)
    totals, (firsts, outputs, grads_in, grads_probe) = lax.scan(one_batch, zero_grads, (inputs, cotangent, segments))
    section_out = jnp.stack([firsts, outputs]).astype(jnp.bfloat16)
    input_grad = jnp.stack([grads_in, grads_probe]).astype(jnp.bfloat16)
    return (section_out, input_grad, totals[0], totals[1], totals[2], totals[3], totals[4], totals[5], totals[6], totals[7], totals[8], totals[9])
```

```python
import jax
import jax.numpy as jnp
import numpy as np
from jax import lax
from jax.sharding import Mesh
from jax.sharding import PartitionSpec as P

HEAD = 128
EPS = 1e-06
NEG = -1e30
THETA = 1000000.0
WIDTH = 1536
QCOLS = 384
LOCAL_FF = 560
PAD_FF = 640
AXES = ("s", "y", "z", "x", "c")
BLOCK_ORDER = (0, 2, 1, 3)
BF = jnp.bfloat16
F32 = jnp.float32


def swap(value, axis):
    return lax.ppermute(value, axis, [(0, 1), (1, 0)])


def exchange(value, axes):
    return lax.all_to_all(value, axes, split_axis=0, concat_axis=0, tiled=True)


def nn(left, right):
    return jnp.dot(left, right, preferred_element_type=F32)


def nt(left, right):
    return lax.dot_general(left, right, (((1,), (1,)), ((), ())), preferred_element_type=F32)


def tn(left, right):
    return lax.dot_general(left, right, (((0,), (0,)), ((), ())), preferred_element_type=F32)


def inverse_rms(values):
    return lax.rsqrt(jnp.mean(values * values, axis=-1, keepdims=True) + EPS)


def halves_swapped(values):
    half = HEAD // 2
    return jnp.concatenate([values[..., half:], values[..., :half]], axis=-1)


def rotate(values, cosine, sine):
    return values * cosine + halves_swapped(values) * sine


def rotate_back(values, cosine, sine):
    return values * cosine - halves_swapped(values) * sine


def gather_block(rows):
    count = 8
    mine = exchange(jnp.broadcast_to(rows[None], (count,) + rows.shape), ("z", "x"))
    mine = mine.reshape(count * rows.shape[0], rows.shape[1])
    return jnp.concatenate([mine, swap(mine, "c")], axis=0)


def scatter_block(part):
    half = part.shape[0] // 2
    given = swap(part[half:].astype(BF), "c")
    joined = (part[:half] + given.astype(F32)).astype(BF)
    pieces = exchange(joined.reshape(8, half // 8, part.shape[1]), ("z", "x"))
    return jnp.sum(pieces.astype(F32), axis=0)


def scatter_heads(part):
    pieces = exchange(part.astype(BF).reshape(4, part.shape[0] // 4, part.shape[1]), ("x", "c"))
    return jnp.sum(pieces.astype(F32), axis=0)


def forward_layer(xin, weights, allowed, cosine, sine, is_key):
    attn, ffn, gain_one, gain_two, bias = weights
    normed_local = (xin * inverse_rms(xin) * gain_one).astype(BF)
    normed = lax.all_gather(normed_local, ("x", "c"), axis=0, tiled=True)
    qkv = nn(normed, attn[:, :512]) + bias
    rows = normed.shape[0]
    query = rotate(qkv[:, :QCOLS].reshape(rows, 3, HEAD), cosine[:, None], sine[:, None]).astype(BF)
    query = query.transpose(1, 0, 2).reshape(3 * rows, HEAD)
    kv = qkv[:, QCOLS:]
    kv = jnp.where(is_key, rotate(kv, cosine, sine), kv).astype(BF)
    kv_mine = exchange(jnp.broadcast_to(kv[None], (16, rows, HEAD)), ("y", "z")).reshape(16 * rows, HEAD)
    kv_other = swap(kv_mine, "c")
    key = jnp.where(is_key, kv_mine, kv_other)
    value = jnp.where(is_key, kv_other, kv_mine)
    scores = nt(query, key).reshape(3, rows, -1) * HEAD**-0.5
    scores = jnp.where(allowed[None], scores, NEG)
    top = jnp.max(scores, axis=-1, keepdims=True)
    raised = jnp.exp(scores - top)
    total = jnp.sum(raised, axis=-1, keepdims=True)
    probs = (raised / total).astype(BF).reshape(3 * rows, -1)
    lse = top + jnp.log(total)
    attended = nn(probs, value).astype(BF)
    attended = attended.reshape(3, rows, HEAD).transpose(1, 0, 2).reshape(rows, QCOLS)
    mixed = xin + scatter_heads(nt(attended, attn[:, 512:]))
    second_local = (mixed * inverse_rms(mixed) * gain_two).astype(BF)
    second = gather_block(second_local)
    gate = nn(second, ffn[:, :PAD_FF])
    up = nn(second, ffn[:, PAD_FF : 2 * PAD_FF])
    hidden = (jax.nn.silu(gate) * up).astype(BF)
    output = mixed + scatter_block(nt(hidden, ffn[:, 2 * PAD_FF :]))
    kept = (xin, mixed, normed, query, key, value, lse, attended, second, gate, up, hidden)
    return output, kept


def backward_layer(grad_out, weights, kept, allowed, cosine, sine, is_key):
    attn, ffn, gain_one, gain_two, bias = weights
    xin, mixed, normed, query, key, value, lse, attended, second, gate, up, hidden = kept
    rows = normed.shape[0]
    grad_low = gather_block(grad_out)
    grad_hidden = nn(grad_low, ffn[:, 2 * PAD_FF :])
    sig = jax.nn.sigmoid(gate)
    grad_gate = (grad_hidden * up * sig * (1.0 + gate * (1.0 - sig))).astype(BF)
    grad_up = (grad_hidden * gate * sig).astype(BF)
    grad_second = scatter_block(nt(grad_gate, ffn[:, :PAD_FF]) + nt(grad_up, ffn[:, PAD_FF : 2 * PAD_FF]))
    grad_ffn = jnp.concatenate(
        [tn(second, grad_gate).astype(BF), tn(second, grad_up).astype(BF), tn(grad_low, hidden).astype(BF)], axis=1
    )
    inv = inverse_rms(mixed)
    norm_mixed = mixed * inv
    grad_gain_two = jnp.sum(grad_second * norm_mixed, axis=0)
    scaled = grad_second * gain_two
    grad_mixed = grad_out.astype(F32) + inv * (
        scaled - norm_mixed * jnp.mean(scaled * norm_mixed, axis=-1, keepdims=True)
    )
    grad_att = lax.all_gather(grad_mixed.astype(BF), ("x", "c"), axis=0, tiled=True)
    grad_out_t = tn(grad_att, attended)
    grad_attended = nn(grad_att, attn[:, 512:]).astype(BF)
    grad_attended = grad_attended.reshape(rows, 3, HEAD).transpose(1, 0, 2).reshape(3 * rows, HEAD)
    scores = nt(query, key).reshape(3, rows, -1) * HEAD**-0.5
    probs = jnp.exp(jnp.where(allowed[None], scores, NEG) - lse).reshape(3 * rows, -1)
    grad_probs = nt(grad_attended, value)
    grad_value = tn(probs.astype(BF), grad_attended)
    grad_scores = (probs * (grad_probs - jnp.sum(probs * grad_probs, axis=-1, keepdims=True))).astype(BF)
    grad_query = nn(grad_scores, key) * HEAD**-0.5
    grad_key = tn(grad_scores, query) * HEAD**-0.5
    kept_half = jnp.where(is_key, grad_key, grad_value)
    sent_half = jnp.where(is_key, grad_value, grad_key).astype(BF)
    grad_kv = (kept_half + swap(sent_half, "c").astype(F32)).astype(BF)
    grad_kv = jnp.sum(exchange(grad_kv.reshape(16, rows, HEAD), ("y", "z")).astype(F32), axis=0)
    grad_kv = jnp.where(is_key, rotate_back(grad_kv, cosine, sine), grad_kv).astype(BF)
    grad_query = rotate_back(grad_query.reshape(3, rows, HEAD), cosine[None], sine[None]).astype(BF)
    grad_query = grad_query.transpose(1, 0, 2).reshape(rows, QCOLS)
    grad_qkv = jnp.concatenate([grad_query, grad_kv], axis=1)
    grad_w_qkv = tn(normed, grad_qkv)
    grad_bias = jnp.sum(grad_qkv, axis=0, dtype=F32)
    grad_normed = scatter_heads(nt(grad_qkv, attn[:, :512]))
    inv_one = inverse_rms(xin)
    norm_one = xin * inv_one
    grad_gain_one = jnp.sum(grad_normed * norm_one, axis=0)
    scaled_one = grad_normed * gain_one
    grad_in = grad_mixed + inv_one * (
        scaled_one - norm_one * jnp.mean(scaled_one * norm_one, axis=-1, keepdims=True)
    )
    grad_attn = jnp.concatenate([grad_w_qkv, grad_out_t], axis=1).astype(BF).reshape(16, 96, 896)
    small = jnp.concatenate(
        [
            jnp.broadcast_to(grad_bias[None], (16, 512)),
            grad_gain_one.reshape(16, 96),
            grad_gain_two.reshape(16, 96),
            jnp.zeros((16, 192), F32),
        ],
        axis=1,
    ).astype(BF)
    grad_attn = jnp.concatenate([grad_attn, small[:, None], jnp.zeros((16, 15, 896), BF)], axis=1)
    return grad_in, grad_attn.reshape(16 * 112, 896), grad_ffn


def local(
    inputs, cotangent, segments, gain_one, w_query, b_query, w_keyval, b_keyval, w_out, gain_two, w_gate, w_up, w_down
):
    on_first = lax.axis_index("s") == 0
    is_key = lax.axis_index("c") == 0
    block = lax.axis_index("y") * 4 + lax.axis_index("z")
    member = lax.axis_index("x") * 2 + lax.axis_index("c")

    def pick(first, second):
        return jnp.where(on_first, first, second)

    small = jnp.concatenate([gain_one[0], gain_two[0], b_keyval[0], jnp.zeros((72,), BF)])
    kv_blocks = w_keyval[0].reshape(24, 4, HEAD).transpose(1, 0, 2)
    kv_blocks = jnp.stack([kv_blocks[b] for b in BLOCK_ORDER])
    payload = jnp.concatenate(
        [kv_blocks, jnp.broadcast_to(small[None, None], (4, 1, HEAD)), jnp.zeros((4, 7, HEAD), BF)], axis=1
    )
    payload = exchange(payload, ("x", "c"))
    kv_rows = payload[:, :24].reshape(96, HEAD)
    small_row = jnp.concatenate([payload[:, 24, :56].reshape(224), jnp.zeros((288,), BF), b_query[0]])
    attn_own = jnp.concatenate(
        [
            jnp.concatenate([w_query[0], kv_rows, w_out[0].T], axis=1),
            small_row[None],
            jnp.zeros((15, 896), BF),
        ],
        axis=0,
    )
    attn_other = swap(attn_own, "s")

    stacked = jnp.stack([w_gate[0], w_up[0], w_down[0].T], axis=1).reshape(96, 3, 4, LOCAL_FF)
    stacked = jnp.pad(stacked, ((0, 0), (0, 0), (0, 0), (0, PAD_FF - LOCAL_FF)))
    ffn_own = exchange(stacked.transpose(2, 0, 1, 3).reshape(4, 96, 3 * PAD_FF), "z").reshape(384, 3 * PAD_FF)
    ffn_other = swap(ffn_own, "s")

    def attn_weights(piece):
        whole = lax.all_gather(piece, ("y", "z"), axis=0, tiled=True).reshape(16, 112, 896)
        matrix = whole[:, :96].reshape(WIDTH, 896)
        row = whole[:, 96]
        bits = row[:, :224].reshape(64, 56)
        gain_a = bits[:, :24].reshape(WIDTH).astype(F32)
        gain_b = bits[:, 24:48].reshape(WIDTH).astype(F32)
        kv_bias = lax.dynamic_slice_in_dim(
            bits[:, 48:].reshape(512), (lax.axis_index("c") * 2 + lax.axis_index("x")) * HEAD, HEAD, 0
        )
        bias = jnp.concatenate([row[0, 512:], kv_bias]).astype(F32)
        return matrix, gain_a, gain_b, bias

    def ffn_weights(piece):
        return lax.all_gather(piece, "y", axis=0, tiled=True)

    layers = []
    for layer in range(2):
        a_piece = pick(attn_own, attn_other) if layer == 0 else pick(attn_other, attn_own)
        f_piece = pick(ffn_own, ffn_other) if layer == 0 else pick(ffn_other, ffn_own)
        matrix, gain_a, gain_b, bias = attn_weights(a_piece)
        layers.append((matrix, ffn_weights(f_piece), gain_a, gain_b, bias))

    rows = 128
    seq = segments.shape[1]
    seg = pick(segments[0], segments[1])
    local_pos = block * rows + jnp.arange(rows, dtype=jnp.int32)
    inverse_freq = THETA ** (-(jnp.arange(HEAD // 2, dtype=F32) * 2.0) / HEAD)
    angles = local_pos.astype(F32)[:, None] * inverse_freq[None, :]
    cosine = jnp.cos(angles)
    sine = jnp.sin(angles)
    cosine = jnp.concatenate([cosine, cosine], axis=1)
    sine = jnp.concatenate([-sine, sine], axis=1)
    local_seg = lax.dynamic_slice_in_dim(seg, block * rows, rows, 0)
    key_pos = jnp.arange(seq, dtype=jnp.int32)
    allowed = (seg[None, :] == local_seg[:, None]) & (key_pos[None, :] <= local_pos[:, None])

    xin = pick(inputs[0], inputs[1]).astype(F32)
    out_one, kept_one = forward_layer(xin, layers[0], allowed, cosine, sine, is_key)
    out_one = out_one.astype(BF)
    out_two, kept_two = forward_layer(out_one.astype(F32), layers[1], allowed, cosine, sine, is_key)
    out_two = out_two.astype(BF)
    cot = pick(cotangent[0], cotangent[1])
    grad_two, attn_two, ffn_two = backward_layer(cot, layers[1], kept_two, allowed, cosine, sine, is_key)
    grad_two = grad_two.astype(BF)
    attn_two = lax.psum_scatter(attn_two, ("y", "z"), scatter_dimension=0, tiled=True)
    ffn_two = lax.psum_scatter(ffn_two, "y", scatter_dimension=0, tiled=True)
    grad_one, attn_one, ffn_one = backward_layer(grad_two, layers[0], kept_one, allowed, cosine, sine, is_key)
    grad_one = grad_one.astype(BF)
    attn_one = lax.psum_scatter(attn_one, ("y", "z"), scatter_dimension=0, tiled=True)
    ffn_one = lax.psum_scatter(ffn_one, "y", scatter_dimension=0, tiled=True)

    def across(first, second):
        return pick(first, second).astype(F32) + (
            lax.ppermute(second, "s", [(0, 1)]).astype(F32) + lax.ppermute(first, "s", [(1, 0)]).astype(F32)
        )

    attn_sum = across(attn_one, attn_two)
    ffn_sum = across(ffn_one, ffn_two)

    pieces = exchange(ffn_sum.astype(BF).reshape(4, 96, 3 * PAD_FF), "z").astype(F32)
    pieces = pieces.reshape(4, 96, 3, PAD_FF)[..., :LOCAL_FF]
    grad_gate = pieces[:, :, 0].transpose(1, 0, 2).reshape(96, 4 * LOCAL_FF)
    grad_up = pieces[:, :, 1].transpose(1, 0, 2).reshape(96, 4 * LOCAL_FF)
    grad_down = pieces[:, :, 2].transpose(0, 2, 1).reshape(4 * LOCAL_FF, 96)

    grad_query = attn_sum[:96, :QCOLS]
    grad_w_out = attn_sum[:96, 512:].T
    grad_row = attn_sum[96]
    grad_b_query = grad_row[:QCOLS]
    kv_bias_row = grad_row[QCOLS:512]
    gains = jnp.concatenate([grad_row[512:608].reshape(4, 24), grad_row[608:704].reshape(4, 24)], axis=1)
    payload = jnp.concatenate(
        [
            attn_sum[:96, QCOLS:512].reshape(4, 24, HEAD),
            jnp.pad(gains, ((0, 0), (0, HEAD - 48)))[:, None],
            jnp.broadcast_to(kv_bias_row[None, None], (4, 1, HEAD)),
            jnp.zeros((4, 6, HEAD), F32),
        ],
        axis=1,
    )
    payload = exchange(payload, ("x", "c"))
    payload = jnp.stack([payload[b] for b in BLOCK_ORDER])
    grad_keyval = payload[:, :24].transpose(1, 0, 2).reshape(24, 512)
    gains = jnp.sum(payload[:, 24], axis=0)
    kv_bias_row = lax.dynamic_index_in_dim(payload[:, 25], lax.axis_index("y"), 0, keepdims=False)
    grad_b_keyval = lax.dynamic_slice_in_dim(kv_bias_row, (lax.axis_index("z") * 4 + member) * 8, 8, 0)

    def both(first, second):
        given = swap(pick(second, first), "s")
        return jnp.stack([pick(first, given), pick(given, second)])[None]

    return (
        both(out_one, out_two),
        both(grad_one, grad_two),
        gains[None, :24],
        grad_query[None],
        grad_b_query[None],
        grad_keyval[None],
        grad_b_keyval[None],
        grad_w_out[None],
        gains[None, 24:48],
        grad_gate[None],
        grad_up[None],
        grad_down[None],
    )


def solution(mesh):
    fine = Mesh(np.asarray(mesh.devices).reshape(2, 4, 4, 2, 2), AXES)
    block, member = ("y", "z"), ("x", "c")
    every = block + member
    tokens = P(None, every, None)
    split = P("s", every)
    columns = P("s", block, member)
    rows = P("s", member, block)
    keyval = P("s", every, None)
    outs = P("s", None, every, None)
    return jax.shard_map(
        local,
        mesh=fine,
        in_specs=(
            tokens, tokens, P(), split, columns, P("s", member), keyval, split, rows, split, columns, columns, rows,
        ),
        out_specs=(
            outs, outs, split, columns, P("s", member), keyval, split, rows, split, columns, columns, rows,
        ),
        check_vma=False,
    )
```

```python
import jax
import jax.numpy as jnp
import numpy as np
from jax import lax
from jax.experimental import pallas as pl
from jax.experimental.pallas import tpu as pltpu
from jax.sharding import Mesh
from jax.sharding import PartitionSpec as P

HEAD = 128
EPS = 1e-06
NEG = -1e30
THETA = 1000000.0
WIDTH = 1536
QCOLS = 384
SEQ = 2048
CHUNK = 512
LOCAL_FF = 560
PAD_FF = 640
GU = 2 * PAD_FF
FW = 3 * PAD_FF
SCALE = HEAD**-0.5
AXES = ("s", "y", "z", "x", "c")
BLOCK_ORDER = (0, 2, 1, 3)
BF = jnp.bfloat16
F32 = jnp.float32
VMEM = pl.BlockSpec(memory_space=pltpu.VMEM)
SMEM = pl.BlockSpec(memory_space=pltpu.SMEM)
ANY = pl.BlockSpec(memory_space=pl.ANY)


def swap(value, axis):
    return lax.ppermute(value, axis, [(0, 1), (1, 0)])


def exchange(value, axes):
    return lax.all_to_all(value, axes, split_axis=0, concat_axis=0, tiled=True)


def nn(left, right):
    return jnp.dot(left, right, preferred_element_type=F32)


def nt(left, right):
    return lax.dot_general(left, right, (((1,), (1,)), ((), ())), preferred_element_type=F32)


def tn(left, right):
    return lax.dot_general(left, right, (((0,), (0,)), ((), ())), preferred_element_type=F32)


def after(value, done):
    return lax.optimization_barrier((value, done))[0]


def inverse_rms(values):
    return lax.rsqrt(jnp.mean(values * values, axis=-1, keepdims=True) + EPS)


def call(kernel, out_shape, in_specs, args, scratch=(), flops=0, size=0, exps=0, **more):
    return pl.pallas_call(
        kernel,
        out_shape=out_shape,
        in_specs=in_specs,
        scratch_shapes=list(scratch),
        compiler_params=pltpu.CompilerParams(vmem_limit_bytes=52 * 1024 * 1024),
        cost_estimate=pl.CostEstimate(flops=flops, bytes_accessed=size, transcendentals=exps),
        **more,
    )(*args)


def arr(shape, dtype=BF):
    return jax.ShapeDtypeStruct(shape, dtype)


def turned(values, cosine, sine):
    return values * cosine + pltpu.roll(values, HEAD // 2, 1) * sine


def whole_weight(ref, scratch, first, size):
    if len(ref.shape) == 2:
        return ref[...]
    for b in range(16):
        scratch[pl.ds(b * 96, 96), :] = ref[b, pl.ds(0, 96), pl.ds(first, size)]
    return scratch[...]


def qkv_kernel(flag, xin, gain, weight, bias, cosine, sine, normed, query, kv, scratch):
    whole = whole_weight(weight, scratch, 0, 512)
    cos, sin = cosine[...], sine[...]
    rows = xin[...].astype(F32)
    low = (rows * inverse_rms(rows) * gain[...]).astype(BF)
    normed[...] = low
    out = nn(low, whole) + bias[...]
    for h in range(3):
        query[h] = turned(out[:, h * HEAD : (h + 1) * HEAD], cos, sin).astype(BF)
    last = out[:, QCOLS:]
    last = jnp.where(flag[0] == 1, turned(last, cos, sin), last).astype(BF)
    for b in range(16):
        kv[b] = last


def qkv_columns(flag, xin, gain, weight, bias, cosine, sine):
    return call(
        qkv_kernel,
        (arr((HEAD, WIDTH)), arr((3, HEAD, HEAD)), arr((16, HEAD, HEAD))),
        [SMEM] + [VMEM] * 6,
        (flag, xin, gain, weight, bias, cosine, sine),
        [pltpu.VMEM((WIDTH, 512), BF)],
        flops=2 * 128 * 1536 * 512,
        size=3_000_000,
    )


def key_scores(query_all, keys, key_seg, query_seg, first_key, first_query):
    scores = nt(keys, query_all) * SCALE
    key_pos = first_key + lax.broadcasted_iota(jnp.int32, (CHUNK, HEAD), 0)
    query_pos = first_query + lax.broadcasted_iota(jnp.int32, (CHUNK, HEAD), 1)
    allowed = (key_seg == query_seg) & (key_pos <= query_pos)
    return [jnp.where(allowed, scores[:, h * HEAD : (h + 1) * HEAD], NEG) for h in range(3)]


def attend_kernel(flag, query, kv_mine, kv_other, seg_col, seg_row, out_t, attended, lse, part, top, total, acc, scratch):
    query_all = query[...].reshape(3 * HEAD, HEAD)
    is_key = flag[0] == 1
    first_query = flag[1] * HEAD
    top[...] = jnp.full(top.shape, -3e38, F32)
    total[...] = jnp.zeros(total.shape, F32)
    acc[...] = jnp.zeros(acc.shape, F32)

    @pl.loop(0, SEQ // CHUNK)
    def _(step):
        at = pl.ds(pl.multiple_of(step * CHUNK, CHUNK), CHUNK)
        mine, other = kv_mine[at, :], kv_other[at, :]
        keys = jnp.where(is_key, mine, other)
        values = jnp.where(is_key, other, mine)
        scores = key_scores(query_all, keys, seg_col[at, :], seg_row[...], step * CHUNK, first_query)
        for h in range(3):
            columns = pl.ds(h * HEAD, HEAD)
            old = top[:, columns]
            new = jnp.maximum(old, jnp.max(scores[h], axis=0, keepdims=True))
            shrink = jnp.exp(old - new)
            raised = jnp.exp(scores[h] - new)
            top[:, columns] = new
            total[:, columns] = total[:, columns] * shrink + jnp.sum(raised, axis=0, keepdims=True)
            acc[:, columns] = acc[:, columns] * shrink + tn(values, raised.astype(BF))

    lse[...] = top[...] + jnp.log(total[...])
    done = acc[...] / total[...]
    for h in range(3):
        attended[:, pl.ds(h * HEAD, HEAD)] = done[:, h * HEAD : (h + 1) * HEAD].T.astype(BF)
    out = nt(attended[...], whole_weight(out_t, scratch, 512, QCOLS)).astype(BF)
    for t in range(4):
        part[t] = out[t * 32 : (t + 1) * 32]


def attend(flag, query, kv_mine, kv_other, seg_col, seg_row, out_t):
    return call(
        attend_kernel,
        (arr((HEAD, QCOLS)), arr((1, QCOLS), F32), arr((4, 32, WIDTH))),
        [SMEM] + [VMEM] * 6,
        (flag, query, kv_mine, kv_other, seg_col, seg_row, out_t),
        [
            pltpu.VMEM((1, QCOLS), F32),
            pltpu.VMEM((1, QCOLS), F32),
            pltpu.VMEM((HEAD, QCOLS), F32),
            pltpu.VMEM((WIDTH, QCOLS), BF),
        ],
        flops=4 * 384 * 2048 * 128 + 2 * 128 * 384 * 1536,
        size=3_000_000,
        exps=384 * 2048,
    )


def attend_back_kernel(
    flag, query, kv_mine, kv_other, seg_col, seg_row, lse, grad_att, out_t, cosine, sine,
    grad_query, kept, sent, low, acc, scratch
):
    query_all = query[...].reshape(3 * HEAD, HEAD)
    is_key = flag[0] == 1
    first_query = flag[1] * HEAD
    grad_attended = nn(grad_att[...], whole_weight(out_t, scratch, 512, QCOLS)).astype(BF)
    for h in range(3):
        low[pl.ds(h * HEAD, HEAD), :] = grad_attended[:, h * HEAD : (h + 1) * HEAD]
    grad_rows = low[...]
    lse_row = lse[...]

    def chunk(step):
        at = pl.ds(pl.multiple_of(step * CHUNK, CHUNK), CHUNK)
        mine, other = kv_mine[at, :], kv_other[at, :]
        keys = jnp.where(is_key, mine, other)
        values = jnp.where(is_key, other, mine)
        scores = key_scores(query_all, keys, seg_col[at, :], seg_row[...], step * CHUNK, first_query)
        probs = [jnp.exp(scores[h] - lse_row[:, h * HEAD : (h + 1) * HEAD]) for h in range(3)]
        grad_probs = nt(values, grad_rows)
        return at, keys, probs, grad_probs

    acc[...] = jnp.zeros(acc.shape, F32)

    def row_sums(step, sums):
        _, _, probs, grad_probs = chunk(step)
        return tuple(
            sums[h] + jnp.sum(probs[h] * grad_probs[:, h * HEAD : (h + 1) * HEAD], axis=0, keepdims=True)
            for h in range(3)
        )

    zero = jnp.zeros((1, HEAD), F32)
    sums = lax.fori_loop(0, SEQ // CHUNK, row_sums, (zero, zero, zero))

    @pl.loop(0, SEQ // CHUNK)
    def _(step):
        at, keys, probs, grad_probs = chunk(step)
        low_probs = jnp.concatenate([p.astype(BF) for p in probs], axis=1)
        low_scores = jnp.concatenate(
            [
                (probs[h] * (grad_probs[:, h * HEAD : (h + 1) * HEAD] - sums[h])).astype(BF)
                for h in range(3)
            ],
            axis=1,
        )
        grad_value = nn(low_probs, grad_rows)
        grad_key = nn(low_scores, query_all) * SCALE
        acc[...] += tn(keys, low_scores)
        kept[at, :] = jnp.where(is_key, grad_key, grad_value)
        sent[at, :] = jnp.where(is_key, grad_value, grad_key).astype(BF)

    cos, sin = cosine[...], sine[...]
    for h in range(3):
        rows = acc[:, pl.ds(h * HEAD, HEAD)].T * SCALE
        grad_query[:, pl.ds(h * HEAD, HEAD)] = turned(rows, cos, -sin).astype(BF)


def attend_back(flag, query, kv_mine, kv_other, seg_col, seg_row, lse, grad_att, out_t, cosine, sine):
    return call(
        attend_back_kernel,
        (arr((HEAD, QCOLS)), arr((SEQ, HEAD), F32), arr((SEQ, HEAD))),
        [SMEM] + [VMEM] * 10,
        (flag, query, kv_mine, kv_other, seg_col, seg_row, lse, grad_att, out_t, cosine, sine),
        [pltpu.VMEM((3 * HEAD, HEAD), BF), pltpu.VMEM((HEAD, QCOLS), F32), pltpu.VMEM((WIDTH, QCOLS), BF)],
        flops=14 * 384 * 2048 * 128 + 2 * 128 * 384 * 1536,
        size=5_000_000,
        exps=2 * 384 * 2048,
    )


def qkv_back_kernel(
    flag, pieces, grad_query, weight, xin, cosine, sine, grad_qkv, grad_bias, grad_gain, part, scratch
):
    whole = whole_weight(weight, scratch, 0, 512)
    total = jnp.sum(pieces[...].astype(F32), axis=0)
    total = jnp.where(flag[0] == 1, turned(total, cosine[...], -sine[...]), total).astype(BF)
    grad_qkv[:, pl.ds(0, QCOLS)] = grad_query[...]
    grad_qkv[:, pl.ds(QCOLS, HEAD)] = total
    grads = grad_qkv[...]
    grad_bias[...] = jnp.sum(grads.astype(F32), axis=0, keepdims=True)
    out = nt(grads, whole)
    rows = xin[...].astype(F32)
    grad_gain[...] = jnp.sum(out * rows * inverse_rms(rows), axis=0, keepdims=True)
    low = out.astype(BF)
    for t in range(4):
        part[t] = low[t * 32 : (t + 1) * 32]


def qkv_back(flag, pieces, grad_query, weight, xin, cosine, sine):
    return call(
        qkv_back_kernel,
        (arr((HEAD, 512)), arr((1, 512), F32), arr((1, WIDTH), F32), arr((4, 32, WIDTH))),
        [SMEM] + [VMEM] * 6,
        (flag, pieces, grad_query, weight, xin, cosine, sine),
        [pltpu.VMEM((WIDTH, 512), BF)],
        flops=2 * 128 * 1536 * 512,
        size=3_000_000,
    )


def weight_copies(own, other, gate_up, down, sems, order):
    copies = {}
    for i, ref in enumerate((own, other)):
        for name in order:
            start, size, buffer = (0, GU, gate_up) if name == "gate_up" else (GU, PAD_FF, down)
            copies[i, name] = pltpu.make_async_copy(
                ref.at[:, pl.ds(start, size)], buffer.at[i], sems.at[2 * i + (name == "down")]
            )
    for i in range(2):
        for name in order:
            copies[i, name].start()
    return copies


def feed_kernel(tokens, own, other, part, gate_up_out, gate_up, down, acc, sems):
    copies = weight_copies(own, other, gate_up, down, sems, ("gate_up", "down"))
    rows = tokens[...]
    for i in range(2):
        copies[i, "gate_up"].wait()
        both = nn(rows, gate_up[i])
        gate_up_out[i] = both.astype(BF)
        gate, up = both[:, :PAD_FF], both[:, PAD_FF:]
        hidden = (gate * jax.nn.sigmoid(gate) * up).astype(BF)
        copies[i, "down"].wait()
        out = nt(hidden, down[i])
        if i == 0:
            acc[...] = out
        else:
            part[...] = (acc[...] + out).astype(BF)


FEED_SCRATCH = [
    pltpu.VMEM((2, WIDTH, GU), BF),
    pltpu.VMEM((2, WIDTH, PAD_FF), BF),
    pltpu.VMEM((256, WIDTH), F32),
    pltpu.SemaphoreType.DMA((4,)),
]


def feed(tokens, own, other):
    return call(
        feed_kernel,
        (arr((256, WIDTH)), arr((2, 256, GU))),
        [VMEM, ANY, ANY],
        (tokens, own, other),
        FEED_SCRATCH,
        flops=2 * 256 * 1536 * 3840,
        size=15_000_000,
        exps=256 * 1280,
    )


def feed_back_kernel(grads, own, other, gate_up_in, part, for_own, for_other, gate_up, down, acc, sems):
    copies = weight_copies(own, other, gate_up, down, sems, ("down", "gate_up"))
    rows = grads[...]
    for i, result in enumerate((for_own, for_other)):
        copies[i, "down"].wait()
        grad_hidden = nn(rows, down[i])
        gate = gate_up_in[i, :, pl.ds(0, PAD_FF)].astype(F32)
        up = gate_up_in[i, :, pl.ds(PAD_FF, PAD_FF)].astype(F32)
        sig = jax.nn.sigmoid(gate)
        silu = gate * sig
        result[:, pl.ds(0, PAD_FF)] = (grad_hidden * up * sig * (1.0 + gate * (1.0 - sig))).astype(BF)
        result[:, pl.ds(PAD_FF, PAD_FF)] = (grad_hidden * silu).astype(BF)
        result[:, pl.ds(GU, PAD_FF)] = (silu * up).astype(BF)
        copies[i, "gate_up"].wait()
        out = nt(result[:, pl.ds(0, GU)], gate_up[i])
        if i == 0:
            acc[...] = out
        else:
            part[...] = (acc[...] + out).astype(BF)


def feed_back(grads, own, other, gate_up):
    return call(
        feed_back_kernel,
        (arr((256, WIDTH)), arr((256, FW)), arr((256, FW))),
        [VMEM, ANY, ANY, VMEM],
        (grads, own, other, gate_up),
        FEED_SCRATCH,
        flops=2 * 256 * 1536 * 3840,
        size=17_000_000,
        exps=256 * 1280,
    )


def feed_grad_kernel(tokens, tokens_other, grads, grads_other, own, given, out):
    gate_up, hidden = pl.ds(0, GU), pl.ds(GU, PAD_FF)
    out[:, gate_up] = (tn(tokens[...], own[:, gate_up]) + tn(tokens_other[...], given[:, gate_up])).astype(BF)
    out[:, hidden] = (tn(grads[...], own[:, hidden]) + tn(grads_other[...], given[:, hidden])).astype(BF)


def feed_grad(tokens, tokens_other, grads, grads_other, own, given):
    rows = 256
    columns = pl.BlockSpec((256, rows), lambda i: (0, i))
    fixed = pl.BlockSpec((256, FW), lambda i: (0, 0))
    return call(
        feed_grad_kernel,
        arr((WIDTH, FW)),
        [columns] * 4 + [fixed] * 2,
        (tokens, tokens_other, grads, grads_other, own, given),
        flops=2 * 512 * 1536 * 1920,
        size=12_000_000,
        grid=(WIDTH // rows,),
        out_specs=pl.BlockSpec((rows, FW), lambda i: (i, 0)),
    )


def shifted(value, axis, steps):
    return lax.ppermute(value, axis, [(i, (i + steps) % 4) for i in range(4)])


def ring_gather(piece, first, second, done):
    some = after(jnp.stack([piece] + [shifted(piece, first, j) for j in (1, 2, 3)]), done)
    return [some] + [shifted(some, second, k) for k in (1, 2, 3)]


def ring_block(place, j, k):
    return lax.rem(place[0] + 4 - j, 4) * place[1] + lax.rem(place[2] + 4 - k, 4) * place[3]


def assemble_kernel(columns, place, *refs):
    pieces, outs, tail = refs[:4], refs[4:-1], refs[-1]
    for k in range(4):
        for j in range(4):
            block = ring_block(place, j, k)
            first = 0
            for out, size in zip(outs, columns, strict=True):
                at = pl.ds(pl.multiple_of(block * 96, 32), 96)
                out[at, :] = pieces[k][j, pl.ds(0, 96), pl.ds(first, size)]
                first += size
            tail[block] = pieces[k][j, pl.ds(96, 16), pl.ds(0, 512)]


def assemble(place, pieces, columns):
    return call(
        lambda *refs: assemble_kernel(columns, *refs),
        tuple(arr((WIDTH, size)) for size in columns) + (arr((16, 16, 512)),),
        [SMEM] + [VMEM] * 4,
        (place, *pieces),
        size=7_000_000,
    )


def weight_grad_kernel(place, normed, grad_qkv, grad_att, attended, bias, gain_a, gain_b, *rest):
    outs, scratch = rest[:-1], rest[-1]
    scratch[:, pl.ds(0, 512)] = tn(normed[...], grad_qkv[...]).astype(BF)
    scratch[:, pl.ds(512, QCOLS)] = tn(grad_att[...], attended[...]).astype(BF)
    gains = [gain_a[...], gain_b[...]]
    first_row = lax.broadcasted_iota(jnp.int32, (16, 896), 0) == 0
    for b in range(16):
        moved = [(pltpu.roll(g, (WIDTH - 96 * b) % WIDTH, 1) if b else g)[:, :HEAD] for g in gains]
        row = jnp.concatenate([bias[...], *moved, jnp.zeros((1, HEAD), F32)], axis=1)
        rest_rows = jnp.where(first_row, jnp.broadcast_to(row, (16, 896)), 0.0).astype(BF)
        y, z = b // 4, b % 4
        if len(outs) == 1:
            outs[0][z, y, pl.ds(0, 96), :] = scratch[pl.ds(b * 96, 96), :]
            outs[0][z, y, pl.ds(96, 16), :] = rest_rows
        else:
            for k in range(4):

                @pl.when(lax.rem(place[2] + k, 4) == z)
                def _(k=k):
                    outs[k][y, pl.ds(0, 96), :] = scratch[pl.ds(b * 96, 96), :]
                    outs[k][y, pl.ds(96, 16), :] = rest_rows


def weight_grad(place, apart, *args):
    shapes = (arr((4, 112, 896)),) * 4 if apart else (arr((4, 4, 112, 896)),)
    return call(
        weight_grad_kernel,
        shapes,
        [SMEM] + [VMEM] * 7,
        (place, *args),
        [pltpu.VMEM((WIDTH, 896), BF)],
        flops=2 * 128 * 1536 * 896,
        size=6_000_000,
    )


def ring_scatter(parts, done, last):
    total = parts[0].astype(F32)
    for k in (1, 2, 3):
        total = total + after(shifted(parts[k], "z", k), done).astype(F32)
    total = total.astype(BF)
    y = lax.axis_index("y")
    blocks = [lax.dynamic_index_in_dim(total, lax.rem(y + j, 4), 0, keepdims=False) for j in range(4)]
    result = blocks[0].astype(F32)
    for j in (1, 2, 3):
        result = result + after(shifted(blocks[j], "y", j), last).astype(F32)
    return result.astype(BF), total


def after_heads_kernel(pieces, xin, gain, mixed, second):
    total = xin[...].astype(F32) + jnp.sum(pieces[...].astype(F32), axis=0)
    mixed[...] = total
    low = (total * inverse_rms(total) * gain[...]).astype(BF)
    for t in range(8):
        second[t] = low


def after_heads(pieces, xin, gain):
    return call(
        after_heads_kernel,
        (arr((32, WIDTH), F32), arr((8, 32, WIDTH))),
        [VMEM] * 3,
        (pieces, xin, gain),
        size=1_500_000,
    )


def after_feed_kernel(pieces, mixed, out):
    out[...] = (mixed[...] + jnp.sum(pieces[...].astype(F32), axis=0)).astype(BF)


def after_feed(pieces, mixed):
    return call(after_feed_kernel, arr((32, WIDTH)), [VMEM] * 2, (pieces, mixed), size=1_500_000)


def norm_back(grad, values, gain, grad_out):
    inverse = inverse_rms(values)
    norm = values * inverse
    scaled = grad * gain
    grad_gain = jnp.sum(grad * norm, axis=0, keepdims=True)
    return grad_out + inverse * (scaled - norm * jnp.mean(scaled * norm, axis=-1, keepdims=True)), grad_gain


def before_heads_kernel(pieces, mixed, gain, grad_out, grad_mixed, low, grad_gain):
    grad = jnp.sum(pieces[...].astype(F32), axis=0)
    result, sums = norm_back(grad, mixed[...], gain[...], grad_out[...].astype(F32))
    grad_mixed[...] = result
    low[...] = result.astype(BF)
    grad_gain[...] = sums


def before_heads(pieces, mixed, gain, grad_out):
    return call(
        before_heads_kernel,
        (arr((32, WIDTH), F32), arr((32, WIDTH)), arr((1, WIDTH), F32)),
        [VMEM] * 4,
        (pieces, mixed, gain, grad_out),
        size=1_500_000,
    )


def layer_start_kernel(pieces, xin, gain, grad_mixed, grad_in, spread):
    grad = jnp.sum(pieces[...].astype(F32), axis=0)
    result, _ = norm_back(grad, xin[...].astype(F32), gain[...], grad_mixed[...])
    low = result.astype(BF)
    grad_in[...] = low
    for t in range(8):
        spread[t] = low


def layer_start(pieces, xin, gain, grad_mixed):
    return call(
        layer_start_kernel,
        (arr((32, WIDTH)), arr((8, 32, WIDTH))),
        [VMEM] * 4,
        (pieces, xin, gain, grad_mixed),
        size=1_500_000,
    )


def pack_kernel(gate, up, down, out):
    out[...] = jnp.zeros(out.shape, BF)
    for z in range(4):
        first = z * PAD_FF
        size = min(PAD_FF, 4 * LOCAL_FF - first)
        pieces = (
            gate[:, pl.ds(first, size)],
            up[:, pl.ds(first, size)],
            down[pl.ds(first, size), :].astype(F32).T.astype(BF),
        )
        for s in range(2):
            for i, piece in enumerate(pieces):
                out[4 * s + z, :, pl.ds(i * PAD_FF, size)] = piece


def pack(gate, up, down):
    return call(pack_kernel, arr((8, 96, FW)), [VMEM] * 3, (gate, up, down), size=4_500_000)


def unpack_kernel(pieces, gate, up, down):
    for z in range(4):
        first = z * PAD_FF
        size = min(PAD_FF, 4 * LOCAL_FF - first)
        total = pieces[z].astype(F32) + pieces[4 + z].astype(F32)
        gate[:, pl.ds(first, size)] = total[:, :size]
        up[:, pl.ds(first, size)] = total[:, PAD_FF : PAD_FF + size]
        down[pl.ds(first, size), :] = total[:, GU : GU + size].T


def unpack(pieces):
    wide = 4 * LOCAL_FF
    return call(
        unpack_kernel,
        (arr((96, wide), F32), arr((96, wide), F32), arr((wide, 96), F32)),
        [VMEM],
        (pieces,),
        size=7_000_000,
    )


def local(
    inputs, cotangent, segments, gain_one, w_query, b_query, w_keyval, b_keyval, w_out, gain_two, w_gate, w_up, w_down
):
    on_first = lax.axis_index("s") == 0
    core, chip = lax.axis_index("c"), lax.axis_index("x")
    block = lax.axis_index("y") * 4 + lax.axis_index("z")
    member = chip * 2 + core
    flag = jnp.stack([(core == 0).astype(jnp.int32), block.astype(jnp.int32)])

    def pick(first, second):
        return jnp.where(on_first, first, second)

    def gathered(piece, axes):
        return lax.all_gather(piece, axes, axis=0, tiled=True)

    def pair_gather(rows, axis):
        given = swap(rows, axis)
        is_low = lax.axis_index(axis) == 0
        return jnp.concatenate([jnp.where(is_low, rows, given), jnp.where(is_low, given, rows)], axis=0)

    def spread(rows, count, axes):
        return exchange(jnp.broadcast_to(rows[None], (count,) + rows.shape), axes)

    small = jnp.concatenate([gain_one[0], gain_two[0], b_keyval[0], jnp.zeros((72,), BF)])
    kv_blocks = w_keyval[0].reshape(24, 4, HEAD).transpose(1, 0, 2)
    kv_blocks = jnp.stack([kv_blocks[b] for b in BLOCK_ORDER])
    payload = jnp.concatenate(
        [kv_blocks, jnp.broadcast_to(small[None, None], (4, 1, HEAD)), jnp.zeros((4, 7, HEAD), BF)], axis=1
    )
    payload = exchange(jnp.concatenate([payload, payload], axis=0), ("s", "x", "c")).reshape(2, 4, 32, HEAD)
    bias_rows = jnp.pad(b_query, ((0, 15), (0, QCOLS)))
    own = jnp.concatenate([jnp.concatenate([w_query[0], w_out[0].T], axis=1), bias_rows], axis=0)
    other = swap(own, "s")

    def attention_rows(layer, matrices):
        kv = payload[layer]
        kv = jnp.concatenate([kv[:, :24].reshape(96, HEAD), kv[:, 24], jnp.zeros((12, HEAD), BF)], axis=0)
        return jnp.concatenate([matrices[:, :QCOLS], kv], axis=1)

    xin = pick(inputs[0], inputs[1])
    cot = pick(cotangent[0], cotangent[1])
    x_block1 = pair_gather(pair_gather(xin, "c"), "x")
    place_y, place_z = lax.axis_index("y").astype(jnp.int32), lax.axis_index("z").astype(jnp.int32)
    y_then_z = jnp.stack([place_y, jnp.int32(4), place_z, jnp.int32(1)])
    z_then_y = jnp.stack([place_z, jnp.int32(1), place_y, jnp.int32(4)])
    first, second = pick(own, other), pick(other, own)
    rows_first = jnp.concatenate([attention_rows(0, first), first[:, QCOLS:]], axis=1)
    rows_second = jnp.concatenate([attention_rows(1, second), second[:, QCOLS:]], axis=1)
    ring = ring_gather(rows_first, "z", "y", x_block1)
    ffn_packed = after(pack(w_gate[0], w_up[0], w_down[0]), ring[0])
    ffn_both = exchange(ffn_packed, ("s", "z")).reshape(2, 384, FW)
    ffn_both = after(ffn_both, ring)
    qkv_first, out_first, tail_first = assemble(z_then_y, ring, (512, QCOLS))

    seg = pick(segments[0], segments[1])
    local_pos = block * HEAD + jnp.arange(HEAD, dtype=jnp.int32)
    inverse_freq = THETA ** (-(jnp.arange(HEAD // 2, dtype=F32) * 2.0) / HEAD)
    angles = local_pos.astype(F32)[:, None] * inverse_freq[None, :]
    cosine = jnp.cos(angles)
    sine = jnp.sin(angles)
    cosine = jnp.concatenate([cosine, cosine], axis=1)
    sine = jnp.concatenate([-sine, sine], axis=1)
    seg_row = lax.dynamic_slice_in_dim(seg, block * HEAD, HEAD, 0)[None]
    seg_col = seg[:, None]

    def smalls(tail):
        bits = tail[:, :4, QCOLS : QCOLS + 56].reshape(64, 56)
        gain_a = bits[:, :24].reshape(1, WIDTH).astype(F32)
        gain_b = bits[:, 24:48].reshape(1, WIDTH).astype(F32)
        kv_bias = lax.dynamic_slice_in_dim(bits[:, 48:].reshape(1, 512), (core * 2 + chip) * HEAD, HEAD, 1)
        bias = jnp.concatenate([tail[:1, 0, :QCOLS], kv_bias], axis=1).astype(F32)
        return gain_a, gain_b, bias

    gain_a1, gain_b1, bias1 = smalls(tail_first)
    normed1, query1, kv = qkv_columns(flag, x_block1, gain_a1, qkv_first, bias1, cosine, sine)
    own1 = gathered(ffn_both[0], "y")
    kv_mine1 = exchange(kv, ("y", "z")).reshape(SEQ, HEAD)
    kv_other1 = swap(kv_mine1, "c")
    attended1, lse1, part = attend(flag, query1, kv_mine1, kv_other1, seg_col, seg_row, out_first)
    all_second = gathered(after(rows_second, part), ("y", "z")).reshape(16, 112, 896)
    mixed1, low = after_heads(exchange(part, ("x", "c")), xin, gain_b1)
    second1 = exchange(low, ("z", "x")).reshape(256, WIDTH)
    cot_low = spread(after(cot, second1), 8, ("z", "x")).reshape(256, WIDTH)
    second1 = after(second1, cot_low)
    own2 = gathered(after(ffn_both[1], second1), "y")
    other1 = swap(own1, "c")
    part, gate_up1 = feed(second1, own1, other1)
    pieces = exchange(part.reshape(8, 32, WIDTH), ("z", "x"))
    out_one = after_feed(pieces, mixed1)

    x_block2 = gathered(out_one, ("x", "c"))
    gain_a2, gain_b2, bias2 = smalls(all_second[:, 96:, :512])
    normed2, query2, kv = qkv_columns(flag, x_block2, gain_a2, all_second, bias2, cosine, sine)
    kv_mine2 = exchange(kv, ("y", "z")).reshape(SEQ, HEAD)
    kv_other2 = swap(kv_mine2, "c")
    attended2, lse2, part = attend(flag, query2, kv_mine2, kv_other2, seg_col, seg_row, all_second)
    mixed2, low = after_heads(exchange(part, ("x", "c")), out_one, gain_b2)
    other2 = swap(after(own2, low), "c")
    second2 = exchange(low, ("z", "x")).reshape(256, WIDTH)
    part, gate_up2 = feed(second2, own2, other2)
    last_part = part

    def backward(grad_out, grad_low, gate_up, second, own, other, mixed, gain_b, xin, x_block, gain_a, query,
                 kv_mine, kv_other, lse, weight, out_t, earlier=None):
        part, for_own, for_other = feed_back(grad_low, own, other, gate_up)
        pieces = exchange(part.reshape(8, 32, WIDTH), ("z", "x"))
        given = swap(for_other, "c")
        second_other, grad_other = swap(second, "c"), swap(grad_low, "c")
        grad_ffn = feed_grad(second, second_other, grad_low, grad_other, for_own, given)
        pieces, grad_ffn = lax.optimization_barrier((pieces, grad_ffn))
        grad_mixed, low, grad_gain_b = before_heads(pieces, mixed, gain_b, grad_out)
        grad_att = gathered(low, ("x", "c"))
        if earlier is not None:
            grad_ffn = after(grad_ffn, (earlier, grad_att))
        grad_ffn = lax.psum_scatter(grad_ffn, "y", scatter_dimension=0, tiled=True)
        grad_query, kept_half, sent_half = attend_back(
            flag, query, kv_mine, kv_other, seg_col, seg_row, lse, grad_att, out_t, cosine, sine
        )
        grad_kv = (kept_half + swap(sent_half, "c").astype(F32)).astype(BF)
        grad_kv = exchange(grad_kv.reshape(16, HEAD, HEAD), ("y", "z"))
        grad_qkv, grad_bias, grad_gain_a, part = qkv_back(flag, grad_kv, grad_query, weight, x_block, cosine, sine)
        pieces = exchange(part, ("x", "c"))
        grad_in, low = layer_start(pieces, xin, gain_a, grad_mixed)
        return grad_in, low, grad_qkv, grad_att, grad_ffn, (grad_bias, grad_gain_a, grad_gain_b)

    grad_two, low, grad_qkv2, grad_att2, ffn_two, small_two = backward(
        cot, cot_low, gate_up2, second2, own2, other2, mixed2, gain_b2, out_one, x_block2, gain_a2, query2, kv_mine2,
        kv_other2, lse2, all_second, all_second
    )
    grad_low = exchange(low, ("z", "x")).reshape(256, WIDTH)
    (attn_two,) = weight_grad(y_then_z, False, normed2, grad_qkv2, grad_att2, attended2, *small_two)
    attn_two, grad_low = lax.optimization_barrier((attn_two, grad_low))
    attn_two = after(attn_two, ffn_two)
    attn_two = lax.psum_scatter(attn_two.reshape(16 * 112, 896), "z", scatter_dimension=0, tiled=True)
    grad_one, _, grad_qkv1, grad_att1, ffn_one, small_one = backward(
        grad_two, grad_low, gate_up1, second1, own1, other1, mixed1, gain_b1, xin, x_block1, gain_a1, query1, kv_mine1,
        kv_other1, lse1, qkv_first, out_first, attn_two
    )
    out_two = after_feed(exchange(after(last_part, grad_one).reshape(8, 32, WIDTH), ("z", "x")), mixed2)
    parts = weight_grad(y_then_z, True, normed1, grad_qkv1, grad_att1, attended1, *small_one)
    ffn_payload = jnp.concatenate([ffn_one, ffn_two], axis=0).reshape(8, 96, FW)
    ffn_sum = exchange(ffn_payload, ("s", "z"))
    attn_one, halfway = ring_scatter(parts, (ffn_payload, out_two), ffn_sum)
    attn_two = lax.psum_scatter(after(attn_two, (ffn_one, grad_one, halfway)), "y", scatter_dimension=0, tiled=True)

    grad_gate, grad_up, grad_down = unpack(ffn_sum)
    attn_sum = pick(attn_one, attn_two).astype(F32) + swap(pick(attn_two, attn_one), "s").astype(F32)
    main, row = attn_sum[:96], attn_sum[96]
    gains = jnp.concatenate([row[512:608].reshape(4, 24), row[640:736].reshape(4, 24)], axis=1)
    payload = jnp.concatenate(
        [
            main[:, QCOLS:512].reshape(4, 24, HEAD),
            jnp.pad(gains, ((0, 0), (0, HEAD - 48)))[:, None],
            jnp.broadcast_to(row[None, None, QCOLS:512], (4, 1, HEAD)),
            jnp.zeros((4, 6, HEAD), F32),
        ],
        axis=1,
    )
    arrived = [lax.dynamic_index_in_dim(payload, member, 0, keepdims=False)]
    for step in (1, 2, 3):
        given = lax.dynamic_index_in_dim(payload, member ^ step, 0, keepdims=False)
        arrived.append(lax.ppermute(given, ("x", "c"), [(m, m ^ step) for m in range(4)]))
    arrived = jnp.stack(arrived)
    payload = jnp.stack([lax.dynamic_index_in_dim(arrived, member ^ b, 0, keepdims=False) for b in BLOCK_ORDER])
    grad_keyval = payload[:, :24].transpose(1, 0, 2).reshape(24, 512)
    gains = jnp.sum(payload[:, 24], axis=0)
    kv_bias_row = lax.dynamic_index_in_dim(payload[:, 25], lax.axis_index("y"), 0, keepdims=False)
    grad_b_keyval = lax.dynamic_slice_in_dim(kv_bias_row, (lax.axis_index("z") * 4 + member) * 8, 8, 0)

    def both(first, second):
        given = swap(pick(second, first), "s")
        return jnp.stack([pick(first, given), pick(given, second)])[None]

    return (
        both(out_one, out_two),
        both(grad_one, grad_two),
        gains[None, :24],
        main[None, :, :QCOLS],
        row[None, :QCOLS],
        grad_keyval[None],
        grad_b_keyval[None],
        main[:, 512:].T[None],
        gains[None, 24:48],
        grad_gate[None],
        grad_up[None],
        grad_down[None],
    )


def solution(mesh):
    fine = Mesh(np.asarray(mesh.devices).reshape(2, 4, 4, 2, 2), AXES)
    block, member = ("y", "z"), ("x", "c")
    every = block + member
    tokens = P(None, every, None)
    split = P("s", every)
    columns = P("s", block, member)
    rows = P("s", member, block)
    keyval = P("s", every, None)
    outs = P("s", None, every, None)
    return jax.shard_map(
        local,
        mesh=fine,
        in_specs=(
            tokens, tokens, P(), split, columns, P("s", member), keyval, split, rows, split, columns, columns, rows,
        ),
        out_specs=(
            outs, outs, split, columns, P("s", member), keyval, split, rows, split, columns, columns, rows,
        ),
        check_vma=False,
    )
```

```python
import jax
import jax.numpy as jnp
import numpy as np
from jax import lax
from jax.experimental import pallas as pl
from jax.experimental.pallas import tpu as pltpu
from jax.sharding import Mesh
from jax.sharding import PartitionSpec as P

HEAD = 128
EPS = 1e-06
NEG = -1e30
THETA = 1000000.0
WIDTH = 1536
QCOLS = 384
SEQ = 2048
CHUNK = 512
LOCAL_FF = 560
PAD_FF = 640
GU = 2 * PAD_FF
FW = 3 * PAD_FF
SCALE = HEAD**-0.5
AXES = ("s", "y", "z", "x", "c")
BLOCK_ORDER = (0, 2, 1, 3)
BF = jnp.bfloat16
F32 = jnp.float32
VMEM = pl.BlockSpec(memory_space=pltpu.VMEM)
SMEM = pl.BlockSpec(memory_space=pltpu.SMEM)
ANY = pl.BlockSpec(memory_space=pl.ANY)


def swap(value, axis):
    return lax.ppermute(value, axis, [(0, 1), (1, 0)])


def exchange(value, axes):
    return lax.all_to_all(value, axes, split_axis=0, concat_axis=0, tiled=True)


def nn(left, right):
    return jnp.dot(left, right, preferred_element_type=F32)


def nt(left, right):
    return lax.dot_general(left, right, (((1,), (1,)), ((), ())), preferred_element_type=F32)


def tn(left, right):
    return lax.dot_general(left, right, (((0,), (0,)), ((), ())), preferred_element_type=F32)


def after(value, done):
    return lax.optimization_barrier((value, done))[0]


def inverse_rms(values):
    return lax.rsqrt(jnp.mean(values * values, axis=-1, keepdims=True) + EPS)


def call(kernel, out_shape, in_specs, args, scratch=(), flops=0, size=0, exps=0, limit=52, **more):
    return pl.pallas_call(
        kernel,
        out_shape=out_shape,
        in_specs=in_specs,
        scratch_shapes=list(scratch),
        compiler_params=pltpu.CompilerParams(vmem_limit_bytes=limit * 1024 * 1024),
        cost_estimate=pl.CostEstimate(flops=flops, bytes_accessed=size, transcendentals=exps),
        **more,
    )(*args)


def arr(shape, dtype=BF):
    return jax.ShapeDtypeStruct(shape, dtype)


def turned(values, cosine, sine):
    return values * cosine + pltpu.roll(values, HEAD // 2, 1) * sine


def whole_weight(ref, scratch, first, size):
    if len(ref.shape) == 2:
        return ref[...]
    for b in range(16):
        scratch[pl.ds(b * 96, 96), :] = ref[b, pl.ds(0, 96), pl.ds(first, size)]
    return scratch[...]


def qkv_kernel(flag, xin, gain, weight, bias, cosine, sine, normed, query, kv, scratch):
    whole = whole_weight(weight, scratch, 0, 512)
    cos, sin = cosine[...], sine[...]
    rows = xin[...].astype(F32)
    low = (rows * inverse_rms(rows) * gain[...]).astype(BF)
    normed[...] = low
    out = nn(low, whole) + bias[...]
    for h in range(3):
        query[h] = turned(out[:, h * HEAD : (h + 1) * HEAD], cos, sin).astype(BF)
    last = out[:, QCOLS:]
    last = jnp.where(flag[0] == 1, turned(last, cos, sin), last).astype(BF)
    for b in range(16):
        kv[b] = last


def qkv_columns(flag, xin, gain, weight, bias, cosine, sine):
    return call(
        qkv_kernel,
        (arr((HEAD, WIDTH)), arr((3, HEAD, HEAD)), arr((16, HEAD, HEAD))),
        [SMEM] + [VMEM] * 6,
        (flag, xin, gain, weight, bias, cosine, sine),
        [pltpu.VMEM((WIDTH, 512), BF)],
        flops=2 * 128 * 1536 * 512,
        size=3_000_000,
    )


def key_scores(query_all, keys, key_seg, query_seg, first_key, first_query):
    scores = nt(keys, query_all) * SCALE
    key_pos = first_key + lax.broadcasted_iota(jnp.int32, (CHUNK, HEAD), 0)
    query_pos = first_query + lax.broadcasted_iota(jnp.int32, (CHUNK, HEAD), 1)
    allowed = (key_seg == query_seg) & (key_pos <= query_pos)
    return [jnp.where(allowed, scores[:, h * HEAD : (h + 1) * HEAD], NEG) for h in range(3)]


def attend_kernel(flag, query, kv_mine, kv_other, seg_col, seg_row, out_t, attended, lse, part, top, total, acc, scratch):
    query_all = query[...].reshape(3 * HEAD, HEAD)
    is_key = flag[0] == 1
    first_query = flag[1] * HEAD
    top[...] = jnp.full(top.shape, -3e38, F32)
    total[...] = jnp.zeros(total.shape, F32)
    acc[...] = jnp.zeros(acc.shape, F32)

    @pl.loop(0, SEQ // CHUNK)
    def _(step):
        at = pl.ds(pl.multiple_of(step * CHUNK, CHUNK), CHUNK)
        mine, other = kv_mine[at, :], kv_other[at, :]
        keys = jnp.where(is_key, mine, other)
        values = jnp.where(is_key, other, mine)
        scores = key_scores(query_all, keys, seg_col[at, :], seg_row[...], step * CHUNK, first_query)
        for h in range(3):
            columns = pl.ds(h * HEAD, HEAD)
            old = top[:, columns]
            new = jnp.maximum(old, jnp.max(scores[h], axis=0, keepdims=True))
            shrink = jnp.exp(old - new)
            raised = jnp.exp(scores[h] - new)
            top[:, columns] = new
            total[:, columns] = total[:, columns] * shrink + jnp.sum(raised, axis=0, keepdims=True)
            acc[:, columns] = acc[:, columns] * shrink + tn(values, raised.astype(BF))

    lse[...] = top[...] + jnp.log(total[...])
    done = acc[...] / total[...]
    for h in range(3):
        attended[:, pl.ds(h * HEAD, HEAD)] = done[:, h * HEAD : (h + 1) * HEAD].T.astype(BF)
    out = nt(attended[...], whole_weight(out_t, scratch, 512, QCOLS)).astype(BF)
    for t in range(4):
        part[t] = out[t * 32 : (t + 1) * 32]


def attend(flag, query, kv_mine, kv_other, seg_col, seg_row, out_t):
    return call(
        attend_kernel,
        (arr((HEAD, QCOLS)), arr((1, QCOLS), F32), arr((4, 32, WIDTH))),
        [SMEM] + [VMEM] * 6,
        (flag, query, kv_mine, kv_other, seg_col, seg_row, out_t),
        [
            pltpu.VMEM((1, QCOLS), F32),
            pltpu.VMEM((1, QCOLS), F32),
            pltpu.VMEM((HEAD, QCOLS), F32),
            pltpu.VMEM((WIDTH, QCOLS), BF),
        ],
        flops=4 * 384 * 2048 * 128 + 2 * 128 * 384 * 1536,
        size=3_000_000,
        exps=384 * 2048,
    )


def attend_back_kernel(
    flag, query, kv_mine, kv_other, seg_col, seg_row, lse, grad_att, out_t, cosine, sine,
    grad_query, kept, sent, low, acc, scratch
):
    query_all = query[...].reshape(3 * HEAD, HEAD)
    is_key = flag[0] == 1
    first_query = flag[1] * HEAD
    grad_attended = nn(grad_att[...], whole_weight(out_t, scratch, 512, QCOLS)).astype(BF)
    for h in range(3):
        low[pl.ds(h * HEAD, HEAD), :] = grad_attended[:, h * HEAD : (h + 1) * HEAD]
    grad_rows = low[...]
    lse_row = lse[...]

    def chunk(step):
        at = pl.ds(pl.multiple_of(step * CHUNK, CHUNK), CHUNK)
        mine, other = kv_mine[at, :], kv_other[at, :]
        keys = jnp.where(is_key, mine, other)
        values = jnp.where(is_key, other, mine)
        scores = key_scores(query_all, keys, seg_col[at, :], seg_row[...], step * CHUNK, first_query)
        probs = [jnp.exp(scores[h] - lse_row[:, h * HEAD : (h + 1) * HEAD]) for h in range(3)]
        grad_probs = nt(values, grad_rows)
        return at, keys, probs, grad_probs

    acc[...] = jnp.zeros(acc.shape, F32)

    def row_sums(step, sums):
        _, _, probs, grad_probs = chunk(step)
        return tuple(
            sums[h] + jnp.sum(probs[h] * grad_probs[:, h * HEAD : (h + 1) * HEAD], axis=0, keepdims=True)
            for h in range(3)
        )

    zero = jnp.zeros((1, HEAD), F32)
    sums = lax.fori_loop(0, SEQ // CHUNK, row_sums, (zero, zero, zero))

    @pl.loop(0, SEQ // CHUNK)
    def _(step):
        at, keys, probs, grad_probs = chunk(step)
        low_probs = jnp.concatenate([p.astype(BF) for p in probs], axis=1)
        low_scores = jnp.concatenate(
            [
                (probs[h] * (grad_probs[:, h * HEAD : (h + 1) * HEAD] - sums[h])).astype(BF)
                for h in range(3)
            ],
            axis=1,
        )
        grad_value = nn(low_probs, grad_rows)
        grad_key = nn(low_scores, query_all) * SCALE
        acc[...] += tn(keys, low_scores)
        kept[at, :] = jnp.where(is_key, grad_key, grad_value)
        sent[at, :] = jnp.where(is_key, grad_value, grad_key).astype(BF)

    cos, sin = cosine[...], sine[...]
    for h in range(3):
        rows = acc[:, pl.ds(h * HEAD, HEAD)].T * SCALE
        grad_query[:, pl.ds(h * HEAD, HEAD)] = turned(rows, cos, -sin).astype(BF)


def attend_back(flag, query, kv_mine, kv_other, seg_col, seg_row, lse, grad_att, out_t, cosine, sine):
    return call(
        attend_back_kernel,
        (arr((HEAD, QCOLS)), arr((SEQ, HEAD), F32), arr((SEQ, HEAD))),
        [SMEM] + [VMEM] * 10,
        (flag, query, kv_mine, kv_other, seg_col, seg_row, lse, grad_att, out_t, cosine, sine),
        [pltpu.VMEM((3 * HEAD, HEAD), BF), pltpu.VMEM((HEAD, QCOLS), F32), pltpu.VMEM((WIDTH, QCOLS), BF)],
        flops=14 * 384 * 2048 * 128 + 2 * 128 * 384 * 1536,
        size=5_000_000,
        exps=2 * 384 * 2048,
    )


def qkv_back_kernel(
    flag, pieces, grad_query, weight, xin, cosine, sine, grad_qkv, grad_bias, grad_gain, part, scratch
):
    whole = whole_weight(weight, scratch, 0, 512)
    total = jnp.sum(pieces[...].astype(F32), axis=0)
    total = jnp.where(flag[0] == 1, turned(total, cosine[...], -sine[...]), total).astype(BF)
    grad_qkv[:, pl.ds(0, QCOLS)] = grad_query[...]
    grad_qkv[:, pl.ds(QCOLS, HEAD)] = total
    grads = grad_qkv[...]
    grad_bias[...] = jnp.sum(grads.astype(F32), axis=0, keepdims=True)
    out = nt(grads, whole)
    rows = xin[...].astype(F32)
    grad_gain[...] = jnp.sum(out * rows * inverse_rms(rows), axis=0, keepdims=True)
    low = out.astype(BF)
    for t in range(4):
        part[t] = low[t * 32 : (t + 1) * 32]


def qkv_back(flag, pieces, grad_query, weight, xin, cosine, sine):
    return call(
        qkv_back_kernel,
        (arr((HEAD, 512)), arr((1, 512), F32), arr((1, WIDTH), F32), arr((4, 32, WIDTH))),
        [SMEM] + [VMEM] * 6,
        (flag, pieces, grad_query, weight, xin, cosine, sine),
        [pltpu.VMEM((WIDTH, 512), BF)],
        flops=2 * 128 * 1536 * 512,
        size=3_000_000,
    )


def weight_copies(own, other, gate_up, down, sems, order):
    copies = {}
    for i, ref in enumerate((own, other)):
        for name in order:
            start, size, buffer = (0, GU, gate_up) if name == "gate_up" else (GU, PAD_FF, down)
            copies[i, name] = pltpu.make_async_copy(
                ref.at[:, pl.ds(start, size)], buffer.at[i], sems.at[2 * i + (name == "down")]
            )
    for i in range(2):
        for name in order:
            copies[i, name].start()
    return copies


def feed_kernel(tokens, own, other, part, gate_up_out, gate_up, down, acc, sems):
    copies = weight_copies(own, other, gate_up, down, sems, ("gate_up", "down"))
    rows = tokens[...]
    for i in range(2):
        copies[i, "gate_up"].wait()
        both = nn(rows, gate_up[i])
        gate_up_out[i] = both.astype(BF)
        gate, up = both[:, :PAD_FF], both[:, PAD_FF:]
        hidden = (gate * jax.nn.sigmoid(gate) * up).astype(BF)
        copies[i, "down"].wait()
        out = nt(hidden, down[i])
        if i == 0:
            acc[...] = out
        else:
            part[...] = (acc[...] + out).astype(BF)


FEED_SCRATCH = [
    pltpu.VMEM((2, WIDTH, GU), BF),
    pltpu.VMEM((2, WIDTH, PAD_FF), BF),
    pltpu.VMEM((256, WIDTH), F32),
    pltpu.SemaphoreType.DMA((4,)),
]


def feed(tokens, own, other):
    return call(
        feed_kernel,
        (arr((256, WIDTH)), arr((2, 256, GU))),
        [VMEM, ANY, ANY],
        (tokens, own, other),
        FEED_SCRATCH,
        flops=2 * 256 * 1536 * 3840,
        size=15_000_000,
        exps=256 * 1280,
    )


def feed_back_kernel(grads, own, other, gate_up_in, part, for_own, for_other, gate_up, down, acc, sems):
    copies = weight_copies(own, other, gate_up, down, sems, ("down", "gate_up"))
    rows = grads[...]
    for i, result in enumerate((for_own, for_other)):
        copies[i, "down"].wait()
        grad_hidden = nn(rows, down[i])
        gate = gate_up_in[i, :, pl.ds(0, PAD_FF)].astype(F32)
        up = gate_up_in[i, :, pl.ds(PAD_FF, PAD_FF)].astype(F32)
        sig = jax.nn.sigmoid(gate)
        silu = gate * sig
        result[:, pl.ds(0, PAD_FF)] = (grad_hidden * up * sig * (1.0 + gate * (1.0 - sig))).astype(BF)
        result[:, pl.ds(PAD_FF, PAD_FF)] = (grad_hidden * silu).astype(BF)
        result[:, pl.ds(GU, PAD_FF)] = (silu * up).astype(BF)
        copies[i, "gate_up"].wait()
        out = nt(result[:, pl.ds(0, GU)], gate_up[i])
        if i == 0:
            acc[...] = out
        else:
            part[...] = (acc[...] + out).astype(BF)


def feed_back(grads, own, other, gate_up):
    return call(
        feed_back_kernel,
        (arr((256, WIDTH)), arr((256, FW)), arr((256, FW))),
        [VMEM, ANY, ANY, VMEM],
        (grads, own, other, gate_up),
        FEED_SCRATCH,
        flops=2 * 256 * 1536 * 3840,
        size=17_000_000,
        exps=256 * 1280,
    )


def feed_grad_kernel(tokens, tokens_other, grads, grads_other, own, given, out):
    gate_up, hidden = pl.ds(0, GU), pl.ds(GU, PAD_FF)
    out[:, gate_up] = (tn(tokens[...], own[:, gate_up]) + tn(tokens_other[...], given[:, gate_up])).astype(BF)
    out[:, hidden] = (tn(grads[...], own[:, hidden]) + tn(grads_other[...], given[:, hidden])).astype(BF)


def feed_grad(tokens, tokens_other, grads, grads_other, own, given):
    rows = 256
    columns = pl.BlockSpec((256, rows), lambda i: (0, i))
    fixed = pl.BlockSpec((256, FW), lambda i: (0, 0))
    return call(
        feed_grad_kernel,
        arr((WIDTH, FW)),
        [columns] * 4 + [fixed] * 2,
        (tokens, tokens_other, grads, grads_other, own, given),
        flops=2 * 512 * 1536 * 1920,
        size=12_000_000,
        grid=(WIDTH // rows,),
        out_specs=pl.BlockSpec((rows, FW), lambda i: (i, 0)),
    )


def shifted(value, axis, steps):
    return lax.ppermute(value, axis, [(i, (i + steps) % 4) for i in range(4)])


def ring_first(piece, axis):
    return jnp.stack([piece] + [shifted(piece, axis, j) for j in (1, 2, 3)])


def ring_second(blocks, axis):
    return [blocks] + [shifted(blocks, axis, k) for k in (1, 2, 3)]


def ring_block(place, j, k):
    return lax.rem(place[0] + 4 - j, 4) * place[1] + lax.rem(place[2] + 4 - k, 4) * place[3]


def assemble_kernel(place, *refs):
    pieces, out, tail = refs[:4], refs[4], refs[5] if len(refs) > 5 else None
    for k in range(4):
        for j in range(4):
            block = ring_block(place, j, k)
            out[pl.ds(pl.multiple_of(block * 96, 32), 96), :] = pieces[k][j, pl.ds(0, 96), :]
            if tail is not None:
                tail[block] = pieces[k][j, pl.ds(96, 16), :]


def assemble(place, pieces):
    _, rows, columns = pieces[0].shape
    whole, tail = arr((WIDTH, columns)), arr((16, 16, columns))
    return call(
        assemble_kernel,
        whole if rows == 96 else (whole, tail),
        [SMEM] + [VMEM] * 4,
        (place, *pieces),
        size=4_000_000,
    )


def weight_grad_kernel(normed, grad_qkv, grad_att, attended, out, scratch):
    scratch[:, pl.ds(0, 512)] = tn(normed[...], grad_qkv[...]).astype(BF)
    scratch[:, pl.ds(512, QCOLS)] = tn(grad_att[...], attended[...]).astype(BF)
    for b in range(16):
        out[b % 4, b // 4] = scratch[pl.ds(b * 96, 96), :]


def weight_grad(*args):
    return call(
        weight_grad_kernel,
        arr((4, 4, 96, 896)),
        [VMEM] * 4,
        args,
        [pltpu.VMEM((WIDTH, 896), BF)],
        flops=2 * 128 * 1536 * 896,
        size=6_000_000,
    )


def apart_kernel(place, normed, grad_qkv, grad_att, attended, *rest):
    smalls, outs, scratch = rest[:-5], rest[-5:-1], rest[-1]
    scratch[:, pl.ds(0, 512)] = tn(normed[...], grad_qkv[...]).astype(BF)
    scratch[:, pl.ds(512, QCOLS)] = tn(grad_att[...], attended[...]).astype(BF)
    row_index = lax.broadcasted_iota(jnp.int32, (16, 512), 0)
    for b in range(16):
        y, z = b // 4, b % 4
        rows = jnp.zeros((16, 512), F32)
        for layer in range(2):
            bias, *gains = (ref[...] for ref in smalls[3 * layer : 3 * layer + 3])
            moved = [(pltpu.roll(g, (WIDTH - 96 * b) % WIDTH, 1) if b else g)[:, :HEAD] for g in gains]
            gain_row = jnp.concatenate([*moved, jnp.zeros((1, 2 * HEAD), F32)], axis=1)
            for at, row in ((2 * layer, bias), (2 * layer + 1, gain_row)):
                rows = jnp.where(row_index == at, jnp.broadcast_to(row, (16, 512)), rows)
        rows = rows.astype(BF)
        for k in range(4):

            @pl.when(lax.rem(place[2] + k, 4) == z)
            def _(k=k):
                outs[k][y, pl.ds(0, 96), :] = scratch[pl.ds(b * 96, 96), :]
                outs[k][y, pl.ds(96, 16), pl.ds(0, 512)] = rows
                outs[k][y, pl.ds(96, 16), pl.ds(512, QCOLS)] = jnp.zeros((16, QCOLS), BF)


def apart(place, factors, smalls):
    parts = call(
        apart_kernel,
        (arr((4, 112, 896)),) * 4,
        [SMEM] + [VMEM] * 10,
        (place, *factors, *smalls),
        [pltpu.VMEM((WIDTH, 896), BF)],
        flops=2 * 128 * 1536 * 896,
        size=6_000_000,
    )
    return [parts[0]] + [shifted(parts[k], "z", k) for k in (1, 2, 3)]


def summed(parts):
    return sum(part.astype(F32) for part in parts).astype(BF)


def scatter_blocks(blocks, last):
    y = lax.axis_index("y")
    own, *others = (lax.dynamic_index_in_dim(blocks, lax.rem(y + j, 4), 0, keepdims=False) for j in range(4))
    return summed([own] + [after(shifted(other, "y", j + 1), last) for j, other in enumerate(others)])


def after_heads_kernel(pieces, xin, gain, mixed, second):
    total = xin[...].astype(F32) + jnp.sum(pieces[...].astype(F32), axis=0)
    mixed[...] = total
    low = (total * inverse_rms(total) * gain[...]).astype(BF)
    for t in range(8):
        second[t] = low


def after_heads(pieces, xin, gain):
    return call(
        after_heads_kernel,
        (arr((32, WIDTH), F32), arr((8, 32, WIDTH))),
        [VMEM] * 3,
        (pieces, xin, gain),
        size=1_500_000,
    )


def after_feed_kernel(pieces, mixed, out):
    out[...] = (mixed[...] + jnp.sum(pieces[...].astype(F32), axis=0)).astype(BF)


def after_feed(pieces, mixed):
    return call(after_feed_kernel, arr((32, WIDTH)), [VMEM] * 2, (pieces, mixed), size=1_500_000)


def norm_back(grad, values, gain, grad_out):
    inverse = inverse_rms(values)
    norm = values * inverse
    scaled = grad * gain
    grad_gain = jnp.sum(grad * norm, axis=0, keepdims=True)
    return grad_out + inverse * (scaled - norm * jnp.mean(scaled * norm, axis=-1, keepdims=True)), grad_gain


def before_heads_kernel(pieces, mixed, gain, grad_out, grad_mixed, low, grad_gain):
    grad = jnp.sum(pieces[...].astype(F32), axis=0)
    result, sums = norm_back(grad, mixed[...], gain[...], grad_out[...].astype(F32))
    grad_mixed[...] = result
    low[...] = result.astype(BF)
    grad_gain[...] = sums


def before_heads(pieces, mixed, gain, grad_out):
    return call(
        before_heads_kernel,
        (arr((32, WIDTH), F32), arr((32, WIDTH)), arr((1, WIDTH), F32)),
        [VMEM] * 4,
        (pieces, mixed, gain, grad_out),
        size=1_500_000,
    )


def layer_start_kernel(pieces, xin, gain, grad_mixed, grad_in, spread):
    grad = jnp.sum(pieces[...].astype(F32), axis=0)
    result, _ = norm_back(grad, xin[...].astype(F32), gain[...], grad_mixed[...])
    low = result.astype(BF)
    grad_in[...] = low
    for t in range(8):
        spread[t] = low


def layer_start(pieces, xin, gain, grad_mixed):
    return call(
        layer_start_kernel,
        (arr((32, WIDTH)), arr((8, 32, WIDTH))),
        [VMEM] * 4,
        (pieces, xin, gain, grad_mixed),
        size=1_500_000,
    )


def pack_kernel(gate, up, down, out):
    out[...] = jnp.zeros(out.shape, BF)
    for z in range(4):
        first = z * PAD_FF
        size = min(PAD_FF, 4 * LOCAL_FF - first)
        pieces = (
            gate[:, pl.ds(first, size)],
            up[:, pl.ds(first, size)],
            down[pl.ds(first, size), :].astype(F32).T.astype(BF),
        )
        for s in range(2):
            for i, piece in enumerate(pieces):
                out[4 * s + z, :, pl.ds(i * PAD_FF, size)] = piece


def pack(gate, up, down):
    return call(pack_kernel, arr((8, 96, FW)), [VMEM] * 3, (gate, up, down), size=4_500_000)


def halves_kernel(pieces, first, second):
    first[...] = pieces[:4].reshape(384, FW)
    second[...] = pieces[4:].reshape(384, FW)


def halves(pieces):
    return call(halves_kernel, (arr((384, FW)), arr((384, FW))), [VMEM], (pieces,), size=6_000_000)


def unpack_kernel(pieces, gate, up, down):
    for z in range(4):
        first = z * PAD_FF
        size = min(PAD_FF, 4 * LOCAL_FF - first)
        total = pieces[z].astype(F32) + pieces[4 + z].astype(F32)
        gate[:, pl.ds(first, size)] = total[:, :size]
        up[:, pl.ds(first, size)] = total[:, PAD_FF : PAD_FF + size]
        down[pl.ds(first, size), :] = total[:, GU : GU + size].T


def unpack(pieces):
    wide = 4 * LOCAL_FF
    return call(
        unpack_kernel,
        (arr((96, wide), F32), arr((96, wide), F32), arr((wide, 96), F32)),
        [VMEM],
        (pieces,),
        size=7_000_000,
    )


def local(
    inputs, cotangent, segments, gain_one, w_query, b_query, w_keyval, b_keyval, w_out, gain_two, w_gate, w_up, w_down
):
    on_first = lax.axis_index("s") == 0
    core, chip = lax.axis_index("c"), lax.axis_index("x")
    block = lax.axis_index("y") * 4 + lax.axis_index("z")
    member = chip * 2 + core
    flag = jnp.stack([(core == 0).astype(jnp.int32), block.astype(jnp.int32)])

    def pick(first, second):
        return jnp.where(on_first, first, second)

    def gathered(piece, axes):
        return lax.all_gather(piece, axes, axis=0, tiled=True)

    def pair_gather(rows, axis):
        given = swap(rows, axis)
        is_low = lax.axis_index(axis) == 0
        return jnp.concatenate([jnp.where(is_low, rows, given), jnp.where(is_low, given, rows)], axis=0)

    def spread(rows, count, axes):
        return exchange(jnp.broadcast_to(rows[None], (count,) + rows.shape), axes)

    small = jnp.concatenate([gain_one[0], gain_two[0], b_keyval[0], jnp.zeros((72,), BF)])
    kv_blocks = w_keyval[0].reshape(24, 4, HEAD).transpose(1, 0, 2)
    kv_blocks = jnp.stack([kv_blocks[b] for b in BLOCK_ORDER])
    payload = jnp.concatenate(
        [kv_blocks, jnp.broadcast_to(small[None, None], (4, 1, HEAD)), jnp.zeros((4, 7, HEAD), BF)], axis=1
    )
    payload = exchange(jnp.concatenate([payload, payload], axis=0), ("s", "x", "c")).reshape(2, 4, 32, HEAD)
    bias_rows = jnp.pad(b_query, ((0, 15), (0, QCOLS)))
    own = jnp.concatenate([jnp.concatenate([w_query[0], w_out[0].T], axis=1), bias_rows], axis=0)
    other = swap(own, "s")

    def attention_rows(layer, matrices):
        kv = payload[layer]
        kv = jnp.concatenate([kv[:, :24].reshape(96, HEAD), kv[:, 24], jnp.zeros((12, HEAD), BF)], axis=0)
        return jnp.concatenate([matrices[:, :QCOLS], kv], axis=1)

    xin = pick(inputs[0], inputs[1])
    cot = pick(cotangent[0], cotangent[1])
    place_y, place_z = lax.axis_index("y").astype(jnp.int32), lax.axis_index("z").astype(jnp.int32)
    y_then_z = jnp.stack([place_y, jnp.int32(4), place_z, jnp.int32(1)])
    first, second = pick(own, other), pick(other, own)
    rows_first, out_rows = attention_rows(0, first), first[:96, QCOLS:]
    rows_second = jnp.concatenate([attention_rows(1, second), second[:, QCOLS:]], axis=1)
    ffn_packed = after(pack(w_gate[0], w_up[0], w_down[0]), (rows_first, rows_second))
    ffn_pieces = exchange(ffn_packed, ("s", "z"))
    blocks, out_blocks = ring_first(rows_first, "y"), ring_first(out_rows, "y")
    blocks, out_blocks, ffn_pieces = lax.optimization_barrier((blocks, out_blocks, ffn_pieces))
    ffn_halves = halves(ffn_pieces)
    x_block1 = pair_gather(pair_gather(after(xin, ffn_pieces), "c"), "x")
    ring = ring_second(blocks, "z")
    qkv_first, tail_first = assemble(y_then_z, ring)
    out_ring = ring_second(after(out_blocks, ring), "z")

    seg = pick(segments[0], segments[1])
    local_pos = block * HEAD + jnp.arange(HEAD, dtype=jnp.int32)
    inverse_freq = THETA ** (-(jnp.arange(HEAD // 2, dtype=F32) * 2.0) / HEAD)
    angles = local_pos.astype(F32)[:, None] * inverse_freq[None, :]
    cosine = jnp.cos(angles)
    sine = jnp.sin(angles)
    cosine = jnp.concatenate([cosine, cosine], axis=1)
    sine = jnp.concatenate([-sine, sine], axis=1)
    seg_row = lax.dynamic_slice_in_dim(seg, block * HEAD, HEAD, 0)[None]
    seg_col = seg[:, None]

    def smalls(tail):
        bits = tail[:, :4, QCOLS : QCOLS + 56].reshape(64, 56)
        gain_a = bits[:, :24].reshape(1, WIDTH).astype(F32)
        gain_b = bits[:, 24:48].reshape(1, WIDTH).astype(F32)
        kv_bias = lax.dynamic_slice_in_dim(bits[:, 48:].reshape(1, 512), (core * 2 + chip) * HEAD, HEAD, 1)
        bias = jnp.concatenate([tail[:1, 0, :QCOLS], kv_bias], axis=1).astype(F32)
        return gain_a, gain_b, bias

    gain_a1, gain_b1, bias1 = smalls(tail_first)
    normed1, query1, kv = qkv_columns(flag, x_block1, gain_a1, qkv_first, bias1, cosine, sine)
    own1 = gathered(ffn_halves[0], "y")
    all_second = gathered(after(rows_second, kv), ("y", "z")).reshape(16, 112, 896)
    kv_mine1 = exchange(kv, ("y", "z")).reshape(SEQ, HEAD)
    kv_mine1, out_ring = lax.optimization_barrier((kv_mine1, out_ring))
    out_first = assemble(y_then_z, out_ring)
    kv_other1 = swap(kv_mine1, "c")
    attended1, lse1, part = attend(flag, query1, kv_mine1, kv_other1, seg_col, seg_row, out_first)
    other1 = swap(after(own1, kv_mine1), "c")
    mixed1, low = after_heads(after(exchange(part, ("x", "c")), other1), xin, gain_b1)
    second1 = exchange(low, ("z", "x")).reshape(256, WIDTH)
    own2 = gathered(after(ffn_halves[1], second1), "y")
    part, gate_up1 = feed(second1, own1, other1)
    pieces = exchange(part.reshape(8, 32, WIDTH), ("z", "x"))
    out_one = after_feed(pieces, mixed1)

    x_block2 = gathered(out_one, ("x", "c"))
    gain_a2, gain_b2, bias2 = smalls(all_second[:, 96:, :512])
    normed2, query2, kv = qkv_columns(flag, x_block2, gain_a2, all_second, bias2, cosine, sine)
    kv_mine2 = exchange(kv, ("y", "z")).reshape(SEQ, HEAD)
    kv_other2 = swap(kv_mine2, "c")
    attended2, lse2, part = attend(flag, query2, kv_mine2, kv_other2, seg_col, seg_row, all_second)
    mixed2, low = after_heads(exchange(part, ("x", "c")), out_one, gain_b2)
    other2 = swap(after(own2, low), "c")
    second2 = exchange(low, ("z", "x")).reshape(256, WIDTH)
    cot_low = spread(after(cot, second2), 8, ("z", "x")).reshape(256, WIDTH)
    part, gate_up2 = feed(second2, own2, other2)
    part, cot_low = lax.optimization_barrier((part, cot_low))
    out_pieces = exchange(part.reshape(8, 32, WIDTH), ("z", "x"))

    def both(first, second):
        given = swap(pick(second, first), "s")
        return jnp.stack([pick(first, given), pick(given, second)])[None]

    def backward(grad_out, grad_low, gate_up, second, own, other, mixed, gain_b, xin, x_block, gain_a, normed, query,
                 attended, kv_mine, kv_other, lse, weight, out_t, before=None, earlier=None):
        part, for_own, for_other = feed_back(grad_low, own, other, gate_up)
        if before is not None:
            part, before = lax.optimization_barrier((part, before))
        pieces = exchange(part.reshape(8, 32, WIDTH), ("z", "x"))
        given = swap(for_other, "c")
        second_other, grad_other = swap(second, "c"), swap(grad_low, "c")
        grad_ffn = feed_grad(second, second_other, grad_low, grad_other, for_own, given)
        pieces, grad_ffn = lax.optimization_barrier((pieces, grad_ffn))
        grad_mixed, low, grad_gain_b = before_heads(pieces, mixed, gain_b, grad_out)
        grad_att = gathered(low, ("x", "c"))
        if earlier is not None:
            grad_ffn = after(grad_ffn, earlier)
        grad_ffn = lax.psum_scatter(grad_ffn, "y", scatter_dimension=0, tiled=True)
        grad_query, kept_half, sent_half = attend_back(
            flag, query, kv_mine, kv_other, seg_col, seg_row, lse, grad_att, out_t, cosine, sine
        )
        grad_kv = (kept_half + swap(sent_half, "c").astype(F32)).astype(BF)
        grad_kv = exchange(grad_kv.reshape(16, HEAD, HEAD), ("y", "z"))
        grad_qkv, grad_bias, grad_gain_a, part = qkv_back(flag, grad_kv, grad_query, weight, x_block, cosine, sine)
        smalls = (grad_bias, grad_gain_a, grad_gain_b)
        factors = (normed, grad_qkv, grad_att, attended)
        if earlier is None:
            parts = smalls, weight_grad(*factors)
        else:
            parts = apart(y_then_z, factors, smalls + small_two)
            part = after(part, parts[0])
        pieces = exchange(part, ("x", "c"))
        grad_in, low = layer_start(pieces, xin, gain_a, grad_mixed)
        return grad_in, low, grad_ffn, parts

    grad_two, low, ffn_two, attn_two = backward(
        cot, cot_low, gate_up2, second2, own2, other2, mixed2, gain_b2, out_one, x_block2, gain_a2, normed2, query2,
        attended2, kv_mine2, kv_other2, lse2, all_second, all_second, before=out_pieces
    )
    out_two = after_feed(out_pieces, mixed2)
    both_out = both(out_one, out_two)
    grad_low = exchange(low, ("z", "x")).reshape(256, WIDTH)
    small_two, attn_two = attn_two
    grad_low = after(grad_low, (attn_two, both_out))
    attn_two = after(attn_two, (ffn_two, low))
    attn_two = lax.psum_scatter(attn_two.reshape(16 * 96, 896), "z", scatter_dimension=0, tiled=True)
    grad_one, _, ffn_one, parts = backward(
        grad_two, grad_low, gate_up1, second1, own1, other1, mixed1, gain_b1, xin, x_block1, gain_a1, normed1, query1,
        attended1, kv_mine1, kv_other1, lse1, qkv_first, out_first, earlier=attn_two
    )
    ffn_payload = jnp.concatenate([ffn_one, ffn_two], axis=0).reshape(8, 96, FW)
    halfway = summed(parts)
    ffn_sum = exchange(after(ffn_payload, parts), ("s", "z"))
    attn_one = scatter_blocks(halfway, ffn_sum)
    attn_two = lax.psum_scatter(after(attn_two, (ffn_one, grad_one, halfway)), "y", scatter_dimension=0, tiled=True)

    grad_gate, grad_up, grad_down = unpack(ffn_sum)
    given = swap(jnp.concatenate([pick(attn_two, attn_one[:96]), attn_one[96:]], axis=0), "s").astype(F32)
    main = pick(attn_one[:96], attn_two).astype(F32) + given[:96]
    row = pick(attn_one[96], attn_one[98]).astype(F32) + pick(given[96], given[98])
    gains = pick(attn_one[97], attn_one[99]).astype(F32) + pick(given[97], given[99])
    gains = jnp.concatenate([gains[:96].reshape(4, 24), gains[128:224].reshape(4, 24)], axis=1)
    payload = jnp.concatenate(
        [
            main[:, QCOLS:512].reshape(4, 24, HEAD),
            jnp.pad(gains, ((0, 0), (0, HEAD - 48)))[:, None],
            jnp.broadcast_to(row[None, None, QCOLS:512], (4, 1, HEAD)),
            jnp.zeros((4, 6, HEAD), F32),
        ],
        axis=1,
    )
    arrived = [lax.dynamic_index_in_dim(payload, member, 0, keepdims=False)]
    for step in (1, 2, 3):
        given = lax.dynamic_index_in_dim(payload, member ^ step, 0, keepdims=False)
        arrived.append(lax.ppermute(given, ("x", "c"), [(m, m ^ step) for m in range(4)]))
    arrived = jnp.stack(arrived)
    payload = jnp.stack([lax.dynamic_index_in_dim(arrived, member ^ b, 0, keepdims=False) for b in BLOCK_ORDER])
    grad_keyval = payload[:, :24].transpose(1, 0, 2).reshape(24, 512)
    gains = jnp.sum(payload[:, 24], axis=0)
    kv_bias_row = lax.dynamic_index_in_dim(payload[:, 25], lax.axis_index("y"), 0, keepdims=False)
    grad_b_keyval = lax.dynamic_slice_in_dim(kv_bias_row, (lax.axis_index("z") * 4 + member) * 8, 8, 0)

    return (
        both_out,
        both(after(grad_one, ffn_sum), grad_two),
        gains[None, :24],
        main[None, :, :QCOLS],
        row[None, :QCOLS],
        grad_keyval[None],
        grad_b_keyval[None],
        main[:, 512:].T[None],
        gains[None, 24:48],
        grad_gate[None],
        grad_up[None],
        grad_down[None],
    )


def solution(mesh):
    fine = Mesh(np.asarray(mesh.devices).reshape(2, 4, 4, 2, 2), AXES)
    block, member = ("y", "z"), ("x", "c")
    every = block + member
    tokens = P(None, every, None)
    split = P("s", every)
    columns = P("s", block, member)
    rows = P("s", member, block)
    keyval = P("s", every, None)
    outs = P("s", None, every, None)
    return jax.shard_map(
        local,
        mesh=fine,
        in_specs=(
            tokens, tokens, P(), split, columns, P("s", member), keyval, split, rows, split, columns, columns, rows,
        ),
        out_specs=(
            outs, outs, split, columns, P("s", member), keyval, split, rows, split, columns, columns, rows,
        ),
        check_vma=False,
    )
```

```python
import functools

import jax
import jax.numpy as jnp
import numpy as np
from jax import lax
from jax.experimental import pallas as pl
from jax.experimental.pallas import tpu as pltpu
from jax.sharding import Mesh
from jax.sharding import PartitionSpec as P

HEAD = 128
EPS = 1e-06
NEG = -1e30
THETA = 1000000.0
WIDTH = 1536
QCOLS = 384
SEQ = 2048
CHUNK = 512
MAIN = 512
PART = 64
TAIL = 4 * MAIN
GU = 2 * MAIN + 2 * PART
DOWN = MAIN + 2 * PART
FW = GU + DOWN
SCALE = HEAD**-0.5
AXES = ("s", "y", "z", "x", "c")
BLOCK_ORDER = (0, 2, 1, 3)
BF = jnp.bfloat16
F32 = jnp.float32
VMEM = pl.BlockSpec(memory_space=pltpu.VMEM)
SMEM = pl.BlockSpec(memory_space=pltpu.SMEM)
ANY = pl.BlockSpec(memory_space=pl.ANY)


def swap(value, axis):
    return lax.ppermute(value, axis, [(0, 1), (1, 0)])


def exchange(value, axes):
    return lax.all_to_all(value, axes, split_axis=0, concat_axis=0, tiled=True)


def nn(left, right):
    return jnp.dot(left, right, preferred_element_type=F32)


def nt(left, right):
    return lax.dot_general(left, right, (((1,), (1,)), ((), ())), preferred_element_type=F32)


def tn(left, right):
    return lax.dot_general(left, right, (((0,), (0,)), ((), ())), preferred_element_type=F32)


def after(value, done):
    return lax.optimization_barrier((value, done))[0]


def inverse_rms(values):
    return lax.rsqrt(jnp.mean(values * values, axis=-1, keepdims=True) + EPS)


def call(kernel, out_shape, in_specs, args, scratch=(), flops=0, size=0, exps=0, limit=52, **more):
    return pl.pallas_call(
        kernel,
        out_shape=out_shape,
        in_specs=in_specs,
        scratch_shapes=list(scratch),
        compiler_params=pltpu.CompilerParams(vmem_limit_bytes=limit * 1024 * 1024),
        cost_estimate=pl.CostEstimate(flops=flops, bytes_accessed=size, transcendentals=exps),
        **more,
    )(*args)


def arr(shape, dtype=BF):
    return jax.ShapeDtypeStruct(shape, dtype)


def turned(values, cosine, sine):
    return values * cosine + pltpu.roll(values, HEAD // 2, 1) * sine


def fetch(weight, first, into, sem):
    copy = pltpu.make_async_copy(weight.at[:, pl.ds(first, into.shape[1])], into, sem)
    copy.start()
    return copy


def fetched(columns):
    return [pltpu.VMEM((WIDTH, columns), BF), pltpu.SemaphoreType.DMA]


def qkv_kernel(flag, xin, gain, weight, bias, cosine, sine, normed, query, kv, whole, sem):
    copy = fetch(weight, 0, whole, sem)
    cos, sin = cosine[...], sine[...]
    rows = xin[...].astype(F32)
    low = (rows * inverse_rms(rows) * gain[...]).astype(BF)
    normed[...] = low
    copy.wait()
    out = nn(low, whole[...]) + bias[...]
    for h in range(3):
        query[h] = turned(out[:, h * HEAD : (h + 1) * HEAD], cos, sin).astype(BF)
    last = out[:, QCOLS:]
    last = jnp.where(flag[0] == 1, turned(last, cos, sin), last).astype(BF)
    for b in range(16):
        kv[b] = last


def qkv_columns(flag, xin, gain, weight, bias, cosine, sine):
    return call(
        qkv_kernel,
        (arr((HEAD, WIDTH)), arr((3, HEAD, HEAD)), arr((16, HEAD, HEAD))),
        [SMEM, VMEM, VMEM, ANY, VMEM, VMEM, VMEM],
        (flag, xin, gain, weight, bias, cosine, sine),
        fetched(512),
        flops=2 * 128 * 1536 * 512,
        size=3_000_000,
    )


def key_scores(query_all, keys, key_seg, query_seg, first_key, first_query):
    scores = nt(keys, query_all) * SCALE
    key_pos = first_key + lax.broadcasted_iota(jnp.int32, (CHUNK, HEAD), 0)
    query_pos = first_query + lax.broadcasted_iota(jnp.int32, (CHUNK, HEAD), 1)
    allowed = (key_seg == query_seg) & (key_pos <= query_pos)
    return [jnp.where(allowed, scores[:, h * HEAD : (h + 1) * HEAD], NEG) for h in range(3)]


def attend_kernel(
    first, flag, query, kv_mine, kv_other, seg_col, seg_row, weight, attended, lse, part, top, total, acc, out_t, sem
):
    copy = fetch(weight, first, out_t, sem)
    query_all = query[...].reshape(3 * HEAD, HEAD)
    is_key = flag[0] == 1
    first_query = flag[1] * HEAD
    top[...] = jnp.full(top.shape, -3e38, F32)
    total[...] = jnp.zeros(total.shape, F32)
    acc[...] = jnp.zeros(acc.shape, F32)

    @pl.loop(0, SEQ // CHUNK)
    def _(step):
        at = pl.ds(pl.multiple_of(step * CHUNK, CHUNK), CHUNK)
        mine, other = kv_mine[at, :], kv_other[at, :]
        keys = jnp.where(is_key, mine, other)
        values = jnp.where(is_key, other, mine)
        scores = key_scores(query_all, keys, seg_col[at, :], seg_row[...], step * CHUNK, first_query)
        for h in range(3):
            columns = pl.ds(h * HEAD, HEAD)
            old = top[:, columns]
            new = jnp.maximum(old, jnp.max(scores[h], axis=0, keepdims=True))
            shrink = jnp.exp(old - new)
            raised = jnp.exp(scores[h] - new)
            top[:, columns] = new
            total[:, columns] = total[:, columns] * shrink + jnp.sum(raised, axis=0, keepdims=True)
            acc[:, columns] = acc[:, columns] * shrink + tn(values, raised.astype(BF))

    lse[...] = top[...] + jnp.log(total[...])
    done = acc[...] / total[...]
    for h in range(3):
        attended[:, pl.ds(h * HEAD, HEAD)] = done[:, h * HEAD : (h + 1) * HEAD].T.astype(BF)
    copy.wait()
    out = nt(attended[...], out_t[...]).astype(BF)
    for t in range(4):
        part[t] = out[t * 32 : (t + 1) * 32]


def attend(flag, query, kv_mine, kv_other, seg_col, seg_row, weight, first):
    return call(
        functools.partial(attend_kernel, first),
        (arr((HEAD, QCOLS)), arr((1, QCOLS), F32), arr((4, 32, WIDTH))),
        [SMEM] + [VMEM] * 5 + [ANY],
        (flag, query, kv_mine, kv_other, seg_col, seg_row, weight),
        [
            pltpu.VMEM((1, QCOLS), F32),
            pltpu.VMEM((1, QCOLS), F32),
            pltpu.VMEM((HEAD, QCOLS), F32),
            *fetched(QCOLS),
        ],
        flops=4 * 384 * 2048 * 128 + 2 * 128 * 384 * 1536,
        size=3_000_000,
        exps=384 * 2048,
    )


def attend_back_kernel(
    first, flag, query, kv_mine, kv_other, seg_col, seg_row, lse, attended, grad_att, cosine, sine, weight,
    grad_query, kept, sent, low, acc, out_t, sem
):
    copy = fetch(weight, first, out_t, sem)
    query_all = query[...].reshape(3 * HEAD, HEAD)
    is_key = flag[0] == 1
    first_query = flag[1] * HEAD
    sums = []
    copy.wait()
    grad_attended = nn(grad_att[...], out_t[...]).astype(BF)
    for h in range(3):
        grad_head = grad_attended[:, h * HEAD : (h + 1) * HEAD]
        low[pl.ds(h * HEAD, HEAD), :] = grad_head
        with_output = grad_head.astype(F32) * attended[:, pl.ds(h * HEAD, HEAD)].astype(F32)
        sums.append(jnp.sum(with_output.T, axis=0, keepdims=True))
    grad_rows = low[...]
    lse_row = lse[...]

    def chunk(step):
        at = pl.ds(pl.multiple_of(step * CHUNK, CHUNK), CHUNK)
        mine, other = kv_mine[at, :], kv_other[at, :]
        keys = jnp.where(is_key, mine, other)
        values = jnp.where(is_key, other, mine)
        scores = key_scores(query_all, keys, seg_col[at, :], seg_row[...], step * CHUNK, first_query)
        probs = [jnp.exp(scores[h] - lse_row[:, h * HEAD : (h + 1) * HEAD]) for h in range(3)]
        grad_probs = nt(values, grad_rows)
        return at, keys, probs, grad_probs

    acc[...] = jnp.zeros(acc.shape, F32)

    @pl.loop(0, SEQ // CHUNK)
    def _(step):
        at, keys, probs, grad_probs = chunk(step)
        low_probs = jnp.concatenate([p.astype(BF) for p in probs], axis=1)
        low_scores = jnp.concatenate(
            [
                (probs[h] * (grad_probs[:, h * HEAD : (h + 1) * HEAD] - sums[h])).astype(BF)
                for h in range(3)
            ],
            axis=1,
        )
        grad_value = nn(low_probs, grad_rows)
        grad_key = nn(low_scores, query_all) * SCALE
        acc[...] += tn(keys, low_scores)
        kept[at, :] = jnp.where(is_key, grad_key, grad_value)
        sent[at, :] = jnp.where(is_key, grad_value, grad_key).astype(BF)

    cos, sin = cosine[...], sine[...]
    for h in range(3):
        rows = acc[:, pl.ds(h * HEAD, HEAD)].T * SCALE
        grad_query[:, pl.ds(h * HEAD, HEAD)] = turned(rows, cos, -sin).astype(BF)


def attend_back(flag, query, kv_mine, kv_other, seg_col, seg_row, lse, attended, grad_att, cosine, sine, weight, first):
    return call(
        functools.partial(attend_back_kernel, first),
        (arr((HEAD, QCOLS)), arr((SEQ, HEAD), F32), arr((SEQ, HEAD))),
        [SMEM] + [VMEM] * 10 + [ANY],
        (flag, query, kv_mine, kv_other, seg_col, seg_row, lse, attended, grad_att, cosine, sine, weight),
        [pltpu.VMEM((3 * HEAD, HEAD), BF), pltpu.VMEM((HEAD, QCOLS), F32), *fetched(QCOLS)],
        flops=10 * 384 * 2048 * 128 + 2 * 128 * 384 * 1536,
        size=5_000_000,
        exps=2 * 384 * 2048,
    )


def qkv_back_kernel(
    flag, pieces, grad_query, weight, xin, cosine, sine, grad_qkv, grad_bias, grad_gain, part, whole, sem
):
    copy = fetch(weight, 0, whole, sem)
    total = jnp.sum(pieces[...].astype(F32), axis=0)
    total = jnp.where(flag[0] == 1, turned(total, cosine[...], -sine[...]), total).astype(BF)
    grad_qkv[:, pl.ds(0, QCOLS)] = grad_query[...]
    grad_qkv[:, pl.ds(QCOLS, HEAD)] = total
    grads = grad_qkv[...]
    grad_bias[...] = jnp.sum(grads.astype(F32), axis=0, keepdims=True)
    copy.wait()
    out = nt(grads, whole[...])
    rows = xin[...].astype(F32)
    grad_gain[...] = jnp.sum(out * rows * inverse_rms(rows), axis=0, keepdims=True)
    low = out.astype(BF)
    for t in range(4):
        part[t] = low[t * 32 : (t + 1) * 32]


def qkv_back(flag, pieces, grad_query, weight, xin, cosine, sine):
    return call(
        qkv_back_kernel,
        (arr((HEAD, 512)), arr((1, 512), F32), arr((1, WIDTH), F32), arr((4, 32, WIDTH))),
        [SMEM, VMEM, VMEM, ANY, VMEM, VMEM, VMEM],
        (flag, pieces, grad_query, weight, xin, cosine, sine),
        fetched(512),
        flops=2 * 128 * 1536 * 512,
        size=3_000_000,
    )


def weight_copies(own, other, gate_up, down, sems, order):
    copies = {}
    for i, ref in enumerate((own, other)):
        for name in order:
            start, size, buffer = (0, GU, gate_up) if name == "gate_up" else (GU, DOWN, down)
            copies[i, name] = pltpu.make_async_copy(
                ref.at[:, pl.ds(start, size)], buffer.at[i], sems.at[2 * i + (name == "down")]
            )
    for i in range(2):
        for name in order:
            copies[i, name].start()
    return copies


def gate_and_up(both):
    tail = both[:, 2 * MAIN :]
    gate = jnp.concatenate([both[:, :MAIN], tail], axis=1)
    return gate, jnp.concatenate([both[:, MAIN : 2 * MAIN], pltpu.roll(tail, PART, 1)], axis=1)


def known(hidden):
    lane = lax.broadcasted_iota(jnp.int32, hidden.shape, 1)
    return jnp.where(lane < MAIN + PART, hidden, 0.0)


def feed_kernel(tokens, own, other, part, gate_up_out, gate_up, down, acc, sems):
    copies = weight_copies(own, other, gate_up, down, sems, ("gate_up", "down"))
    rows = tokens[...]
    for i in range(2):
        copies[i, "gate_up"].wait()
        both = nn(rows, gate_up[i])
        gate_up_out[i] = both.astype(BF)
        gate, up = gate_and_up(both)
        hidden = known(gate * jax.nn.sigmoid(gate) * up).astype(BF)
        copies[i, "down"].wait()
        out = nt(hidden, down[i])
        if i == 0:
            acc[...] = out
        else:
            part[...] = (acc[...] + out).astype(BF)


FEED_SCRATCH = [
    pltpu.VMEM((2, WIDTH, GU), BF),
    pltpu.VMEM((2, WIDTH, DOWN), BF),
    pltpu.VMEM((256, WIDTH), F32),
    pltpu.SemaphoreType.DMA((4,)),
]


def feed(tokens, own, other):
    return call(
        feed_kernel,
        (arr((256, WIDTH)), arr((2, 256, GU))),
        [VMEM, ANY, ANY],
        (tokens, own, other),
        FEED_SCRATCH,
        flops=2 * 256 * 1536 * 3840,
        size=15_000_000,
        exps=256 * 1280,
    )


def feed_back_kernel(grads, own, other, gate_up_in, part, for_own, for_other, gate_up, down, acc, sems):
    copies = weight_copies(own, other, gate_up, down, sems, ("down", "gate_up"))
    rows = grads[...]
    for i, result in enumerate((for_own, for_other)):
        copies[i, "down"].wait()
        grad_hidden = nn(rows, down[i])
        gate, up = gate_and_up(gate_up_in[i].astype(F32))
        sig = jax.nn.sigmoid(gate)
        silu = gate * sig
        grad_gate = grad_hidden * up * sig * (1.0 + gate * (1.0 - sig))
        grad_up = grad_hidden * silu
        tail = grad_gate[:, MAIN:] + pltpu.roll(grad_up[:, MAIN:], PART, 1)
        result[:, pl.ds(0, MAIN)] = grad_gate[:, :MAIN].astype(BF)
        result[:, pl.ds(MAIN, MAIN)] = grad_up[:, :MAIN].astype(BF)
        result[:, pl.ds(2 * MAIN, 2 * PART)] = tail.astype(BF)
        result[:, pl.ds(GU, DOWN)] = known(silu * up).astype(BF)
        copies[i, "gate_up"].wait()
        out = nt(result[:, pl.ds(0, GU)], gate_up[i])
        if i == 0:
            acc[...] = out
        else:
            part[...] = (acc[...] + out).astype(BF)


def feed_back(grads, own, other, gate_up):
    return call(
        feed_back_kernel,
        (arr((256, WIDTH)), arr((256, FW)), arr((256, FW))),
        [VMEM, ANY, ANY, VMEM],
        (grads, own, other, gate_up),
        FEED_SCRATCH,
        flops=2 * 256 * 1536 * 3840,
        size=17_000_000,
        exps=256 * 1280,
    )


def feed_grad_kernel(tokens, tokens_other, grads, grads_other, own, given, out):
    gate_up, hidden = pl.ds(0, GU), pl.ds(GU, DOWN)
    out[:, gate_up] = (tn(tokens[...], own[:, gate_up]) + tn(tokens_other[...], given[:, gate_up])).astype(BF)
    out[:, hidden] = (tn(grads[...], own[:, hidden]) + tn(grads_other[...], given[:, hidden])).astype(BF)


def feed_grad(tokens, tokens_other, grads, grads_other, own, given):
    rows = 256
    columns = pl.BlockSpec((256, rows), lambda i: (0, i))
    fixed = pl.BlockSpec((256, FW), lambda i: (0, 0))
    return call(
        feed_grad_kernel,
        arr((WIDTH, FW)),
        [columns] * 4 + [fixed] * 2,
        (tokens, tokens_other, grads, grads_other, own, given),
        flops=2 * 512 * 1536 * 1920,
        size=12_000_000,
        grid=(WIDTH // rows,),
        out_specs=pl.BlockSpec((rows, FW), lambda i: (i, 0)),
    )


def shifted(value, axis, steps):
    return lax.ppermute(value, axis, [(i, (i + steps) % 4) for i in range(4)])


def ring_first(piece, axis):
    return jnp.stack([piece] + [shifted(piece, axis, j) for j in (1, 2, 3)])


def ring_second(blocks, axis):
    return [blocks] + [shifted(blocks, axis, k) for k in (1, 2, 3)]


def ring_block(place, j, k):
    return lax.rem(place[0] + 4 - j, 4) * place[1] + lax.rem(place[2] + 4 - k, 4) * place[3]


def assemble_kernel(place, *refs):
    pieces, out, tail = refs[:4], refs[4], refs[5] if len(refs) > 5 else None
    for k in range(4):
        for j in range(4):
            block = ring_block(place, j, k)
            out[pl.ds(pl.multiple_of(block * 96, 32), 96), :] = pieces[k][j, pl.ds(0, 96), :]
            if tail is not None:
                tail[block] = pieces[k][j, pl.ds(96, 16), :]


def assemble(place, pieces):
    _, rows, columns = pieces[0].shape
    whole, tail = arr((WIDTH, columns)), arr((16, 16, columns))
    return call(
        assemble_kernel,
        whole if rows == 96 else (whole, tail),
        [SMEM] + [VMEM] * 4,
        (place, *pieces),
        size=4_000_000,
    )


def weight_grad_kernel(normed, grad_qkv, grad_att, attended, out, scratch):
    scratch[:, pl.ds(0, 512)] = tn(normed[...], grad_qkv[...]).astype(BF)
    scratch[:, pl.ds(512, QCOLS)] = tn(grad_att[...], attended[...]).astype(BF)
    for b in range(16):
        out[b % 4, b // 4] = scratch[pl.ds(b * 96, 96), :]


def weight_grad(*args):
    return call(
        weight_grad_kernel,
        arr((4, 4, 96, 896)),
        [VMEM] * 4,
        args,
        [pltpu.VMEM((WIDTH, 896), BF)],
        flops=2 * 128 * 1536 * 896,
        size=6_000_000,
    )


def apart_kernel(place, normed, grad_qkv, grad_att, attended, *rest):
    smalls, outs, scratch, scratch_out = rest[:-10], rest[-10:-2], rest[-2], rest[-1]
    scratch[...] = tn(normed[...], grad_qkv[...]).astype(BF)
    scratch_out[...] = tn(grad_att[...], attended[...]).astype(BF)
    row_index = lax.broadcasted_iota(jnp.int32, (16, 512), 0)
    for b in range(16):
        y, z = b // 4, b % 4
        rows = jnp.zeros((16, 512), F32)
        for layer in range(2):
            bias, *gains = (ref[...] for ref in smalls[3 * layer : 3 * layer + 3])
            moved = [(pltpu.roll(g, (WIDTH - 96 * b) % WIDTH, 1) if b else g)[:, :HEAD] for g in gains]
            gain_row = jnp.concatenate([*moved, jnp.zeros((1, 2 * HEAD), F32)], axis=1)
            for at, row in ((2 * layer, bias), (2 * layer + 1, gain_row)):
                rows = jnp.where(row_index == at, jnp.broadcast_to(row, (16, 512)), rows)
        rows = rows.astype(BF)
        for k in range(4):

            @pl.when(lax.rem(place[2] + k, 4) == z)
            def _(k=k):
                outs[k][y, pl.ds(0, 96), :] = scratch[pl.ds(b * 96, 96), :]
                outs[k][y, pl.ds(96, 16), :] = rows

            @pl.when(lax.rem(place[0] + k, 4) == y)
            def _(k=k):
                outs[4 + k][z] = scratch_out[pl.ds(b * 96, 96), :]


def apart(place, factors, smalls):
    parts = call(
        apart_kernel,
        (arr((4, 112, 512)),) * 4 + (arr((4, 96, QCOLS)),) * 4,
        [SMEM] + [VMEM] * 10,
        (place, *factors, *smalls),
        [pltpu.VMEM((WIDTH, 512), BF), pltpu.VMEM((WIDTH, QCOLS), BF)],
        flops=2 * 128 * 1536 * 896,
        size=6_000_000,
    )
    return parts[:4], parts[4:]


def sent(parts, axis):
    return [parts[0]] + [shifted(parts[k], axis, k) for k in (1, 2, 3)]


def summed(parts):
    return sum(part.astype(F32) for part in parts).astype(BF)


def scatter_blocks(blocks, axis, last):
    here = lax.axis_index(axis)
    own, *others = (lax.dynamic_index_in_dim(blocks, lax.rem(here + j, 4), 0, keepdims=False) for j in range(4))
    return summed([own] + [after(shifted(other, axis, j + 1), last) for j, other in enumerate(others)])


def after_heads_kernel(pieces, xin, gain, mixed, second):
    total = xin[...].astype(F32) + jnp.sum(pieces[...].astype(F32), axis=0)
    mixed[...] = total
    low = (total * inverse_rms(total) * gain[...]).astype(BF)
    for t in range(8):
        second[t] = low


def after_heads(pieces, xin, gain):
    return call(
        after_heads_kernel,
        (arr((32, WIDTH), F32), arr((8, 32, WIDTH))),
        [VMEM] * 3,
        (pieces, xin, gain),
        size=1_500_000,
    )


def after_feed_kernel(pieces, mixed, out):
    out[...] = (mixed[...] + jnp.sum(pieces[...].astype(F32), axis=0)).astype(BF)


def after_feed(pieces, mixed):
    return call(after_feed_kernel, arr((32, WIDTH)), [VMEM] * 2, (pieces, mixed), size=1_500_000)


def norm_back(grad, values, gain, grad_out):
    inverse = inverse_rms(values)
    norm = values * inverse
    scaled = grad * gain
    grad_gain = jnp.sum(grad * norm, axis=0, keepdims=True)
    return grad_out + inverse * (scaled - norm * jnp.mean(scaled * norm, axis=-1, keepdims=True)), grad_gain


def before_heads_kernel(pieces, mixed, gain, grad_out, grad_mixed, low, grad_gain):
    grad = jnp.sum(pieces[...].astype(F32), axis=0)
    result, sums = norm_back(grad, mixed[...], gain[...], grad_out[...].astype(F32))
    grad_mixed[...] = result
    low[...] = result.astype(BF)
    grad_gain[...] = sums


def before_heads(pieces, mixed, gain, grad_out):
    return call(
        before_heads_kernel,
        (arr((32, WIDTH), F32), arr((32, WIDTH)), arr((1, WIDTH), F32)),
        [VMEM] * 4,
        (pieces, mixed, gain, grad_out),
        size=1_500_000,
    )


def layer_start_kernel(pieces, xin, gain, grad_mixed, grad_in, spread):
    grad = jnp.sum(pieces[...].astype(F32), axis=0)
    result, _ = norm_back(grad, xin[...].astype(F32), gain[...], grad_mixed[...])
    low = result.astype(BF)
    grad_in[...] = low
    for t in range(8):
        spread[t] = low


def layer_start(pieces, xin, gain, grad_mixed):
    return call(
        layer_start_kernel,
        (arr((32, WIDTH)), arr((8, 32, WIDTH))),
        [VMEM] * 4,
        (pieces, xin, gain, grad_mixed),
        size=1_500_000,
    )


def pack_kernel(gate, up, down, tails, out):
    for z in range(4):
        main = pl.ds(z * MAIN, MAIN)
        pieces = (
            (0, gate[:, main]),
            (MAIN, up[:, main]),
            (2 * MAIN, tails[z, :, pl.ds(0, 2 * PART)]),
            (GU, down[main, :].astype(F32).T.astype(BF)),
            (GU + MAIN, tails[z, :, pl.ds(2 * PART, 2 * PART)]),
        )
        for s in range(2):
            for at, piece in pieces:
                out[4 * s + z, :, pl.ds(at, piece.shape[1])] = piece


def pack(gate, up, down):
    rest = [jnp.pad(w, ((0, 0), (0, PART))).reshape(96, 4, PART) for w in (gate[:, TAIL:], up[:, TAIL:], down[TAIL:].T)]
    tails = jnp.concatenate([*rest, jnp.zeros((96, 4, PART), BF)], axis=2).transpose(1, 0, 2)
    return call(pack_kernel, arr((8, 96, FW)), [VMEM] * 4, (gate, up, down, tails), size=4_500_000)


def halves_kernel(pieces, first, second):
    first[...] = pieces[:4].reshape(384, FW)
    second[...] = pieces[4:].reshape(384, FW)


def halves(pieces):
    return call(halves_kernel, (arr((384, FW)), arr((384, FW))), [VMEM], (pieces,), size=6_000_000)


def unpack_kernel(pieces, gate, up, down):
    low = lax.broadcasted_iota(jnp.int32, (96, 2 * PART), 1) < PART
    tails = []
    for z in range(4):
        main = pl.ds(z * MAIN, MAIN)
        total = pieces[z].astype(F32) + pieces[4 + z].astype(F32)
        gate[:, main] = total[:, :MAIN]
        up[:, main] = total[:, MAIN : 2 * MAIN]
        down[main, :] = total[:, GU : GU + MAIN].T
        if z < 3:
            tails.append(total[:, 2 * MAIN : GU])
            down[pl.ds(TAIL + z * PART, PART), :] = total[:, GU + MAIN :].T[:PART]
    turned_tails = [pltpu.roll(tail, PART, 1) for tail in tails]
    gate[:, pl.ds(TAIL, 2 * PART)] = jnp.where(low, tails[0], turned_tails[1])
    gate[:, pl.ds(TAIL + 2 * PART, PART)] = tails[2][:, :PART]
    up[:, pl.ds(TAIL, 2 * PART)] = jnp.where(low, turned_tails[0], tails[1])
    up[:, pl.ds(TAIL + 2 * PART, PART)] = turned_tails[2][:, :PART]


def unpack(pieces):
    wide = TAIL + 3 * PART
    return call(
        unpack_kernel,
        (arr((96, wide), F32), arr((96, wide), F32), arr((wide, 96), F32)),
        [VMEM],
        (pieces,),
        size=7_000_000,
    )


def local(
    inputs, cotangent, segments, gain_one, w_query, b_query, w_keyval, b_keyval, w_out, gain_two, w_gate, w_up, w_down
):
    on_first = lax.axis_index("s") == 0
    core, chip = lax.axis_index("c"), lax.axis_index("x")
    block = lax.axis_index("y") * 4 + lax.axis_index("z")
    member = chip * 2 + core
    flag = jnp.stack([(core == 0).astype(jnp.int32), block.astype(jnp.int32)])

    def pick(first, second):
        return jnp.where(on_first, first, second)

    def gathered(piece, axes):
        return lax.all_gather(piece, axes, axis=0, tiled=True)

    def pair_gather(rows, axis):
        given = swap(rows, axis)
        is_low = lax.axis_index(axis) == 0
        return jnp.concatenate([jnp.where(is_low, rows, given), jnp.where(is_low, given, rows)], axis=0)

    def spread(rows, count, axes):
        return exchange(jnp.broadcast_to(rows[None], (count,) + rows.shape), axes)

    small = jnp.concatenate([gain_one[0], gain_two[0], b_keyval[0], jnp.zeros((72,), BF)])
    kv_blocks = w_keyval[0].reshape(24, 4, HEAD).transpose(1, 0, 2)
    kv_blocks = jnp.stack([kv_blocks[b] for b in BLOCK_ORDER])
    payload = jnp.concatenate(
        [kv_blocks, jnp.broadcast_to(small[None, None], (4, 1, HEAD)), jnp.zeros((4, 7, HEAD), BF)], axis=1
    )
    payload = exchange(jnp.concatenate([payload, payload], axis=0), ("s", "x", "c")).reshape(2, 4, 32, HEAD)
    bias_rows = jnp.pad(b_query, ((0, 15), (0, QCOLS)))
    own = jnp.concatenate([jnp.concatenate([w_query[0], w_out[0].T], axis=1), bias_rows], axis=0)
    other = swap(own, "s")

    def attention_rows(layer, matrices):
        return jnp.concatenate([matrices[:96, :QCOLS], payload[layer, :, :24].reshape(96, HEAD)], axis=1)

    def small_rows(layer, matrices):
        return jnp.concatenate([matrices[96:100, :QCOLS], payload[layer, :, 24]], axis=1)

    xin = pick(inputs[0], inputs[1])
    cot = pick(cotangent[0], cotangent[1])
    place_y, place_z = lax.axis_index("y").astype(jnp.int32), lax.axis_index("z").astype(jnp.int32)
    y_then_z = jnp.stack([place_y, jnp.int32(4), place_z, jnp.int32(1)])
    first, second = pick(own, other), pick(other, own)
    rows_first, out_rows = attention_rows(0, first), first[:96, QCOLS:]
    tails = [small_rows(0, first), small_rows(1, second), jnp.zeros((8, 512), BF)]
    rows_first = jnp.concatenate([rows_first, *tails], axis=0)
    rows_second = jnp.concatenate([attention_rows(1, second), second[:96, QCOLS:]], axis=1)
    ffn_packed = after(pack(w_gate[0], w_up[0], w_down[0]), (rows_first, rows_second))
    ffn_pieces = exchange(ffn_packed, ("s", "z"))
    blocks, out_blocks = ring_first(rows_first, "y"), ring_first(out_rows, "y")
    blocks, out_blocks, ffn_pieces = lax.optimization_barrier((blocks, out_blocks, ffn_pieces))
    ffn_halves = halves(ffn_pieces)
    x_block1 = pair_gather(pair_gather(after(xin, ffn_pieces), "c"), "x")
    ring = ring_second(blocks, "z")
    qkv_first, tail_first = assemble(y_then_z, ring)
    out_ring = ring_second(after(out_blocks, (ring[1], ring[3])), "z")

    seg = pick(segments[0], segments[1])
    local_pos = block * HEAD + jnp.arange(HEAD, dtype=jnp.int32)
    inverse_freq = THETA ** (-(jnp.arange(HEAD // 2, dtype=F32) * 2.0) / HEAD)
    angles = local_pos.astype(F32)[:, None] * inverse_freq[None, :]
    cosine = jnp.cos(angles)
    sine = jnp.sin(angles)
    cosine = jnp.concatenate([cosine, cosine], axis=1)
    sine = jnp.concatenate([-sine, sine], axis=1)
    seg_row = lax.dynamic_slice_in_dim(seg, block * HEAD, HEAD, 0)[None]
    seg_col = seg[:, None]

    def smalls(tail):
        bits = tail[:, :, QCOLS : QCOLS + 56].reshape(64, 56)
        gain_a = bits[:, :24].reshape(1, WIDTH).astype(F32)
        gain_b = bits[:, 24:48].reshape(1, WIDTH).astype(F32)
        kv_bias = lax.dynamic_slice_in_dim(bits[:, 48:].reshape(1, 512), (core * 2 + chip) * HEAD, HEAD, 1)
        bias = jnp.concatenate([tail[:1, 0, :QCOLS], kv_bias], axis=1).astype(F32)
        return gain_a, gain_b, bias

    gain_a1, gain_b1, bias1 = smalls(tail_first[:, :4])
    normed1, query1, kv = qkv_columns(flag, x_block1, gain_a1, qkv_first, bias1, cosine, sine)
    own1 = gathered(ffn_halves[0], "y")
    all_second = gathered(after(rows_second, kv), ("y", "z"))
    kv, out_ring = lax.optimization_barrier((kv, out_ring))
    out_first = assemble(y_then_z, out_ring)
    kv_mine1 = exchange(kv, ("y", "z")).reshape(SEQ, HEAD)
    kv_other1 = swap(kv_mine1, "c")
    attended1, lse1, part = attend(flag, query1, kv_mine1, kv_other1, seg_col, seg_row, out_first, 0)
    other1 = swap(after(own1, part), "c")
    mixed1, low = after_heads(after(exchange(part, ("x", "c")), other1), xin, gain_b1)
    second1 = exchange(low, ("z", "x")).reshape(256, WIDTH)
    own2 = gathered(after(ffn_halves[1], second1), "y")
    part, gate_up1 = feed(second1, own1, other1)
    pieces = exchange(part.reshape(8, 32, WIDTH), ("z", "x"))
    out_one = after_feed(pieces, mixed1)

    x_block2 = gathered(out_one, ("x", "c"))
    gain_a2, gain_b2, bias2 = smalls(tail_first[:, 4:8])
    normed2, query2, kv = qkv_columns(flag, x_block2, gain_a2, all_second, bias2, cosine, sine)
    kv_mine2 = exchange(kv, ("y", "z")).reshape(SEQ, HEAD)
    kv_other2 = swap(kv_mine2, "c")
    attended2, lse2, part = attend(flag, query2, kv_mine2, kv_other2, seg_col, seg_row, all_second, 512)
    mixed2, low = after_heads(exchange(part, ("x", "c")), out_one, gain_b2)
    second2 = exchange(low, ("z", "x")).reshape(256, WIDTH)
    other2 = swap(after(own2, second2), "c")
    cot_low = spread(after(cot, (second2, own2)), 8, ("z", "x")).reshape(256, WIDTH)
    second2 = after(second2, cot_low)
    part, gate_up2 = feed(second2, own2, other2)
    out_pieces = exchange(part.reshape(8, 32, WIDTH), ("z", "x"))

    def backward(grad_out, grad_low, gate_up, second, own, other, mixed, gain_b, xin, x_block, gain_a, normed, query,
                 attended, kv_mine, kv_other, lse, weight, out_t, first, before=None, earlier=None):
        part, for_own, for_other = feed_back(grad_low, own, other, gate_up)
        if before is not None:
            part, before = lax.optimization_barrier((part, before))
        pieces = exchange(part.reshape(8, 32, WIDTH), ("z", "x"))
        given = swap(for_other, "c")
        second_other, grad_other = swap(second, "c"), swap(grad_low, "c")
        grad_ffn = feed_grad(second, second_other, grad_low, grad_other, for_own, given)
        pieces, grad_ffn = lax.optimization_barrier((pieces, grad_ffn))
        grad_mixed, low, grad_gain_b = before_heads(pieces, mixed, gain_b, grad_out)
        grad_att = gathered(low, ("x", "c"))
        if earlier is not None:
            grad_ffn = after(grad_ffn, earlier)
        grad_ffn = lax.psum_scatter(grad_ffn, "y", scatter_dimension=0, tiled=True)
        grad_query, kept_half, sent_half = attend_back(
            flag, query, kv_mine, kv_other, seg_col, seg_row, lse, attended, grad_att, cosine, sine, out_t, first
        )
        grad_kv = (kept_half + swap(sent_half, "c").astype(F32)).astype(BF)
        grad_kv = exchange(grad_kv.reshape(16, HEAD, HEAD), ("y", "z"))
        grad_qkv, grad_bias, grad_gain_a, part = qkv_back(flag, grad_kv, grad_query, weight, x_block, cosine, sine)
        smalls = (grad_bias, grad_gain_a, grad_gain_b)
        factors = (normed, grad_qkv, grad_att, attended)
        if earlier is None:
            parts = smalls, weight_grad(*factors)
        else:
            parts = apart(y_then_z, factors, smalls + small_two)
            part = after(part, parts)
        pieces = exchange(part, ("x", "c"))
        grad_in, low = layer_start(pieces, xin, gain_a, grad_mixed)
        return grad_in, low, grad_ffn, parts

    grad_two, low, ffn_two, attn_two = backward(
        cot, cot_low, gate_up2, second2, own2, other2, mixed2, gain_b2, out_one, x_block2, gain_a2, normed2, query2,
        attended2, kv_mine2, kv_other2, lse2, all_second, all_second, 512, before=out_pieces
    )
    out_two = after_feed(out_pieces, mixed2)
    grad_low = exchange(low, ("z", "x")).reshape(256, WIDTH)
    small_two, attn_two = attn_two
    grad_low = after(grad_low, attn_two)
    attn_two = after(attn_two, (ffn_two, grad_low))
    attn_two = lax.psum_scatter(attn_two.reshape(16 * 96, 896), "z", scatter_dimension=0, tiled=True)
    grad_one, _, ffn_one, parts = backward(
        grad_two, grad_low, gate_up1, second1, own1, other1, mixed1, gain_b1, xin, x_block1, gain_a1, normed1, query1,
        attended1, kv_mine1, kv_other1, lse1, qkv_first, out_first, 0, earlier=attn_two
    )
    ffn_payload = jnp.concatenate([ffn_one, ffn_two], axis=0).reshape(8, 96, FW)
    qkv_parts = sent(parts[0], "z")
    ffn_sum = exchange(after(ffn_payload, qkv_parts), ("s", "z"))
    halfway = summed(qkv_parts)
    out_parts = sent(after(parts[1], ffn_payload), "y")
    qkv_one = scatter_blocks(halfway, "y", ffn_sum)
    out_one_grad = scatter_blocks(summed(out_parts), "z", ffn_sum)
    attn_one = jnp.concatenate([qkv_one, jnp.pad(out_one_grad, ((0, 16), (0, 0)))], axis=1)
    attn_two = lax.psum_scatter(after(attn_two, (ffn_one, grad_one, halfway)), "y", scatter_dimension=0, tiled=True)

    grad_gate, grad_up, grad_down = unpack(ffn_sum)
    given = swap(jnp.concatenate([pick(attn_two, attn_one[:96]), attn_one[96:]], axis=0), "s").astype(F32)
    main = pick(attn_one[:96], attn_two).astype(F32) + given[:96]
    row = pick(attn_one[96], attn_one[98]).astype(F32) + pick(given[96], given[98])
    gains = pick(attn_one[97], attn_one[99]).astype(F32) + pick(given[97], given[99])
    gains = jnp.concatenate([gains[:96].reshape(4, 24), gains[128:224].reshape(4, 24)], axis=1)
    payload = jnp.concatenate(
        [
            main[:, QCOLS:512].reshape(4, 24, HEAD),
            jnp.pad(gains, ((0, 0), (0, HEAD - 48)))[:, None],
            jnp.broadcast_to(row[None, None, QCOLS:512], (4, 1, HEAD)),
            jnp.zeros((4, 6, HEAD), F32),
        ],
        axis=1,
    )
    arrived = [lax.dynamic_index_in_dim(payload, member, 0, keepdims=False)]
    for step in (1, 2, 3):
        given = lax.dynamic_index_in_dim(payload, member ^ step, 0, keepdims=False)
        arrived.append(lax.ppermute(given, ("x", "c"), [(m, m ^ step) for m in range(4)]))
    arrived = jnp.stack(arrived)
    payload = jnp.stack([lax.dynamic_index_in_dim(arrived, member ^ b, 0, keepdims=False) for b in BLOCK_ORDER])
    grad_keyval = payload[:, :24].transpose(1, 0, 2).reshape(24, 512)
    gains = jnp.sum(payload[:, 24], axis=0)
    kv_bias_row = lax.dynamic_index_in_dim(payload[:, 25], lax.axis_index("y"), 0, keepdims=False)
    grad_b_keyval = lax.dynamic_slice_in_dim(kv_bias_row, (lax.axis_index("z") * 4 + member) * 8, 8, 0)

    firsts, seconds = jnp.stack([out_one, grad_one]), jnp.stack([out_two, grad_two])
    given = swap(after(pick(seconds, firsts), ffn_sum), "s")
    rows = jnp.stack([pick(firsts, given), pick(given, seconds)], axis=1)[:, None]
    section_out, input_grad = rows[0], rows[1]

    return (
        section_out,
        input_grad,
        gains[None, :24],
        main[None, :, :QCOLS],
        row[None, :QCOLS],
        grad_keyval[None],
        grad_b_keyval[None],
        main[:, 512:].T[None],
        gains[None, 24:48],
        grad_gate[None],
        grad_up[None],
        grad_down[None],
    )


def solution(mesh):
    fine = Mesh(np.asarray(mesh.devices).reshape(2, 4, 4, 2, 2), AXES)
    block, member = ("y", "z"), ("x", "c")
    every = block + member
    tokens = P(None, every, None)
    split = P("s", every)
    columns = P("s", block, member)
    rows = P("s", member, block)
    keyval = P("s", every, None)
    outs = P("s", None, every, None)
    return jax.shard_map(
        local,
        mesh=fine,
        in_specs=(
            tokens, tokens, P(), split, columns, P("s", member), keyval, split, rows, split, columns, columns, rows,
        ),
        out_specs=(
            outs, outs, split, columns, P("s", member), keyval, split, rows, split, columns, columns, rows,
        ),
        check_vma=False,
    )
```

```python
import functools

import jax
import jax.numpy as jnp
import numpy as np
from jax import lax
from jax.experimental import pallas as pl
from jax.experimental.pallas import tpu as pltpu
from jax.sharding import Mesh
from jax.sharding import PartitionSpec as P

HEAD = 128
EPS = 1e-06
NEG = -1e30
THETA = 1000000.0
WIDTH = 1536
QCOLS = 384
SEQ = 2048
CHUNK = 512
MAIN = 512
PART = 64
TAIL = 4 * MAIN
GU = 2 * MAIN + 2 * PART
DOWN = MAIN + 2 * PART
FW = GU + DOWN
SCALE = HEAD**-0.5
AXES = ("s", "y", "z", "x", "c")
BLOCK_ORDER = (0, 2, 1, 3)
BF = jnp.bfloat16
F32 = jnp.float32
VMEM = pl.BlockSpec(memory_space=pltpu.VMEM)
SMEM = pl.BlockSpec(memory_space=pltpu.SMEM)
ANY = pl.BlockSpec(memory_space=pl.ANY)


def swap(value, axis):
    return lax.ppermute(value, axis, [(0, 1), (1, 0)])


def exchange(value, axes):
    return lax.all_to_all(value, axes, split_axis=0, concat_axis=0, tiled=True)


def nn(left, right):
    return jnp.dot(left, right, preferred_element_type=F32)


def nt(left, right):
    return lax.dot_general(left, right, (((1,), (1,)), ((), ())), preferred_element_type=F32)


def tn(left, right):
    return lax.dot_general(left, right, (((0,), (0,)), ((), ())), preferred_element_type=F32)


def after(value, done):
    return lax.optimization_barrier((value, done))[0]


def inverse_rms(values):
    return lax.rsqrt(jnp.mean(values * values, axis=-1, keepdims=True) + EPS)


def call(kernel, out_shape, in_specs, args, scratch=(), flops=0, size=0, exps=0, limit=52, **more):
    return pl.pallas_call(
        kernel,
        out_shape=out_shape,
        in_specs=in_specs,
        scratch_shapes=list(scratch),
        compiler_params=pltpu.CompilerParams(vmem_limit_bytes=limit * 1024 * 1024),
        cost_estimate=pl.CostEstimate(flops=flops, bytes_accessed=size, transcendentals=exps),
        **more,
    )(*args)


def arr(shape, dtype=BF):
    return jax.ShapeDtypeStruct(shape, dtype)


def turned(values, cosine, sine):
    return values * cosine + pltpu.roll(values, HEAD // 2, 1) * sine


def fetch(weight, first, into, sem):
    copy = pltpu.make_async_copy(weight.at[:, pl.ds(first, into.shape[1])], into, sem)
    copy.start()
    return copy


def fetched(columns):
    return [pltpu.VMEM((WIDTH, columns), BF), pltpu.SemaphoreType.DMA]


def qkv_kernel(flag, xin, gain, weight, bias, cosine, sine, normed, query, kv, whole, sem):
    copy = fetch(weight, 0, whole, sem)
    cos, sin = cosine[...], sine[...]
    rows = xin[...].astype(F32)
    low = (rows * inverse_rms(rows) * gain[...]).astype(BF)
    normed[...] = low
    copy.wait()
    out = nn(low, whole[...]) + bias[...]
    for h in range(3):
        query[h] = turned(out[:, h * HEAD : (h + 1) * HEAD], cos, sin).astype(BF)
    last = out[:, QCOLS:]
    last = jnp.where(flag[0] == 1, turned(last, cos, sin), last).astype(BF)
    for b in range(16):
        kv[b] = last


def qkv_columns(flag, xin, gain, weight, bias, cosine, sine):
    return call(
        qkv_kernel,
        (arr((HEAD, WIDTH)), arr((3, HEAD, HEAD)), arr((16, HEAD, HEAD))),
        [SMEM, VMEM, VMEM, ANY, VMEM, VMEM, VMEM],
        (flag, xin, gain, weight, bias, cosine, sine),
        fetched(512),
        flops=2 * 128 * 1536 * 512,
        size=3_000_000,
    )


def key_scores(query_all, keys, key_seg, query_seg, first_key, first_query):
    scores = nt(keys, query_all) * SCALE
    key_pos = first_key + lax.broadcasted_iota(jnp.int32, (CHUNK, HEAD), 0)
    query_pos = first_query + lax.broadcasted_iota(jnp.int32, (CHUNK, HEAD), 1)
    allowed = (key_seg == query_seg) & (key_pos <= query_pos)
    return [jnp.where(allowed, scores[:, h * HEAD : (h + 1) * HEAD], NEG) for h in range(3)]


def attend_kernel(
    first, flag, query, kv_mine, kv_other, seg_col, seg_row, weight, attended, wide, lse, part, top, total, acc, out_t, sem
):
    copy = fetch(weight, first, out_t, sem)
    query_all = query[...].reshape(3 * HEAD, HEAD)
    is_key = flag[0] == 1
    first_query = flag[1] * HEAD
    top[...] = jnp.full(top.shape, -3e38, F32)
    total[...] = jnp.zeros(total.shape, F32)
    acc[...] = jnp.zeros(acc.shape, F32)

    @pl.loop(0, SEQ // CHUNK)
    def _(step):
        at = pl.ds(pl.multiple_of(step * CHUNK, CHUNK), CHUNK)
        mine, other = kv_mine[at, :], kv_other[at, :]
        keys = jnp.where(is_key, mine, other)
        values = jnp.where(is_key, other, mine)
        scores = key_scores(query_all, keys, seg_col[at, :], seg_row[...], step * CHUNK, first_query)
        for h in range(3):
            columns = pl.ds(h * HEAD, HEAD)
            old = top[:, columns]
            new = jnp.maximum(old, jnp.max(scores[h], axis=0, keepdims=True))
            shrink = jnp.exp(old - new)
            raised = jnp.exp(scores[h] - new)
            top[:, columns] = new
            total[:, columns] = total[:, columns] * shrink + jnp.sum(raised, axis=0, keepdims=True)
            acc[:, columns] = acc[:, columns] * shrink + tn(values, raised.astype(BF))

    lse[...] = top[...] + jnp.log(total[...])
    done = acc[...] / total[...]
    wide[...] = done
    for h in range(3):
        attended[:, pl.ds(h * HEAD, HEAD)] = done[:, h * HEAD : (h + 1) * HEAD].T.astype(BF)
    copy.wait()
    out = nt(attended[...], out_t[...]).astype(BF)
    for t in range(4):
        part[t] = out[t * 32 : (t + 1) * 32]


def attend(flag, query, kv_mine, kv_other, seg_col, seg_row, weight, first):
    return call(
        functools.partial(attend_kernel, first),
        (arr((HEAD, QCOLS)), arr((HEAD, QCOLS), F32), arr((1, QCOLS), F32), arr((4, 32, WIDTH))),
        [SMEM] + [VMEM] * 5 + [ANY],
        (flag, query, kv_mine, kv_other, seg_col, seg_row, weight),
        [
            pltpu.VMEM((1, QCOLS), F32),
            pltpu.VMEM((1, QCOLS), F32),
            pltpu.VMEM((HEAD, QCOLS), F32),
            *fetched(QCOLS),
        ],
        flops=4 * 384 * 2048 * 128 + 2 * 128 * 384 * 1536,
        size=3_000_000,
        exps=384 * 2048,
    )


def attend_back_kernel(
    first, flag, query, kv_mine, kv_other, seg_col, seg_row, lse, wide, grad_att, cosine, sine, weight,
    grad_query, kept, sent, low, acc, out_t, sem
):
    copy = fetch(weight, first, out_t, sem)
    query_all = query[...].reshape(3 * HEAD, HEAD)
    is_key = flag[0] == 1
    first_query = flag[1] * HEAD
    sums = []
    copy.wait()
    grad_attended = nn(grad_att[...], out_t[...]).astype(BF)
    for h in range(3):
        grad_head = grad_attended[:, h * HEAD : (h + 1) * HEAD]
        low[pl.ds(h * HEAD, HEAD), :] = grad_head
        with_output = grad_head.astype(F32).T * wide[:, pl.ds(h * HEAD, HEAD)]
        sums.append(jnp.sum(with_output, axis=0, keepdims=True))
    grad_rows = low[...]
    lse_row = lse[...]

    def chunk(step):
        at = pl.ds(pl.multiple_of(step * CHUNK, CHUNK), CHUNK)
        mine, other = kv_mine[at, :], kv_other[at, :]
        keys = jnp.where(is_key, mine, other)
        values = jnp.where(is_key, other, mine)
        scores = key_scores(query_all, keys, seg_col[at, :], seg_row[...], step * CHUNK, first_query)
        probs = [jnp.exp(scores[h] - lse_row[:, h * HEAD : (h + 1) * HEAD]) for h in range(3)]
        grad_probs = nt(values, grad_rows)
        return at, keys, probs, grad_probs

    acc[...] = jnp.zeros(acc.shape, F32)

    @pl.loop(0, SEQ // CHUNK)
    def _(step):
        at, keys, probs, grad_probs = chunk(step)
        low_probs = jnp.concatenate([p.astype(BF) for p in probs], axis=1)
        low_scores = jnp.concatenate(
            [
                (probs[h] * (grad_probs[:, h * HEAD : (h + 1) * HEAD] - sums[h])).astype(BF)
                for h in range(3)
            ],
            axis=1,
        )
        grad_value = nn(low_probs, grad_rows)
        grad_key = nn(low_scores, query_all) * SCALE
        acc[...] += tn(keys, low_scores)
        kept[at, :] = jnp.where(is_key, grad_key, grad_value)
        sent[at, :] = jnp.where(is_key, grad_value, grad_key).astype(BF)

    cos, sin = cosine[...], sine[...]
    for h in range(3):
        rows = acc[:, pl.ds(h * HEAD, HEAD)].T * SCALE
        grad_query[:, pl.ds(h * HEAD, HEAD)] = turned(rows, cos, -sin).astype(BF)


def attend_back(flag, query, kv_mine, kv_other, seg_col, seg_row, lse, wide, grad_att, cosine, sine, weight, first):
    return call(
        functools.partial(attend_back_kernel, first),
        (arr((HEAD, QCOLS)), arr((SEQ, HEAD), F32), arr((SEQ, HEAD))),
        [SMEM] + [VMEM] * 10 + [ANY],
        (flag, query, kv_mine, kv_other, seg_col, seg_row, lse, wide, grad_att, cosine, sine, weight),
        [pltpu.VMEM((3 * HEAD, HEAD), BF), pltpu.VMEM((HEAD, QCOLS), F32), *fetched(QCOLS)],
        flops=10 * 384 * 2048 * 128 + 2 * 128 * 384 * 1536,
        size=5_000_000,
        exps=2 * 384 * 2048,
    )


def qkv_back_kernel(
    flag, pieces, grad_query, weight, xin, cosine, sine, grad_qkv, grad_bias, grad_gain, part, whole, sem
):
    copy = fetch(weight, 0, whole, sem)
    total = jnp.sum(pieces[...].astype(F32), axis=0)
    total = jnp.where(flag[0] == 1, turned(total, cosine[...], -sine[...]), total).astype(BF)
    grad_qkv[:, pl.ds(0, QCOLS)] = grad_query[...]
    grad_qkv[:, pl.ds(QCOLS, HEAD)] = total
    grads = grad_qkv[...]
    grad_bias[...] = jnp.sum(grads.astype(F32), axis=0, keepdims=True)
    copy.wait()
    out = nt(grads, whole[...])
    rows = xin[...].astype(F32)
    grad_gain[...] = jnp.sum(out * rows * inverse_rms(rows), axis=0, keepdims=True)
    low = out.astype(BF)
    for t in range(4):
        part[t] = low[t * 32 : (t + 1) * 32]


def qkv_back(flag, pieces, grad_query, weight, xin, cosine, sine):
    return call(
        qkv_back_kernel,
        (arr((HEAD, 512)), arr((1, 512), F32), arr((1, WIDTH), F32), arr((4, 32, WIDTH))),
        [SMEM, VMEM, VMEM, ANY, VMEM, VMEM, VMEM],
        (flag, pieces, grad_query, weight, xin, cosine, sine),
        fetched(512),
        flops=2 * 128 * 1536 * 512,
        size=3_000_000,
    )


def weight_copies(own, other, gate_up, down, sems, order):
    copies = {}
    for i, ref in enumerate((own, other)):
        for name in order:
            start, size, buffer = (0, GU, gate_up) if name == "gate_up" else (GU, DOWN, down)
            copies[i, name] = pltpu.make_async_copy(
                ref.at[:, pl.ds(start, size)], buffer.at[i], sems.at[2 * i + (name == "down")]
            )
    for i in range(2):
        for name in order:
            copies[i, name].start()
    return copies


def gate_and_up(both):
    tail = both[:, 2 * MAIN :]
    gate = jnp.concatenate([both[:, :MAIN], tail], axis=1)
    return gate, jnp.concatenate([both[:, MAIN : 2 * MAIN], pltpu.roll(tail, PART, 1)], axis=1)


def known(hidden):
    lane = lax.broadcasted_iota(jnp.int32, hidden.shape, 1)
    return jnp.where(lane < MAIN + PART, hidden, 0.0)


def feed_kernel(tokens, own, other, part, gate_up_out, gate_up, down, acc, sems):
    copies = weight_copies(own, other, gate_up, down, sems, ("gate_up", "down"))
    rows = tokens[...]
    for i in range(2):
        copies[i, "gate_up"].wait()
        both = nn(rows, gate_up[i])
        gate_up_out[i] = both.astype(BF)
        gate, up = gate_and_up(both)
        hidden = known(gate * jax.nn.sigmoid(gate) * up).astype(BF)
        copies[i, "down"].wait()
        out = nt(hidden, down[i])
        if i == 0:
            acc[...] = out
        else:
            part[...] = (acc[...] + out).astype(BF)


FEED_SCRATCH = [
    pltpu.VMEM((2, WIDTH, GU), BF),
    pltpu.VMEM((2, WIDTH, DOWN), BF),
    pltpu.VMEM((256, WIDTH), F32),
    pltpu.SemaphoreType.DMA((4,)),
]


def feed(tokens, own, other):
    return call(
        feed_kernel,
        (arr((256, WIDTH)), arr((2, 256, GU))),
        [VMEM, ANY, ANY],
        (tokens, own, other),
        FEED_SCRATCH,
        flops=2 * 256 * 1536 * 3840,
        size=15_000_000,
        exps=256 * 1280,
    )


def feed_grads(gate, up, grad_hidden, result):
    sig = jax.nn.sigmoid(gate)
    silu = gate * sig
    grad_gate = grad_hidden * up * sig * (1.0 + gate * (1.0 - sig))
    grad_up = grad_hidden * silu
    tail = grad_gate[:, MAIN:] + pltpu.roll(grad_up[:, MAIN:], PART, 1)
    hidden = known(silu * up).astype(BF)
    result[:, pl.ds(0, MAIN)] = grad_gate[:, :MAIN].astype(BF)
    result[:, pl.ds(MAIN, MAIN)] = grad_up[:, :MAIN].astype(BF)
    result[:, pl.ds(2 * MAIN, 2 * PART)] = tail.astype(BF)
    result[:, pl.ds(GU, DOWN)] = hidden
    return hidden


def feed_back_kernel(grads, own, other, gate_up_in, part, for_own, for_other, gate_up, down, acc, sems):
    copies = weight_copies(own, other, gate_up, down, sems, ("down", "gate_up"))
    rows = grads[...]
    for i, result in enumerate((for_own, for_other)):
        copies[i, "down"].wait()
        grad_hidden = nn(rows, down[i])
        gate, up = gate_and_up(gate_up_in[i].astype(F32))
        feed_grads(gate, up, grad_hidden, result)
        copies[i, "gate_up"].wait()
        out = nt(result[:, pl.ds(0, GU)], gate_up[i])
        if i == 0:
            acc[...] = out
        else:
            part[...] = (acc[...] + out).astype(BF)


def feed_back(grads, own, other, gate_up):
    return call(
        feed_back_kernel,
        (arr((256, WIDTH)), arr((256, FW)), arr((256, FW))),
        [VMEM, ANY, ANY, VMEM],
        (grads, own, other, gate_up),
        FEED_SCRATCH,
        flops=2 * 256 * 1536 * 3840,
        size=17_000_000,
        exps=256 * 1280,
    )


def feed_both_kernel(
    tokens, grads, own, other, part, for_own, for_other, gate_up, down, acc, acc_back, sems
):
    copies = weight_copies(own, other, gate_up, down, sems, ("gate_up", "down"))
    rows, grad_rows = tokens[...], grads[...]
    for i, result in enumerate((for_own, for_other)):
        copies[i, "gate_up"].wait()
        gate, up = gate_and_up(nn(rows, gate_up[i]))
        copies[i, "down"].wait()
        grad_hidden = nn(grad_rows, down[i])
        hidden = feed_grads(gate, up, grad_hidden, result)
        out, back = nt(hidden, down[i]), nt(result[:, pl.ds(0, GU)], gate_up[i])
        if i == 0:
            acc[...] = out
            acc_back[...] = back
        else:
            part[:, pl.ds(0, 32), :] = (acc_back[...] + back).astype(BF).reshape(8, 32, WIDTH)
            part[:, pl.ds(32, 32), :] = (acc[...] + out).astype(BF).reshape(8, 32, WIDTH)


def feed_both(tokens, grads, own, other):
    return call(
        feed_both_kernel,
        (arr((8, 64, WIDTH)), arr((256, FW)), arr((256, FW))),
        [VMEM, VMEM, ANY, ANY],
        (tokens, grads, own, other),
        FEED_SCRATCH[:3] + [pltpu.VMEM((256, WIDTH), F32)] + FEED_SCRATCH[3:],
        flops=4 * 256 * 1536 * 3840,
        size=17_000_000,
        exps=256 * 1280,
    )


def feed_grad_kernel(tokens, tokens_other, grads, grads_other, own, given, out):
    gate_up, hidden = pl.ds(0, GU), pl.ds(GU, DOWN)
    out[:, gate_up] = (tn(tokens[...], own[:, gate_up]) + tn(tokens_other[...], given[:, gate_up])).astype(BF)
    out[:, hidden] = (tn(grads[...], own[:, hidden]) + tn(grads_other[...], given[:, hidden])).astype(BF)


def feed_grad(tokens, tokens_other, grads, grads_other, own, given):
    rows = 256
    columns = pl.BlockSpec((256, rows), lambda i: (0, i))
    fixed = pl.BlockSpec((256, FW), lambda i: (0, 0))
    return call(
        feed_grad_kernel,
        arr((WIDTH, FW)),
        [columns] * 4 + [fixed] * 2,
        (tokens, tokens_other, grads, grads_other, own, given),
        flops=2 * 512 * 1536 * 1920,
        size=12_000_000,
        grid=(WIDTH // rows,),
        out_specs=pl.BlockSpec((rows, FW), lambda i: (i, 0)),
    )


def shifted(value, axis, steps):
    return lax.ppermute(value, axis, [(i, (i + steps) % 4) for i in range(4)])


def ring_first(piece, axis):
    return jnp.stack([piece] + [shifted(piece, axis, j) for j in (1, 2, 3)])


def ring_second(blocks, axis):
    return [blocks] + [shifted(blocks, axis, k) for k in (1, 2, 3)]


def ring_block(place, j, k):
    return lax.rem(place[0] + 4 - j, 4) * place[1] + lax.rem(place[2] + 4 - k, 4) * place[3]


def assemble_kernel(place, *refs):
    pieces, out, tail = refs[:4], refs[4], refs[5] if len(refs) > 5 else None
    for k in range(4):
        for j in range(4):
            block = ring_block(place, j, k)
            out[pl.ds(pl.multiple_of(block * 96, 32), 96), :] = pieces[k][j, pl.ds(0, 96), :]
            if tail is not None:
                tail[block] = pieces[k][j, pl.ds(96, 16), :]


def assemble(place, pieces):
    _, rows, columns = pieces[0].shape
    whole, tail = arr((WIDTH, columns)), arr((16, 16, columns))
    return call(
        assemble_kernel,
        whole if rows == 96 else (whole, tail),
        [SMEM] + [VMEM] * 4,
        (place, *pieces),
        size=4_000_000,
    )


def weight_grad_kernel(normed, grad_qkv, grad_att, attended, out, scratch):
    scratch[:, pl.ds(0, 512)] = tn(normed[...], grad_qkv[...]).astype(BF)
    scratch[:, pl.ds(512, QCOLS)] = tn(grad_att[...], attended[...]).astype(BF)
    for b in range(16):
        out[b % 4, b // 4] = scratch[pl.ds(b * 96, 96), :]


def weight_grad(*args):
    return call(
        weight_grad_kernel,
        arr((4, 4, 96, 896)),
        [VMEM] * 4,
        args,
        [pltpu.VMEM((WIDTH, 896), BF)],
        flops=2 * 128 * 1536 * 896,
        size=6_000_000,
    )


def apart_kernel(place, normed, grad_qkv, grad_att, attended, *rest):
    smalls, outs, scratch, scratch_out = rest[:-10], rest[-10:-2], rest[-2], rest[-1]
    scratch[...] = tn(normed[...], grad_qkv[...]).astype(BF)
    scratch_out[...] = tn(grad_att[...], attended[...]).astype(BF)
    row_index = lax.broadcasted_iota(jnp.int32, (16, 512), 0)
    for b in range(16):
        y, z = b // 4, b % 4
        rows = jnp.zeros((16, 512), F32)
        for layer in range(2):
            bias, *gains = (ref[...] for ref in smalls[3 * layer : 3 * layer + 3])
            moved = [(pltpu.roll(g, (WIDTH - 96 * b) % WIDTH, 1) if b else g)[:, :HEAD] for g in gains]
            gain_row = jnp.concatenate([*moved, jnp.zeros((1, 2 * HEAD), F32)], axis=1)
            for at, row in ((2 * layer, bias), (2 * layer + 1, gain_row)):
                rows = jnp.where(row_index == at, jnp.broadcast_to(row, (16, 512)), rows)
        rows = rows.astype(BF)
        for k in range(4):

            @pl.when(lax.rem(place[2] + k, 4) == z)
            def _(k=k):
                outs[k][y, pl.ds(0, 96), :] = scratch[pl.ds(b * 96, 96), :]
                outs[k][y, pl.ds(96, 16), :] = rows

            @pl.when(lax.rem(place[0] + k, 4) == y)
            def _(k=k):
                outs[4 + k][z] = scratch_out[pl.ds(b * 96, 96), :]


def apart(place, factors, smalls):
    parts = call(
        apart_kernel,
        (arr((4, 112, 512)),) * 4 + (arr((4, 96, QCOLS)),) * 4,
        [SMEM] + [VMEM] * 10,
        (place, *factors, *smalls),
        [pltpu.VMEM((WIDTH, 512), BF), pltpu.VMEM((WIDTH, QCOLS), BF)],
        flops=2 * 128 * 1536 * 896,
        size=6_000_000,
    )
    return parts[:4], parts[4:]


def sent(parts, axis):
    return [parts[0]] + [shifted(parts[k], axis, k) for k in (1, 2, 3)]


def summed(parts):
    return sum(part.astype(F32) for part in parts).astype(BF)


def scatter_blocks(blocks, axis, last):
    here = lax.axis_index(axis)
    own, *others = (lax.dynamic_index_in_dim(blocks, lax.rem(here + j, 4), 0, keepdims=False) for j in range(4))
    return summed([own] + [after(shifted(other, axis, j + 1), last) for j, other in enumerate(others)])


def after_heads_kernel(pieces, xin, gain, mixed, second):
    total = xin[...].astype(F32) + jnp.sum(pieces[...].astype(F32), axis=0)
    mixed[...] = total
    low = (total * inverse_rms(total) * gain[...]).astype(BF)
    for t in range(8):
        second[t] = low


def after_heads(pieces, xin, gain):
    return call(
        after_heads_kernel,
        (arr((32, WIDTH), F32), arr((8, 32, WIDTH))),
        [VMEM] * 3,
        (pieces, xin, gain),
        size=1_500_000,
    )


def after_feed_kernel(pieces, mixed, out):
    last = pl.ds(pieces.shape[1] - 32, 32)
    out[...] = (mixed[...] + jnp.sum(pieces[:, last, :].astype(F32), axis=0)).astype(BF)


def after_feed(pieces, mixed):
    return call(after_feed_kernel, arr((32, WIDTH)), [VMEM] * 2, (pieces, mixed), size=1_500_000)


def norm_back(grad, values, gain, grad_out):
    inverse = inverse_rms(values)
    norm = values * inverse
    scaled = grad * gain
    grad_gain = jnp.sum(grad * norm, axis=0, keepdims=True)
    return grad_out + inverse * (scaled - norm * jnp.mean(scaled * norm, axis=-1, keepdims=True)), grad_gain


def before_heads_kernel(pieces, mixed, gain, grad_out, grad_mixed, low, grad_gain):
    grad = jnp.sum(pieces[:, pl.ds(0, 32), :].astype(F32), axis=0)
    result, sums = norm_back(grad, mixed[...], gain[...], grad_out[...].astype(F32))
    grad_mixed[...] = result
    low[...] = result.astype(BF)
    grad_gain[...] = sums


def before_heads(pieces, mixed, gain, grad_out):
    return call(
        before_heads_kernel,
        (arr((32, WIDTH), F32), arr((32, WIDTH)), arr((1, WIDTH), F32)),
        [VMEM] * 4,
        (pieces, mixed, gain, grad_out),
        size=1_500_000,
    )


def layer_start_kernel(pieces, xin, gain, grad_mixed, grad_in, spread):
    grad = jnp.sum(pieces[...].astype(F32), axis=0)
    result, _ = norm_back(grad, xin[...].astype(F32), gain[...], grad_mixed[...])
    low = result.astype(BF)
    grad_in[...] = low
    for t in range(8):
        spread[t] = low


def layer_start(pieces, xin, gain, grad_mixed):
    return call(
        layer_start_kernel,
        (arr((32, WIDTH)), arr((8, 32, WIDTH))),
        [VMEM] * 4,
        (pieces, xin, gain, grad_mixed),
        size=1_500_000,
    )


def pack_kernel(gate, up, down, tails, out):
    for z in range(4):
        main = pl.ds(z * MAIN, MAIN)
        pieces = (
            (0, gate[:, main]),
            (MAIN, up[:, main]),
            (2 * MAIN, tails[z, :, pl.ds(0, 2 * PART)]),
            (GU, down[main, :].astype(F32).T.astype(BF)),
            (GU + MAIN, tails[z, :, pl.ds(2 * PART, 2 * PART)]),
        )
        for s in range(2):
            for at, piece in pieces:
                out[4 * s + z, :, pl.ds(at, piece.shape[1])] = piece


def pack(gate, up, down):
    rest = [jnp.pad(w, ((0, 0), (0, PART))).reshape(96, 4, PART) for w in (gate[:, TAIL:], up[:, TAIL:], down[TAIL:].T)]
    tails = jnp.concatenate([*rest, jnp.zeros((96, 4, PART), BF)], axis=2).transpose(1, 0, 2)
    return call(pack_kernel, arr((8, 96, FW)), [VMEM] * 4, (gate, up, down, tails), size=4_500_000)


def halves_kernel(pieces, first, second):
    first[...] = pieces[:4].reshape(384, FW)
    second[...] = pieces[4:].reshape(384, FW)


def halves(pieces):
    return call(halves_kernel, (arr((384, FW)), arr((384, FW))), [VMEM], (pieces,), size=6_000_000)


def unpack_kernel(pieces, gate, up, down):
    low = lax.broadcasted_iota(jnp.int32, (96, 2 * PART), 1) < PART
    tails = []
    for z in range(4):
        main = pl.ds(z * MAIN, MAIN)
        total = pieces[z].astype(F32) + pieces[4 + z].astype(F32)
        gate[:, main] = total[:, :MAIN]
        up[:, main] = total[:, MAIN : 2 * MAIN]
        down[main, :] = total[:, GU : GU + MAIN].T
        if z < 3:
            tails.append(total[:, 2 * MAIN : GU])
            down[pl.ds(TAIL + z * PART, PART), :] = total[:, GU + MAIN :].T[:PART]
    turned_tails = [pltpu.roll(tail, PART, 1) for tail in tails]
    gate[:, pl.ds(TAIL, 2 * PART)] = jnp.where(low, tails[0], turned_tails[1])
    gate[:, pl.ds(TAIL + 2 * PART, PART)] = tails[2][:, :PART]
    up[:, pl.ds(TAIL, 2 * PART)] = jnp.where(low, turned_tails[0], tails[1])
    up[:, pl.ds(TAIL + 2 * PART, PART)] = turned_tails[2][:, :PART]


def unpack(pieces):
    wide = TAIL + 3 * PART
    return call(
        unpack_kernel,
        (arr((96, wide), F32), arr((96, wide), F32), arr((wide, 96), F32)),
        [VMEM],
        (pieces,),
        size=7_000_000,
    )


def local(
    inputs, cotangent, segments, gain_one, w_query, b_query, w_keyval, b_keyval, w_out, gain_two, w_gate, w_up, w_down
):
    on_first = lax.axis_index("s") == 0
    core, chip = lax.axis_index("c"), lax.axis_index("x")
    block = lax.axis_index("y") * 4 + lax.axis_index("z")
    member = chip * 2 + core
    flag = jnp.stack([(core == 0).astype(jnp.int32), block.astype(jnp.int32)])

    def pick(first, second):
        return jnp.where(on_first, first, second)

    def gathered(piece, axes):
        return lax.all_gather(piece, axes, axis=0, tiled=True)

    def pair_gather(rows, axis):
        given = swap(rows, axis)
        is_low = lax.axis_index(axis) == 0
        return jnp.concatenate([jnp.where(is_low, rows, given), jnp.where(is_low, given, rows)], axis=0)

    def spread(rows, count, axes):
        return exchange(jnp.broadcast_to(rows[None], (count,) + rows.shape), axes)

    small = jnp.concatenate([gain_one[0], gain_two[0], b_keyval[0], jnp.zeros((72,), BF)])
    kv_blocks = w_keyval[0].reshape(24, 4, HEAD).transpose(1, 0, 2)
    kv_blocks = jnp.stack([kv_blocks[b] for b in BLOCK_ORDER])
    payload = jnp.concatenate(
        [kv_blocks, jnp.broadcast_to(small[None, None], (4, 1, HEAD)), jnp.zeros((4, 7, HEAD), BF)], axis=1
    )
    payload = exchange(jnp.concatenate([payload, payload], axis=0), ("s", "x", "c")).reshape(2, 4, 32, HEAD)
    bias_rows = jnp.pad(b_query, ((0, 15), (0, QCOLS)))
    own = jnp.concatenate([jnp.concatenate([w_query[0], w_out[0].T], axis=1), bias_rows], axis=0)
    other = swap(own, "s")

    def attention_rows(layer, matrices):
        return jnp.concatenate([matrices[:96, :QCOLS], payload[layer, :, :24].reshape(96, HEAD)], axis=1)

    def small_rows(layer, matrices):
        return jnp.concatenate([matrices[96:100, :QCOLS], payload[layer, :, 24]], axis=1)

    xin = pick(inputs[0], inputs[1])
    cot = pick(cotangent[0], cotangent[1])
    place_y, place_z = lax.axis_index("y").astype(jnp.int32), lax.axis_index("z").astype(jnp.int32)
    y_then_z = jnp.stack([place_y, jnp.int32(4), place_z, jnp.int32(1)])
    first, second = pick(own, other), pick(other, own)
    rows_first, out_rows = attention_rows(0, first), first[:96, QCOLS:]
    tails = [small_rows(0, first), small_rows(1, second), jnp.zeros((8, 512), BF)]
    rows_first = jnp.concatenate([rows_first, *tails], axis=0)
    rows_second = jnp.concatenate([attention_rows(1, second), second[:96, QCOLS:]], axis=1)
    ffn_packed = after(pack(w_gate[0], w_up[0], w_down[0]), (rows_first, rows_second))
    ffn_pieces = exchange(ffn_packed, ("s", "z"))
    blocks, out_blocks = ring_first(rows_first, "y"), ring_first(out_rows, "y")
    blocks, out_blocks, ffn_pieces = lax.optimization_barrier((blocks, out_blocks, ffn_pieces))
    ffn_halves = halves(ffn_pieces)
    x_block1 = pair_gather(pair_gather(after(xin, ffn_pieces), "c"), "x")
    ring = ring_second(blocks, "z")
    qkv_first, tail_first = assemble(y_then_z, ring)
    out_ring = ring_second(after(out_blocks, (ring[1], ring[3])), "z")

    seg = pick(segments[0], segments[1])
    local_pos = block * HEAD + jnp.arange(HEAD, dtype=jnp.int32)
    inverse_freq = THETA ** (-(jnp.arange(HEAD // 2, dtype=F32) * 2.0) / HEAD)
    angles = local_pos.astype(F32)[:, None] * inverse_freq[None, :]
    cosine = jnp.cos(angles)
    sine = jnp.sin(angles)
    cosine = jnp.concatenate([cosine, cosine], axis=1)
    sine = jnp.concatenate([-sine, sine], axis=1)
    seg_row = lax.dynamic_slice_in_dim(seg, block * HEAD, HEAD, 0)[None]
    seg_col = seg[:, None]

    def smalls(tail):
        bits = tail[:, :, QCOLS : QCOLS + 56].reshape(64, 56)
        gain_a = bits[:, :24].reshape(1, WIDTH).astype(F32)
        gain_b = bits[:, 24:48].reshape(1, WIDTH).astype(F32)
        kv_bias = lax.dynamic_slice_in_dim(bits[:, 48:].reshape(1, 512), (core * 2 + chip) * HEAD, HEAD, 1)
        bias = jnp.concatenate([tail[:1, 0, :QCOLS], kv_bias], axis=1).astype(F32)
        return gain_a, gain_b, bias

    gain_a1, gain_b1, bias1 = smalls(tail_first[:, :4])
    normed1, query1, kv = qkv_columns(flag, x_block1, gain_a1, qkv_first, bias1, cosine, sine)
    own1 = gathered(ffn_halves[0], "y")
    all_second = gathered(after(rows_second, kv), ("y", "z"))
    kv, out_ring = lax.optimization_barrier((kv, out_ring))
    out_first = assemble(y_then_z, out_ring)
    kv_mine1 = exchange(kv, ("y", "z")).reshape(SEQ, HEAD)
    kv_other1 = swap(kv_mine1, "c")
    attended1, wide1, lse1, part = attend(flag, query1, kv_mine1, kv_other1, seg_col, seg_row, out_first, 0)
    other1 = swap(after(own1, part), "c")
    mixed1, low = after_heads(after(exchange(part, ("x", "c")), other1), xin, gain_b1)
    second1 = exchange(low, ("z", "x")).reshape(256, WIDTH)
    own2 = gathered(after(ffn_halves[1], second1), "y")
    part, gate_up1 = feed(second1, own1, other1)
    pieces = exchange(part.reshape(8, 32, WIDTH), ("z", "x"))
    out_one = after_feed(pieces, mixed1)

    x_block2 = gathered(out_one, ("x", "c"))
    gain_a2, gain_b2, bias2 = smalls(tail_first[:, 4:8])
    normed2, query2, kv = qkv_columns(flag, x_block2, gain_a2, all_second, bias2, cosine, sine)
    kv_mine2 = exchange(kv, ("y", "z")).reshape(SEQ, HEAD)
    kv_other2 = swap(kv_mine2, "c")
    attended2, wide2, lse2, part = attend(flag, query2, kv_mine2, kv_other2, seg_col, seg_row, all_second, 512)
    mixed2, low = after_heads(exchange(part, ("x", "c")), out_one, gain_b2)
    second2 = exchange(low, ("z", "x")).reshape(256, WIDTH)
    other2 = swap(after(own2, second2), "c")
    cot_low = spread(after(cot, (second2, own2)), 8, ("z", "x")).reshape(256, WIDTH)
    second2 = after(second2, cot_low)
    fed2 = feed_both(second2, cot_low, own2, other2)

    def backward(grad_out, grad_low, fed, second, mixed, gain_b, xin, x_block, gain_a, normed, query, attended, wide,
                 kv_mine, kv_other, lse, weight, out_t, first, earlier=None):
        part, for_own, for_other = fed
        pieces = fed_pieces = exchange(part.reshape(8, -1, WIDTH), ("z", "x"))
        given = swap(for_other, "c")
        second_other, grad_other = swap(second, "c"), swap(grad_low, "c")
        grad_ffn = feed_grad(second, second_other, grad_low, grad_other, for_own, given)
        pieces, grad_ffn = lax.optimization_barrier((pieces, grad_ffn))
        grad_mixed, low, grad_gain_b = before_heads(pieces, mixed, gain_b, grad_out)
        grad_att = gathered(low, ("x", "c"))
        if earlier is not None:
            grad_ffn = after(grad_ffn, (earlier, grad_att))
        grad_ffn = lax.psum_scatter(grad_ffn, "y", scatter_dimension=0, tiled=True)
        grad_query, kept_half, sent_half = attend_back(
            flag, query, kv_mine, kv_other, seg_col, seg_row, lse, wide, grad_att, cosine, sine, out_t, first
        )
        grad_kv = (kept_half + swap(sent_half, "c").astype(F32)).astype(BF)
        grad_kv = exchange(grad_kv.reshape(16, HEAD, HEAD), ("y", "z"))
        grad_qkv, grad_bias, grad_gain_a, part = qkv_back(flag, grad_kv, grad_query, weight, x_block, cosine, sine)
        smalls = (grad_bias, grad_gain_a, grad_gain_b)
        factors = (normed, grad_qkv, grad_att, attended)
        if earlier is None:
            parts = smalls, weight_grad(*factors)
        else:
            parts = apart(y_then_z, factors, smalls + small_two)
            part = after(part, parts)
        pieces = exchange(part, ("x", "c"))
        grad_in, low = layer_start(pieces, xin, gain_a, grad_mixed)
        return grad_in, low, grad_ffn, parts, fed_pieces

    grad_two, low, ffn_two, attn_two, out_pieces = backward(
        cot, cot_low, fed2, second2, mixed2, gain_b2, out_one, x_block2, gain_a2, normed2, query2, attended2, wide2,
        kv_mine2, kv_other2, lse2, all_second, all_second, 512
    )
    out_two = after_feed(out_pieces, mixed2)
    grad_low = exchange(low, ("z", "x")).reshape(256, WIDTH)
    small_two, attn_two = attn_two
    grad_low = after(grad_low, attn_two)
    attn_two = after(attn_two, (ffn_two, grad_low))
    attn_two = lax.psum_scatter(attn_two.reshape(16 * 96, 896), "z", scatter_dimension=0, tiled=True)
    fed1 = feed_back(grad_low, own1, other1, gate_up1)
    grad_one, _, ffn_one, parts, _ = backward(
        grad_two, grad_low, fed1, second1, mixed1, gain_b1, xin, x_block1, gain_a1, normed1, query1, attended1, wide1,
        kv_mine1, kv_other1, lse1, qkv_first, out_first, 0, earlier=attn_two
    )
    ffn_payload = jnp.concatenate([ffn_one, ffn_two], axis=0).reshape(8, 96, FW)
    qkv_parts = sent(parts[0], "z")
    ffn_sum = exchange(after(ffn_payload, qkv_parts), ("s", "z"))
    halfway = summed(qkv_parts)
    out_parts = sent(after(parts[1], ffn_payload), "y")
    qkv_one = scatter_blocks(halfway, "y", ffn_sum)
    out_one_grad = scatter_blocks(summed(out_parts), "z", ffn_sum)
    attn_one = jnp.concatenate([qkv_one, jnp.pad(out_one_grad, ((0, 16), (0, 0)))], axis=1)
    attn_two = lax.psum_scatter(after(attn_two, (ffn_one, grad_one, halfway)), "y", scatter_dimension=0, tiled=True)

    grad_gate, grad_up, grad_down = unpack(ffn_sum)
    given = swap(jnp.concatenate([pick(attn_two, attn_one[:96]), attn_one[96:]], axis=0), "s").astype(F32)
    main = pick(attn_one[:96], attn_two).astype(F32) + given[:96]
    row = pick(attn_one[96], attn_one[98]).astype(F32) + pick(given[96], given[98])
    gains = pick(attn_one[97], attn_one[99]).astype(F32) + pick(given[97], given[99])
    gains = jnp.concatenate([gains[:96].reshape(4, 24), gains[128:224].reshape(4, 24)], axis=1)
    payload = jnp.concatenate(
        [
            main[:, QCOLS:512].reshape(4, 24, HEAD),
            jnp.pad(gains, ((0, 0), (0, HEAD - 48)))[:, None],
            jnp.broadcast_to(row[None, None, QCOLS:512], (4, 1, HEAD)),
            jnp.zeros((4, 6, HEAD), F32),
        ],
        axis=1,
    )
    arrived = [lax.dynamic_index_in_dim(payload, member, 0, keepdims=False)]
    for step in (1, 2, 3):
        given = lax.dynamic_index_in_dim(payload, member ^ step, 0, keepdims=False)
        arrived.append(lax.ppermute(given, ("x", "c"), [(m, m ^ step) for m in range(4)]))
    arrived = jnp.stack(arrived)
    payload = jnp.stack([lax.dynamic_index_in_dim(arrived, member ^ b, 0, keepdims=False) for b in BLOCK_ORDER])
    grad_keyval = payload[:, :24].transpose(1, 0, 2).reshape(24, 512)
    gains = jnp.sum(payload[:, 24], axis=0)
    kv_bias_row = lax.dynamic_index_in_dim(payload[:, 25], lax.axis_index("y"), 0, keepdims=False)
    grad_b_keyval = lax.dynamic_slice_in_dim(kv_bias_row, (lax.axis_index("z") * 4 + member) * 8, 8, 0)

    firsts, seconds = jnp.stack([out_one, grad_one]), jnp.stack([out_two, grad_two])
    given = swap(after(pick(seconds, firsts), ffn_sum), "s")
    rows = jnp.stack([pick(firsts, given), pick(given, seconds)], axis=1)[:, None]
    section_out, input_grad = rows[0], rows[1]

    return (
        section_out,
        input_grad,
        gains[None, :24],
        main[None, :, :QCOLS],
        row[None, :QCOLS],
        grad_keyval[None],
        grad_b_keyval[None],
        main[:, 512:].T[None],
        gains[None, 24:48],
        grad_gate[None],
        grad_up[None],
        grad_down[None],
    )


def solution(mesh):
    fine = Mesh(np.asarray(mesh.devices).reshape(2, 4, 4, 2, 2), AXES)
    block, member = ("y", "z"), ("x", "c")
    every = block + member
    tokens = P(None, every, None)
    split = P("s", every)
    columns = P("s", block, member)
    rows = P("s", member, block)
    keyval = P("s", every, None)
    outs = P("s", None, every, None)
    return jax.shard_map(
        local,
        mesh=fine,
        in_specs=(
            tokens, tokens, P(), split, columns, P("s", member), keyval, split, rows, split, columns, columns, rows,
        ),
        out_specs=(
            outs, outs, split, columns, P("s", member), keyval, split, rows, split, columns, columns, rows,
        ),
        check_vma=False,
    )
```

```python
import functools

import jax
import jax.numpy as jnp
import numpy as np
from jax import lax
from jax.experimental import pallas as pl
from jax.experimental.pallas import tpu as pltpu
from jax.sharding import Mesh
from jax.sharding import PartitionSpec as P

HEAD = 128
EPS = 1e-06
NEG = -1e30
THETA = 1000000.0
WIDTH = 1536
QCOLS = 384
SEQ = 2048
CHUNK = 512
MAIN = 512
PART = 64
TAIL = 4 * MAIN
GU = 2 * MAIN + 2 * PART
DOWN = MAIN + 2 * PART
FW = GU + DOWN
SCALE = HEAD**-0.5
AXES = ("s", "y", "z", "x", "c")
BLOCK_ORDER = (0, 2, 1, 3)
BF = jnp.bfloat16
F32 = jnp.float32
VMEM = pl.BlockSpec(memory_space=pltpu.VMEM)
SMEM = pl.BlockSpec(memory_space=pltpu.SMEM)
ANY = pl.BlockSpec(memory_space=pl.ANY)


def swap(value, axis):
    return lax.ppermute(value, axis, [(0, 1), (1, 0)])


def exchange(value, axes):
    return lax.all_to_all(value, axes, split_axis=0, concat_axis=0, tiled=True)


def nn(left, right):
    return jnp.dot(left, right, preferred_element_type=F32)


def nt(left, right):
    return lax.dot_general(left, right, (((1,), (1,)), ((), ())), preferred_element_type=F32)


def tn(left, right):
    return lax.dot_general(left, right, (((0,), (0,)), ((), ())), preferred_element_type=F32)


def after(value, done):
    return lax.optimization_barrier((value, done))[0]


def inverse_rms(values):
    return lax.rsqrt(jnp.mean(values * values, axis=-1, keepdims=True) + EPS)


def call(kernel, out_shape, in_specs, args, scratch=(), flops=0, size=0, exps=0, limit=52, **more):
    return pl.pallas_call(
        kernel,
        out_shape=out_shape,
        in_specs=in_specs,
        scratch_shapes=list(scratch),
        compiler_params=pltpu.CompilerParams(vmem_limit_bytes=limit * 1024 * 1024),
        cost_estimate=pl.CostEstimate(flops=flops, bytes_accessed=size, transcendentals=exps),
        **more,
    )(*args)


def arr(shape, dtype=BF):
    return jax.ShapeDtypeStruct(shape, dtype)


def turned(values, cosine, sine):
    return values * cosine + pltpu.roll(values, HEAD // 2, 1) * sine


def fetch(weight, first, into, sem):
    copy = pltpu.make_async_copy(weight.at[:, pl.ds(first, into.shape[1])], into, sem)
    copy.start()
    return copy


def fetched(columns):
    return [pltpu.VMEM((WIDTH, columns), BF), pltpu.SemaphoreType.DMA]


def qkv_kernel(flag, xin, gain, weight, bias, cosine, sine, normed, query, kv, whole, sem):
    copy = fetch(weight, 0, whole, sem)
    cos, sin = cosine[...], sine[...]
    rows = xin[...].astype(F32)
    low = (rows * inverse_rms(rows) * gain[...]).astype(BF)
    normed[...] = low
    copy.wait()
    out = nn(low, whole[...]) + bias[...]
    for h in range(3):
        query[h] = turned(out[:, h * HEAD : (h + 1) * HEAD], cos, sin).astype(BF)
    last = out[:, QCOLS:]
    last = jnp.where(flag[0] == 1, turned(last, cos, sin), last).astype(BF)
    for b in range(16):
        kv[b] = last


def qkv_columns(flag, xin, gain, weight, bias, cosine, sine):
    return call(
        qkv_kernel,
        (arr((HEAD, WIDTH)), arr((3, HEAD, HEAD)), arr((16, HEAD, HEAD))),
        [SMEM, VMEM, VMEM, ANY, VMEM, VMEM, VMEM],
        (flag, xin, gain, weight, bias, cosine, sine),
        fetched(512),
        flops=2 * 128 * 1536 * 512,
        size=3_000_000,
    )


def key_scores(query_all, keys, key_seg, query_seg, first_key, first_query):
    scores = nt(keys, query_all) * SCALE
    key_pos = first_key + lax.broadcasted_iota(jnp.int32, (CHUNK, HEAD), 0)
    query_pos = first_query + lax.broadcasted_iota(jnp.int32, (CHUNK, HEAD), 1)
    allowed = (key_seg == query_seg) & (key_pos <= query_pos)
    return [jnp.where(allowed, scores[:, h * HEAD : (h + 1) * HEAD], NEG) for h in range(3)]


def attend_kernel(
    first, flag, query, kv_mine, kv_other, seg_col, seg_row, weight, attended, wide, lse, part, top, total, acc, out_t, sem
):
    copy = fetch(weight, first, out_t, sem)
    query_all = query[...].reshape(3 * HEAD, HEAD)
    is_key = flag[0] == 1
    first_query = flag[1] * HEAD
    top[...] = jnp.full(top.shape, -3e38, F32)
    total[...] = jnp.zeros(total.shape, F32)
    acc[...] = jnp.zeros(acc.shape, F32)

    @pl.loop(0, SEQ // CHUNK)
    def _(step):
        at = pl.ds(pl.multiple_of(step * CHUNK, CHUNK), CHUNK)
        mine, other = kv_mine[at, :], kv_other[at, :]
        keys = jnp.where(is_key, mine, other)
        values = jnp.where(is_key, other, mine)
        scores = key_scores(query_all, keys, seg_col[at, :], seg_row[...], step * CHUNK, first_query)
        for h in range(3):
            columns = pl.ds(h * HEAD, HEAD)
            old = top[:, columns]
            new = jnp.maximum(old, jnp.max(scores[h], axis=0, keepdims=True))
            shrink = jnp.exp(old - new)
            raised = jnp.exp(scores[h] - new)
            top[:, columns] = new
            total[:, columns] = total[:, columns] * shrink + jnp.sum(raised, axis=0, keepdims=True)
            acc[:, columns] = acc[:, columns] * shrink + tn(values, raised.astype(BF))

    lse[...] = top[...] + jnp.log(total[...])
    done = acc[...] / total[...]
    wide[...] = done
    for h in range(3):
        attended[:, pl.ds(h * HEAD, HEAD)] = done[:, h * HEAD : (h + 1) * HEAD].T.astype(BF)
    copy.wait()
    out = nt(attended[...], out_t[...]).astype(BF)
    for t in range(4):
        part[t] = out[t * 32 : (t + 1) * 32]


def attend(flag, query, kv_mine, kv_other, seg_col, seg_row, weight, first):
    return call(
        functools.partial(attend_kernel, first),
        (arr((HEAD, QCOLS)), arr((HEAD, QCOLS), F32), arr((1, QCOLS), F32), arr((4, 32, WIDTH))),
        [SMEM] + [VMEM] * 5 + [ANY],
        (flag, query, kv_mine, kv_other, seg_col, seg_row, weight),
        [
            pltpu.VMEM((1, QCOLS), F32),
            pltpu.VMEM((1, QCOLS), F32),
            pltpu.VMEM((HEAD, QCOLS), F32),
            *fetched(QCOLS),
        ],
        flops=4 * 384 * 2048 * 128 + 2 * 128 * 384 * 1536,
        size=3_000_000,
        exps=384 * 2048,
    )


def attend_back_kernel(
    first, flag, query, kv_mine, kv_other, seg_col, seg_row, lse, wide, grad_att, cosine, sine, weight,
    grad_query, kept, sent, low, acc, out_t, sem
):
    copy = fetch(weight, first, out_t, sem)
    query_all = query[...].reshape(3 * HEAD, HEAD)
    is_key = flag[0] == 1
    first_query = flag[1] * HEAD
    sums = []
    copy.wait()
    grad_attended = nn(grad_att[...], out_t[...]).astype(BF)
    for h in range(3):
        grad_head = grad_attended[:, h * HEAD : (h + 1) * HEAD]
        low[pl.ds(h * HEAD, HEAD), :] = grad_head
        with_output = grad_head.astype(F32).T * wide[:, pl.ds(h * HEAD, HEAD)]
        sums.append(jnp.sum(with_output, axis=0, keepdims=True))
    grad_rows = low[...]
    lse_row = lse[...]

    def chunk(step):
        at = pl.ds(pl.multiple_of(step * CHUNK, CHUNK), CHUNK)
        mine, other = kv_mine[at, :], kv_other[at, :]
        keys = jnp.where(is_key, mine, other)
        values = jnp.where(is_key, other, mine)
        scores = key_scores(query_all, keys, seg_col[at, :], seg_row[...], step * CHUNK, first_query)
        probs = [jnp.exp(scores[h] - lse_row[:, h * HEAD : (h + 1) * HEAD]) for h in range(3)]
        grad_probs = nt(values, grad_rows)
        return at, keys, probs, grad_probs

    acc[...] = jnp.zeros(acc.shape, F32)

    @pl.loop(0, SEQ // CHUNK)
    def _(step):
        at, keys, probs, grad_probs = chunk(step)
        low_probs = jnp.concatenate([p.astype(BF) for p in probs], axis=1)
        low_scores = jnp.concatenate(
            [
                (probs[h] * (grad_probs[:, h * HEAD : (h + 1) * HEAD] - sums[h])).astype(BF)
                for h in range(3)
            ],
            axis=1,
        )
        grad_value = nn(low_probs, grad_rows)
        grad_key = nn(low_scores, query_all) * SCALE
        acc[...] += tn(keys, low_scores)
        kept[at, :] = jnp.where(is_key, grad_key, grad_value)
        sent[at, :] = jnp.where(is_key, grad_value, grad_key).astype(BF)

    cos, sin = cosine[...], sine[...]
    for h in range(3):
        rows = acc[:, pl.ds(h * HEAD, HEAD)].T * SCALE
        grad_query[:, pl.ds(h * HEAD, HEAD)] = turned(rows, cos, -sin).astype(BF)


def attend_back(flag, query, kv_mine, kv_other, seg_col, seg_row, lse, wide, grad_att, cosine, sine, weight, first):
    return call(
        functools.partial(attend_back_kernel, first),
        (arr((HEAD, QCOLS)), arr((SEQ, HEAD), F32), arr((SEQ, HEAD))),
        [SMEM] + [VMEM] * 10 + [ANY],
        (flag, query, kv_mine, kv_other, seg_col, seg_row, lse, wide, grad_att, cosine, sine, weight),
        [pltpu.VMEM((3 * HEAD, HEAD), BF), pltpu.VMEM((HEAD, QCOLS), F32), *fetched(QCOLS)],
        flops=10 * 384 * 2048 * 128 + 2 * 128 * 384 * 1536,
        size=5_000_000,
        exps=2 * 384 * 2048,
    )


def qkv_back_kernel(
    flag, pieces, grad_query, weight, xin, cosine, sine, grad_qkv, grad_bias, grad_gain, part, whole, sem
):
    copy = fetch(weight, 0, whole, sem)
    total = jnp.sum(pieces[...].astype(F32), axis=0)
    total = jnp.where(flag[0] == 1, turned(total, cosine[...], -sine[...]), total).astype(BF)
    grad_qkv[:, pl.ds(0, QCOLS)] = grad_query[...]
    grad_qkv[:, pl.ds(QCOLS, HEAD)] = total
    grads = grad_qkv[...]
    grad_bias[...] = jnp.sum(grads.astype(F32), axis=0, keepdims=True)
    copy.wait()
    out = nt(grads, whole[...])
    rows = xin[...].astype(F32)
    grad_gain[...] = jnp.sum(out * rows * inverse_rms(rows), axis=0, keepdims=True)
    low = out.astype(BF)
    for t in range(4):
        part[t] = low[t * 32 : (t + 1) * 32]


def qkv_back(flag, pieces, grad_query, weight, xin, cosine, sine):
    return call(
        qkv_back_kernel,
        (arr((HEAD, 512)), arr((1, 512), F32), arr((1, WIDTH), F32), arr((4, 32, WIDTH))),
        [SMEM, VMEM, VMEM, ANY, VMEM, VMEM, VMEM],
        (flag, pieces, grad_query, weight, xin, cosine, sine),
        fetched(512),
        flops=2 * 128 * 1536 * 512,
        size=3_000_000,
    )


def weight_copies(own, other, gate_up, down, sems, order):
    copies = {}
    for i, ref in enumerate((own, other)):
        for name in order:
            start, size, buffer = (0, GU, gate_up) if name == "gate_up" else (GU, DOWN, down)
            copies[i, name] = pltpu.make_async_copy(
                ref.at[:, pl.ds(start, size)], buffer.at[i], sems.at[2 * i + (name == "down")]
            )
    for i in range(2):
        for name in order:
            copies[i, name].start()
    return copies


def gate_and_up(both):
    tail = both[:, 2 * MAIN :]
    gate = jnp.concatenate([both[:, :MAIN], tail], axis=1)
    return gate, jnp.concatenate([both[:, MAIN : 2 * MAIN], pltpu.roll(tail, PART, 1)], axis=1)


def known(hidden):
    lane = lax.broadcasted_iota(jnp.int32, hidden.shape, 1)
    return jnp.where(lane < MAIN + PART, hidden, 0.0)


def feed_kernel(tokens, own, other, part, gate_up_out, gate_up, down, acc, sems):
    copies = weight_copies(own, other, gate_up, down, sems, ("gate_up", "down"))
    rows = tokens[...]
    for i in range(2):
        copies[i, "gate_up"].wait()
        both = nn(rows, gate_up[i])
        gate_up_out[i] = both.astype(BF)
        gate, up = gate_and_up(both)
        hidden = known(gate * jax.nn.sigmoid(gate) * up).astype(BF)
        copies[i, "down"].wait()
        out = nt(hidden, down[i])
        if i == 0:
            acc[...] = out
        else:
            part[...] = (acc[...] + out).astype(BF)


FEED_SCRATCH = [
    pltpu.VMEM((2, WIDTH, GU), BF),
    pltpu.VMEM((2, WIDTH, DOWN), BF),
    pltpu.VMEM((256, WIDTH), F32),
    pltpu.SemaphoreType.DMA((4,)),
]


def feed(tokens, own, other):
    return call(
        feed_kernel,
        (arr((256, WIDTH)), arr((2, 256, GU))),
        [VMEM, ANY, ANY],
        (tokens, own, other),
        FEED_SCRATCH,
        flops=2 * 256 * 1536 * 3840,
        size=15_000_000,
        exps=256 * 1280,
    )


def feed_grads(gate, up, grad_hidden, result):
    sig = jax.nn.sigmoid(gate)
    silu = gate * sig
    grad_gate = grad_hidden * up * sig * (1.0 + gate * (1.0 - sig))
    grad_up = grad_hidden * silu
    tail = grad_gate[:, MAIN:] + pltpu.roll(grad_up[:, MAIN:], PART, 1)
    hidden = known(silu * up).astype(BF)
    result[:, pl.ds(0, MAIN)] = grad_gate[:, :MAIN].astype(BF)
    result[:, pl.ds(MAIN, MAIN)] = grad_up[:, :MAIN].astype(BF)
    result[:, pl.ds(2 * MAIN, 2 * PART)] = tail.astype(BF)
    result[:, pl.ds(GU, DOWN)] = hidden
    return hidden


def feed_back_kernel(grads, own, other, gate_up_in, part, for_own, for_other, gate_up, down, acc, sems):
    copies = weight_copies(own, other, gate_up, down, sems, ("down", "gate_up"))
    rows = grads[...]
    for i, result in enumerate((for_own, for_other)):
        copies[i, "down"].wait()
        grad_hidden = nn(rows, down[i])
        gate, up = gate_and_up(gate_up_in[i].astype(F32))
        feed_grads(gate, up, grad_hidden, result)
        copies[i, "gate_up"].wait()
        out = nt(result[:, pl.ds(0, GU)], gate_up[i])
        if i == 0:
            acc[...] = out
        else:
            part[...] = (acc[...] + out).astype(BF)


def feed_back(grads, own, other, gate_up):
    return call(
        feed_back_kernel,
        (arr((256, WIDTH)), arr((256, FW)), arr((256, FW))),
        [VMEM, ANY, ANY, VMEM],
        (grads, own, other, gate_up),
        FEED_SCRATCH,
        flops=2 * 256 * 1536 * 3840,
        size=17_000_000,
        exps=256 * 1280,
    )


def feed_both_kernel(
    tokens, grads, own, other, part, for_own, for_other, gate_up, down, acc, acc_back, sems
):
    copies = weight_copies(own, other, gate_up, down, sems, ("gate_up", "down"))
    rows, grad_rows = tokens[...], grads[...]
    for i, result in enumerate((for_own, for_other)):
        copies[i, "gate_up"].wait()
        gate, up = gate_and_up(nn(rows, gate_up[i]))
        copies[i, "down"].wait()
        grad_hidden = nn(grad_rows, down[i])
        hidden = feed_grads(gate, up, grad_hidden, result)
        out, back = nt(hidden, down[i]), nt(result[:, pl.ds(0, GU)], gate_up[i])
        if i == 0:
            acc[...] = out
            acc_back[...] = back
        else:
            part[:, pl.ds(0, 32), :] = (acc_back[...] + back).astype(BF).reshape(8, 32, WIDTH)
            part[:, pl.ds(32, 32), :] = (acc[...] + out).astype(BF).reshape(8, 32, WIDTH)


def feed_both(tokens, grads, own, other):
    return call(
        feed_both_kernel,
        (arr((8, 64, WIDTH)), arr((256, FW)), arr((256, FW))),
        [VMEM, VMEM, ANY, ANY],
        (tokens, grads, own, other),
        FEED_SCRATCH[:3] + [pltpu.VMEM((256, WIDTH), F32)] + FEED_SCRATCH[3:],
        flops=4 * 256 * 1536 * 3840,
        size=17_000_000,
        exps=256 * 1280,
    )


def feed_grad_kernel(tokens, tokens_other, grads, grads_other, own, given, out):
    gate_up, hidden = pl.ds(0, GU), pl.ds(GU, DOWN)
    out[:, gate_up] = (tn(tokens[...], own[:, gate_up]) + tn(tokens_other[...], given[:, gate_up])).astype(BF)
    out[:, hidden] = (tn(grads[...], own[:, hidden]) + tn(grads_other[...], given[:, hidden])).astype(BF)


def feed_grad(tokens, tokens_other, grads, grads_other, own, given):
    rows = 256
    columns = pl.BlockSpec((256, rows), lambda i: (0, i))
    fixed = pl.BlockSpec((256, FW), lambda i: (0, 0))
    return call(
        feed_grad_kernel,
        arr((WIDTH, FW)),
        [columns] * 4 + [fixed] * 2,
        (tokens, tokens_other, grads, grads_other, own, given),
        flops=2 * 512 * 1536 * 1920,
        size=12_000_000,
        grid=(WIDTH // rows,),
        out_specs=pl.BlockSpec((rows, FW), lambda i: (i, 0)),
    )


def shifted(value, axis, steps):
    return lax.ppermute(value, axis, [(i, (i + steps) % 4) for i in range(4)])


def ring_first(piece, axis):
    return jnp.stack([piece] + [shifted(piece, axis, j) for j in (1, 2, 3)])


def ring_second(blocks, axis):
    return [blocks] + [shifted(blocks, axis, k) for k in (1, 2, 3)]


def ring_block(place, j, k):
    return lax.rem(place[0] + 4 - j, 4) * place[1] + lax.rem(place[2] + 4 - k, 4) * place[3]


def assemble_kernel(place, *refs):
    pieces, out, tail = refs[:4], refs[4], refs[5] if len(refs) > 5 else None
    for k in range(4):
        for j in range(4):
            block = ring_block(place, j, k)
            out[pl.ds(pl.multiple_of(block * 96, 32), 96), :] = pieces[k][j, pl.ds(0, 96), :]
            if tail is not None:
                tail[block] = pieces[k][j, pl.ds(96, 16), :]


def assemble(place, pieces):
    _, rows, columns = pieces[0].shape
    whole, tail = arr((WIDTH, columns)), arr((16, 16, columns))
    return call(
        assemble_kernel,
        whole if rows == 96 else (whole, tail),
        [SMEM] + [VMEM] * 4,
        (place, *pieces),
        size=4_000_000,
    )


def weight_grad_kernel(normed, grad_qkv, grad_att, attended, out, scratch):
    scratch[:, pl.ds(0, 512)] = tn(normed[...], grad_qkv[...]).astype(BF)
    scratch[:, pl.ds(512, QCOLS)] = tn(grad_att[...], attended[...]).astype(BF)
    for b in range(16):
        out[b // 4, b % 4] = scratch[pl.ds(b * 96, 96), :]


def weight_grad(*args):
    return call(
        weight_grad_kernel,
        arr((4, 4, 96, 896)),
        [VMEM] * 4,
        args,
        [pltpu.VMEM((WIDTH, 896), BF)],
        flops=2 * 128 * 1536 * 896,
        size=6_000_000,
    )


def apart_kernel(place, normed, grad_qkv, grad_att, attended, *rest):
    smalls, outs, scratch, scratch_out = rest[:-10], rest[-10:-2], rest[-2], rest[-1]
    scratch[...] = tn(normed[...], grad_qkv[...]).astype(BF)
    scratch_out[...] = tn(grad_att[...], attended[...]).astype(BF)
    row_index = lax.broadcasted_iota(jnp.int32, (16, 512), 0)
    for b in range(16):
        y, z = b // 4, b % 4
        rows = jnp.zeros((16, 512), F32)
        for layer in range(2):
            bias, *gains = (ref[...] for ref in smalls[3 * layer : 3 * layer + 3])
            moved = [(pltpu.roll(g, (WIDTH - 96 * b) % WIDTH, 1) if b else g)[:, :HEAD] for g in gains]
            gain_row = jnp.concatenate([*moved, jnp.zeros((1, 2 * HEAD), F32)], axis=1)
            for at, row in ((2 * layer, bias), (2 * layer + 1, gain_row)):
                rows = jnp.where(row_index == at, jnp.broadcast_to(row, (16, 512)), rows)
        rows = rows.astype(BF)
        for k in range(4):

            @pl.when(lax.rem(place[2] + k, 4) == z)
            def _(k=k):
                outs[k][y, pl.ds(0, 96), :] = scratch[pl.ds(b * 96, 96), :]
                outs[k][y, pl.ds(96, 16), :] = rows

            @pl.when(lax.rem(place[0] + k, 4) == y)
            def _(k=k):
                outs[4 + k][z] = scratch_out[pl.ds(b * 96, 96), :]


def apart(place, factors, smalls):
    parts = call(
        apart_kernel,
        (arr((4, 112, 512)),) * 4 + (arr((4, 96, QCOLS)),) * 4,
        [SMEM] + [VMEM] * 10,
        (place, *factors, *smalls),
        [pltpu.VMEM((WIDTH, 512), BF), pltpu.VMEM((WIDTH, QCOLS), BF)],
        flops=2 * 128 * 1536 * 896,
        size=6_000_000,
    )
    return parts[:4], parts[4:]


def sent(parts, axis):
    return [parts[0]] + [shifted(parts[k], axis, k) for k in (1, 2, 3)]


def summed(parts):
    return sum(part.astype(F32) for part in parts).astype(BF)


def scatter_blocks(blocks, axis, last):
    here = lax.axis_index(axis)
    own, *others = (lax.dynamic_index_in_dim(blocks, lax.rem(here + j, 4), 0, keepdims=False) for j in range(4))
    return summed([own] + [after(shifted(other, axis, j + 1), last) for j, other in enumerate(others)])


def after_heads_kernel(pieces, xin, gain, mixed, second):
    total = xin[...].astype(F32) + jnp.sum(pieces[...].astype(F32), axis=0)
    mixed[...] = total
    low = (total * inverse_rms(total) * gain[...]).astype(BF)
    for t in range(8):
        second[t] = low


def after_heads(pieces, xin, gain):
    return call(
        after_heads_kernel,
        (arr((32, WIDTH), F32), arr((8, 32, WIDTH))),
        [VMEM] * 3,
        (pieces, xin, gain),
        size=1_500_000,
    )


def after_feed_kernel(pieces, mixed, out):
    last = pl.ds(pieces.shape[1] - 32, 32)
    out[...] = (mixed[...] + jnp.sum(pieces[:, last, :].astype(F32), axis=0)).astype(BF)


def after_feed(pieces, mixed):
    return call(after_feed_kernel, arr((32, WIDTH)), [VMEM] * 2, (pieces, mixed), size=1_500_000)


def norm_back(grad, values, gain, grad_out):
    inverse = inverse_rms(values)
    norm = values * inverse
    scaled = grad * gain
    grad_gain = jnp.sum(grad * norm, axis=0, keepdims=True)
    return grad_out + inverse * (scaled - norm * jnp.mean(scaled * norm, axis=-1, keepdims=True)), grad_gain


def before_heads_kernel(pieces, mixed, gain, grad_out, grad_mixed, low, grad_gain):
    grad = jnp.sum(pieces[:, pl.ds(0, 32), :].astype(F32), axis=0)
    result, sums = norm_back(grad, mixed[...], gain[...], grad_out[...].astype(F32))
    grad_mixed[...] = result
    low[...] = result.astype(BF)
    grad_gain[...] = sums


def before_heads(pieces, mixed, gain, grad_out):
    return call(
        before_heads_kernel,
        (arr((32, WIDTH), F32), arr((32, WIDTH)), arr((1, WIDTH), F32)),
        [VMEM] * 4,
        (pieces, mixed, gain, grad_out),
        size=1_500_000,
    )


def layer_start_kernel(pieces, xin, gain, grad_mixed, grad_in, spread):
    grad = jnp.sum(pieces[...].astype(F32), axis=0)
    result, _ = norm_back(grad, xin[...].astype(F32), gain[...], grad_mixed[...])
    low = result.astype(BF)
    grad_in[...] = low
    for t in range(8):
        spread[t] = low


def layer_start(pieces, xin, gain, grad_mixed):
    return call(
        layer_start_kernel,
        (arr((32, WIDTH)), arr((8, 32, WIDTH))),
        [VMEM] * 4,
        (pieces, xin, gain, grad_mixed),
        size=1_500_000,
    )


def pack_kernel(gate, up, down, tails, out):
    for z in range(4):
        main = pl.ds(z * MAIN, MAIN)
        pieces = (
            (0, gate[:, main]),
            (MAIN, up[:, main]),
            (2 * MAIN, tails[z, :, pl.ds(0, 2 * PART)]),
            (GU, down[main, :].astype(F32).T.astype(BF)),
            (GU + MAIN, tails[z, :, pl.ds(2 * PART, 2 * PART)]),
        )
        for s in range(2):
            for at, piece in pieces:
                out[4 * s + z, :, pl.ds(at, piece.shape[1])] = piece


def pack(gate, up, down):
    rest = [jnp.pad(w, ((0, 0), (0, PART))).reshape(96, 4, PART) for w in (gate[:, TAIL:], up[:, TAIL:], down[TAIL:].T)]
    tails = jnp.concatenate([*rest, jnp.zeros((96, 4, PART), BF)], axis=2).transpose(1, 0, 2)
    return call(pack_kernel, arr((8, 96, FW)), [VMEM] * 4, (gate, up, down, tails), size=4_500_000)


def halves_kernel(pieces, first, second):
    first[...] = pieces[:4].reshape(384, FW)
    second[...] = pieces[4:].reshape(384, FW)


def halves(pieces):
    return call(halves_kernel, (arr((384, FW)), arr((384, FW))), [VMEM], (pieces,), size=6_000_000)


def unpack_kernel(pieces, gate, up, down):
    low = lax.broadcasted_iota(jnp.int32, (96, 2 * PART), 1) < PART
    tails = []
    for z in range(4):
        main = pl.ds(z * MAIN, MAIN)
        total = pieces[z].astype(F32) + pieces[4 + z].astype(F32)
        gate[:, main] = total[:, :MAIN]
        up[:, main] = total[:, MAIN : 2 * MAIN]
        down[main, :] = total[:, GU : GU + MAIN].T
        if z < 3:
            tails.append(total[:, 2 * MAIN : GU])
            down[pl.ds(TAIL + z * PART, PART), :] = total[:, GU + MAIN :].T[:PART]
    turned_tails = [pltpu.roll(tail, PART, 1) for tail in tails]
    gate[:, pl.ds(TAIL, 2 * PART)] = jnp.where(low, tails[0], turned_tails[1])
    gate[:, pl.ds(TAIL + 2 * PART, PART)] = tails[2][:, :PART]
    up[:, pl.ds(TAIL, 2 * PART)] = jnp.where(low, turned_tails[0], tails[1])
    up[:, pl.ds(TAIL + 2 * PART, PART)] = turned_tails[2][:, :PART]


def unpack(pieces):
    wide = TAIL + 3 * PART
    return call(
        unpack_kernel,
        (arr((96, wide), F32), arr((96, wide), F32), arr((wide, 96), F32)),
        [VMEM],
        (pieces,),
        size=7_000_000,
    )


def local(
    inputs, cotangent, segments, gain_one, w_query, b_query, w_keyval, b_keyval, w_out, gain_two, w_gate, w_up, w_down
):
    on_first = lax.axis_index("s") == 0
    core, chip = lax.axis_index("c"), lax.axis_index("x")
    block = lax.axis_index("y") * 4 + lax.axis_index("z")
    member = chip * 2 + core
    flag = jnp.stack([(core == 0).astype(jnp.int32), block.astype(jnp.int32)])

    def pick(first, second):
        return jnp.where(on_first, first, second)

    def gathered(piece, axes):
        return lax.all_gather(piece, axes, axis=0, tiled=True)

    def pair_gather(rows, axis):
        given = swap(rows, axis)
        is_low = lax.axis_index(axis) == 0
        return jnp.concatenate([jnp.where(is_low, rows, given), jnp.where(is_low, given, rows)], axis=0)

    def spread(rows, count, axes):
        return exchange(jnp.broadcast_to(rows[None], (count,) + rows.shape), axes)

    small = jnp.concatenate([gain_one[0], gain_two[0], b_keyval[0], jnp.zeros((72,), BF)])
    kv_blocks = w_keyval[0].reshape(24, 4, HEAD).transpose(1, 0, 2)
    kv_blocks = jnp.stack([kv_blocks[b] for b in BLOCK_ORDER])
    payload = jnp.concatenate(
        [kv_blocks, jnp.broadcast_to(small[None, None], (4, 1, HEAD)), jnp.zeros((4, 7, HEAD), BF)], axis=1
    )
    bias_rows = jnp.pad(b_query, ((0, 15), (0, QCOLS)))
    own = jnp.concatenate([jnp.concatenate([w_query[0], w_out[0].T], axis=1), bias_rows], axis=0)
    payload = after(payload, own)
    payload = exchange(jnp.concatenate([payload, payload], axis=0), ("s", "x", "c")).reshape(2, 4, 32, HEAD)
    other = swap(own, "s")

    def attention_rows(layer, matrices):
        return jnp.concatenate([matrices[:96, :QCOLS], payload[layer, :, :24].reshape(96, HEAD)], axis=1)

    def small_rows(layer, matrices):
        return jnp.concatenate([matrices[96:100, :QCOLS], payload[layer, :, 24]], axis=1)

    xin = pick(inputs[0], inputs[1])
    cot = pick(cotangent[0], cotangent[1])
    place_y, place_z = lax.axis_index("y").astype(jnp.int32), lax.axis_index("z").astype(jnp.int32)
    y_then_z = jnp.stack([place_y, jnp.int32(4), place_z, jnp.int32(1)])
    first, second = pick(own, other), pick(other, own)
    rows_first, out_rows = attention_rows(0, first), first[:96, QCOLS:]
    tails = [small_rows(0, first), small_rows(1, second), jnp.zeros((8, 512), BF)]
    rows_first = jnp.concatenate([rows_first, *tails], axis=0)
    rows_second = jnp.concatenate([attention_rows(1, second), second[:96, QCOLS:]], axis=1)
    ffn_packed = after(pack(w_gate[0], w_up[0], w_down[0]), (rows_first, rows_second))
    ffn_pieces = exchange(ffn_packed, ("s", "z"))
    blocks, out_blocks = ring_first(rows_first, "y"), ring_first(out_rows, "y")
    blocks, out_blocks, ffn_pieces = lax.optimization_barrier((blocks, out_blocks, ffn_pieces))
    ffn_halves = halves(ffn_pieces)
    x_block1 = pair_gather(pair_gather(after(xin, ffn_pieces), "c"), "x")
    ring = ring_second(blocks, "z")
    qkv_first, tail_first = assemble(y_then_z, ring)
    out_ring = ring_second(after(out_blocks, (ring[1], ring[3])), "z")

    seg = pick(segments[0], segments[1])
    local_pos = block * HEAD + jnp.arange(HEAD, dtype=jnp.int32)
    inverse_freq = THETA ** (-(jnp.arange(HEAD // 2, dtype=F32) * 2.0) / HEAD)
    angles = local_pos.astype(F32)[:, None] * inverse_freq[None, :]
    cosine = jnp.cos(angles)
    sine = jnp.sin(angles)
    cosine = jnp.concatenate([cosine, cosine], axis=1)
    sine = jnp.concatenate([-sine, sine], axis=1)
    seg_row = lax.dynamic_slice_in_dim(seg, block * HEAD, HEAD, 0)[None]
    seg_col = seg[:, None]

    def smalls(tail):
        bits = tail[:, :, QCOLS : QCOLS + 56].reshape(64, 56)
        gain_a = bits[:, :24].reshape(1, WIDTH).astype(F32)
        gain_b = bits[:, 24:48].reshape(1, WIDTH).astype(F32)
        kv_bias = lax.dynamic_slice_in_dim(bits[:, 48:].reshape(1, 512), (core * 2 + chip) * HEAD, HEAD, 1)
        bias = jnp.concatenate([tail[:1, 0, :QCOLS], kv_bias], axis=1).astype(F32)
        return gain_a, gain_b, bias

    gain_a1, gain_b1, bias1 = smalls(tail_first[:, :4])
    normed1, query1, kv = qkv_columns(flag, x_block1, gain_a1, qkv_first, bias1, cosine, sine)
    own1 = gathered(ffn_halves[0], "y")
    all_second = gathered(after(rows_second, kv), ("y", "z"))
    kv_mine1 = exchange(after(kv, (out_ring[1], out_ring[3])), ("y", "z")).reshape(SEQ, HEAD)
    kv_mine1, out_ring = lax.optimization_barrier((kv_mine1, out_ring))
    out_first = assemble(y_then_z, out_ring)
    kv_other1 = swap(kv_mine1, "c")
    attended1, wide1, lse1, part = attend(flag, query1, kv_mine1, kv_other1, seg_col, seg_row, out_first, 0)
    other1 = swap(after(own1, part), "c")
    mixed1, low = after_heads(after(exchange(part, ("x", "c")), other1), xin, gain_b1)
    second1 = exchange(low, ("z", "x")).reshape(256, WIDTH)
    own2 = gathered(after(ffn_halves[1], second1), "y")
    part, gate_up1 = feed(second1, own1, other1)
    pieces = exchange(part.reshape(8, 32, WIDTH), ("z", "x"))
    out_one = after_feed(pieces, mixed1)

    x_block2 = gathered(out_one, ("x", "c"))
    gain_a2, gain_b2, bias2 = smalls(tail_first[:, 4:8])
    normed2, query2, kv = qkv_columns(flag, x_block2, gain_a2, all_second, bias2, cosine, sine)
    kv_mine2 = exchange(kv, ("y", "z")).reshape(SEQ, HEAD)
    kv_other2 = swap(kv_mine2, "c")
    attended2, wide2, lse2, part = attend(flag, query2, kv_mine2, kv_other2, seg_col, seg_row, all_second, 512)
    mixed2, low = after_heads(exchange(part, ("x", "c")), out_one, gain_b2)
    second2 = exchange(low, ("z", "x")).reshape(256, WIDTH)
    other2 = swap(after(own2, second2), "c")
    cot_low = spread(after(cot, (second2, own2)), 8, ("z", "x")).reshape(256, WIDTH)
    second2 = after(second2, cot_low)
    fed2 = feed_both(second2, cot_low, own2, other2)

    def backward(grad_out, grad_low, fed, second, mixed, gain_b, xin, x_block, gain_a, normed, query, attended, wide,
                 kv_mine, kv_other, lse, weight, out_t, first, earlier=None):
        part, for_own, for_other = fed
        pieces = fed_pieces = exchange(part.reshape(8, -1, WIDTH), ("z", "x"))
        given = swap(for_other, "c")
        second_other, grad_other = swap(second, "c"), swap(grad_low, "c")
        grad_ffn = feed_grad(second, second_other, grad_low, grad_other, for_own, given)
        pieces, grad_ffn = lax.optimization_barrier((pieces, grad_ffn))
        grad_mixed, low, grad_gain_b = before_heads(pieces, mixed, gain_b, grad_out)
        grad_att = gathered(low, ("x", "c"))
        if earlier is not None:
            grad_ffn = after(grad_ffn, (earlier, grad_att))
        grad_ffn = lax.psum_scatter(grad_ffn, "y", scatter_dimension=0, tiled=True)
        grad_query, kept_half, sent_half = attend_back(
            flag, query, kv_mine, kv_other, seg_col, seg_row, lse, wide, grad_att, cosine, sine, out_t, first
        )
        grad_kv = (kept_half + swap(sent_half, "c").astype(F32)).astype(BF)
        grad_kv = exchange(grad_kv.reshape(16, HEAD, HEAD), ("y", "z"))
        grad_qkv, grad_bias, grad_gain_a, part = qkv_back(flag, grad_kv, grad_query, weight, x_block, cosine, sine)
        smalls = (grad_bias, grad_gain_a, grad_gain_b)
        factors = (normed, grad_qkv, grad_att, attended)
        if earlier is None:
            parts = smalls, weight_grad(*factors)
        else:
            parts = apart(y_then_z, factors, smalls + small_two)
            part = after(part, parts)
        pieces = exchange(part, ("x", "c"))
        grad_in, low = layer_start(pieces, xin, gain_a, grad_mixed)
        return grad_in, low, grad_ffn, parts, fed_pieces

    grad_two, low, ffn_two, attn_two, out_pieces = backward(
        cot, cot_low, fed2, second2, mixed2, gain_b2, out_one, x_block2, gain_a2, normed2, query2, attended2, wide2,
        kv_mine2, kv_other2, lse2, all_second, all_second, 512
    )
    out_two = after_feed(out_pieces, mixed2)
    grad_low = exchange(low, ("z", "x")).reshape(256, WIDTH)
    small_two, attn_two = attn_two
    grad_low = after(grad_low, attn_two)
    attn_two = after(attn_two, (ffn_two, grad_low))
    attn_two = lax.psum_scatter(attn_two.reshape(16 * 96, 896), "y", scatter_dimension=0, tiled=True)
    fed1 = feed_back(grad_low, own1, other1, gate_up1)
    grad_one, _, ffn_one, parts, _ = backward(
        grad_two, grad_low, fed1, second1, mixed1, gain_b1, xin, x_block1, gain_a1, normed1, query1, attended1, wide1,
        kv_mine1, kv_other1, lse1, qkv_first, out_first, 0, earlier=attn_two
    )
    ffn_payload = jnp.concatenate([ffn_one, ffn_two], axis=0).reshape(8, 96, FW)
    qkv_parts = sent(parts[0], "z")
    ffn_sum = exchange(after(ffn_payload, qkv_parts), ("s", "z"))
    halfway = summed(qkv_parts)
    out_parts = sent(after(parts[1], ffn_payload), "y")
    qkv_one = scatter_blocks(halfway, "y", ffn_sum)
    out_one_grad = scatter_blocks(summed(out_parts), "z", ffn_sum)
    attn_one = jnp.concatenate([qkv_one, jnp.pad(out_one_grad, ((0, 16), (0, 0)))], axis=1)
    attn_two = lax.psum_scatter(after(attn_two, (ffn_one, grad_one, halfway)), "z", scatter_dimension=0, tiled=True)

    grad_gate, grad_up, grad_down = unpack(ffn_sum)
    given = swap(jnp.concatenate([pick(attn_two, attn_one[:96]), attn_one[96:]], axis=0), "s").astype(F32)
    main = pick(attn_one[:96], attn_two).astype(F32) + given[:96]
    row = pick(attn_one[96], attn_one[98]).astype(F32) + pick(given[96], given[98])
    gains = pick(attn_one[97], attn_one[99]).astype(F32) + pick(given[97], given[99])
    gains = jnp.concatenate([gains[:96].reshape(4, 24), gains[128:224].reshape(4, 24)], axis=1)
    payload = jnp.concatenate(
        [
            main[:, QCOLS:512].reshape(4, 24, HEAD),
            jnp.pad(gains, ((0, 0), (0, HEAD - 48)))[:, None],
            jnp.broadcast_to(row[None, None, QCOLS:512], (4, 1, HEAD)),
            jnp.zeros((4, 6, HEAD), F32),
        ],
        axis=1,
    )
    arrived = [lax.dynamic_index_in_dim(payload, member, 0, keepdims=False)]
    for step in (1, 2, 3):
        given = lax.dynamic_index_in_dim(payload, member ^ step, 0, keepdims=False)
        arrived.append(lax.ppermute(given, ("x", "c"), [(m, m ^ step) for m in range(4)]))
    arrived = jnp.stack(arrived)
    payload = jnp.stack([lax.dynamic_index_in_dim(arrived, member ^ b, 0, keepdims=False) for b in BLOCK_ORDER])
    grad_keyval = payload[:, :24].transpose(1, 0, 2).reshape(24, 512)
    gains = jnp.sum(payload[:, 24], axis=0)
    kv_bias_row = lax.dynamic_index_in_dim(payload[:, 25], lax.axis_index("y"), 0, keepdims=False)
    grad_b_keyval = lax.dynamic_slice_in_dim(kv_bias_row, (lax.axis_index("z") * 4 + member) * 8, 8, 0)

    firsts, seconds = jnp.stack([out_one, grad_one]), jnp.stack([out_two, grad_two])
    given = swap(after(pick(seconds, firsts), ffn_sum), "s")
    rows = jnp.stack([pick(firsts, given), pick(given, seconds)], axis=1)[:, None]
    section_out, input_grad = rows[0], rows[1]

    return (
        section_out,
        input_grad,
        gains[None, :24],
        main[None, :, :QCOLS],
        row[None, :QCOLS],
        grad_keyval[None],
        grad_b_keyval[None],
        main[:, 512:].T[None],
        gains[None, 24:48],
        grad_gate[None],
        grad_up[None],
        grad_down[None],
    )


def solution(mesh):
    fine = Mesh(np.asarray(mesh.devices).reshape(2, 4, 4, 2, 2), AXES)
    block, member = ("y", "z"), ("x", "c")
    every = block + member
    tokens = P(None, every, None)
    split = P("s", every)
    columns = P("s", block, member)
    rows = P("s", member, block)
    keyval = P("s", every, None)
    outs = P("s", None, every, None)
    return jax.shard_map(
        local,
        mesh=fine,
        in_specs=(
            tokens, tokens, P(), split, columns, P("s", member), keyval, split, rows, split, columns, columns, rows,
        ),
        out_specs=(
            outs, outs, split, columns, P("s", member), keyval, split, rows, split, columns, columns, rows,
        ),
        check_vma=False,
    )
```

```python
import functools

import jax
import jax.numpy as jnp
import numpy as np
from jax import lax
from jax.experimental import pallas as pl
from jax.experimental.pallas import tpu as pltpu
from jax.sharding import Mesh
from jax.sharding import PartitionSpec as P

HEAD = 128
EPS = 1e-06
NEG = -1e30
THETA = 1000000.0
WIDTH = 1536
QCOLS = 384
SEQ = 2048
CHUNK = 512
MAIN = 512
PART = 64
TAIL = 4 * MAIN
GU = 2 * MAIN + 2 * PART
DOWN = MAIN + 2 * PART
FW = GU + DOWN
SCALE = HEAD**-0.5
AXES = ("s", "y", "z", "x", "c")
BLOCK_ORDER = (0, 2, 1, 3)
BF = jnp.bfloat16
F32 = jnp.float32
VMEM = pl.BlockSpec(memory_space=pltpu.VMEM)
SMEM = pl.BlockSpec(memory_space=pltpu.SMEM)
ANY = pl.BlockSpec(memory_space=pl.ANY)


def swap(value, axis):
    return lax.ppermute(value, axis, [(0, 1), (1, 0)])


def exchange(value, axes):
    return lax.all_to_all(value, axes, split_axis=0, concat_axis=0, tiled=True)


def nn(left, right):
    return jnp.dot(left, right, preferred_element_type=F32)


def nt(left, right):
    return lax.dot_general(left, right, (((1,), (1,)), ((), ())), preferred_element_type=F32)


def tn(left, right):
    return lax.dot_general(left, right, (((0,), (0,)), ((), ())), preferred_element_type=F32)


def after(value, done):
    return lax.optimization_barrier((value, done))[0]


def inverse_rms(values):
    return lax.rsqrt(jnp.mean(values * values, axis=-1, keepdims=True) + EPS)


def call(kernel, out_shape, in_specs, args, scratch=(), flops=0, size=0, exps=0, limit=52, **more):
    return pl.pallas_call(
        kernel,
        out_shape=out_shape,
        in_specs=in_specs,
        scratch_shapes=list(scratch),
        compiler_params=pltpu.CompilerParams(vmem_limit_bytes=limit * 1024 * 1024),
        cost_estimate=pl.CostEstimate(flops=flops, bytes_accessed=size, transcendentals=exps),
        **more,
    )(*args)


def arr(shape, dtype=BF):
    return jax.ShapeDtypeStruct(shape, dtype)


def turned(values, cosine, sine):
    return values * cosine + pltpu.roll(values, HEAD // 2, 1) * sine


def fetch(weight, first, into, sem):
    copy = pltpu.make_async_copy(weight.at[:, pl.ds(first, into.shape[1])], into, sem)
    copy.start()
    return copy


def fetched(columns):
    return [pltpu.VMEM((WIDTH, columns), BF), pltpu.SemaphoreType.DMA]


def qkv_kernel(flag, xin, gain, weight, bias, cosine, sine, normed, query, kv, whole, sem):
    copy = fetch(weight, 0, whole, sem)
    cos, sin = cosine[...], sine[...]
    rows = xin[...].astype(F32)
    low = (rows * inverse_rms(rows) * gain[...]).astype(BF)
    normed[...] = low
    copy.wait()
    out = nn(low, whole[...]) + bias[...]
    for h in range(3):
        query[h] = turned(out[:, h * HEAD : (h + 1) * HEAD], cos, sin).astype(BF)
    last = out[:, QCOLS:]
    last = jnp.where(flag[0] == 1, turned(last, cos, sin), last).astype(BF)
    for b in range(16):
        kv[b] = last


def qkv_columns(flag, xin, gain, weight, bias, cosine, sine):
    return call(
        qkv_kernel,
        (arr((HEAD, WIDTH)), arr((3, HEAD, HEAD)), arr((16, HEAD, HEAD))),
        [SMEM, VMEM, VMEM, ANY, VMEM, VMEM, VMEM],
        (flag, xin, gain, weight, bias, cosine, sine),
        fetched(512),
        flops=2 * 128 * 1536 * 512,
        size=3_000_000,
    )


def key_scores(query_all, keys, key_seg, query_seg, first_key, first_query):
    scores = nt(keys, query_all) * SCALE
    key_pos = first_key + lax.broadcasted_iota(jnp.int32, (CHUNK, HEAD), 0)
    query_pos = first_query + lax.broadcasted_iota(jnp.int32, (CHUNK, HEAD), 1)
    allowed = (key_seg == query_seg) & (key_pos <= query_pos)
    return [jnp.where(allowed, scores[:, h * HEAD : (h + 1) * HEAD], NEG) for h in range(3)]


def attend_kernel(
    first, flag, query, kv_mine, kv_other, seg_col, seg_row, weight, attended, wide, lse, part, top, total, acc, out_t, sem
):
    copy = fetch(weight, first, out_t, sem)
    query_all = query[...].reshape(3 * HEAD, HEAD)
    is_key = flag[0] == 1
    first_query = flag[1] * HEAD
    top[...] = jnp.full(top.shape, -3e38, F32)
    total[...] = jnp.zeros(total.shape, F32)
    acc[...] = jnp.zeros(acc.shape, F32)

    @pl.loop(0, SEQ // CHUNK)
    def _(step):
        at = pl.ds(pl.multiple_of(step * CHUNK, CHUNK), CHUNK)
        mine, other = kv_mine[at, :], kv_other[at, :]
        keys = jnp.where(is_key, mine, other)
        values = jnp.where(is_key, other, mine)
        scores = key_scores(query_all, keys, seg_col[at, :], seg_row[...], step * CHUNK, first_query)
        for h in range(3):
            columns = pl.ds(h * HEAD, HEAD)
            old = top[:, columns]
            new = jnp.maximum(old, jnp.max(scores[h], axis=0, keepdims=True))
            shrink = jnp.exp(old - new)
            raised = jnp.exp(scores[h] - new)
            top[:, columns] = new
            total[:, columns] = total[:, columns] * shrink + jnp.sum(raised, axis=0, keepdims=True)
            acc[:, columns] = acc[:, columns] * shrink + tn(values, raised.astype(BF))

    lse[...] = top[...] + jnp.log(total[...])
    done = acc[...] / total[...]
    wide[...] = done
    for h in range(3):
        attended[:, pl.ds(h * HEAD, HEAD)] = done[:, h * HEAD : (h + 1) * HEAD].T.astype(BF)
    copy.wait()
    out = nt(attended[...], out_t[...]).astype(BF)
    for t in range(4):
        part[t] = out[t * 32 : (t + 1) * 32]


def attend(flag, query, kv_mine, kv_other, seg_col, seg_row, weight, first):
    return call(
        functools.partial(attend_kernel, first),
        (arr((HEAD, QCOLS)), arr((HEAD, QCOLS), F32), arr((1, QCOLS), F32), arr((4, 32, WIDTH))),
        [SMEM] + [VMEM] * 5 + [ANY],
        (flag, query, kv_mine, kv_other, seg_col, seg_row, weight),
        [
            pltpu.VMEM((1, QCOLS), F32),
            pltpu.VMEM((1, QCOLS), F32),
            pltpu.VMEM((HEAD, QCOLS), F32),
            *fetched(QCOLS),
        ],
        flops=4 * 384 * 2048 * 128 + 2 * 128 * 384 * 1536,
        size=3_000_000,
        exps=384 * 2048,
    )


def attend_back_kernel(
    first, flag, query, kv_mine, kv_other, seg_col, seg_row, lse, wide, grad_att, cosine, sine, weight,
    grad_query, kept, sent, low, acc, out_t, sem
):
    copy = fetch(weight, first, out_t, sem)
    query_all = query[...].reshape(3 * HEAD, HEAD)
    is_key = flag[0] == 1
    first_query = flag[1] * HEAD
    sums = []
    copy.wait()
    grad_attended = nn(grad_att[...], out_t[...]).astype(BF)
    for h in range(3):
        grad_head = grad_attended[:, h * HEAD : (h + 1) * HEAD]
        low[pl.ds(h * HEAD, HEAD), :] = grad_head
        with_output = grad_head.astype(F32).T * wide[:, pl.ds(h * HEAD, HEAD)]
        sums.append(jnp.sum(with_output, axis=0, keepdims=True))
    grad_rows = low[...]
    lse_row = lse[...]

    def chunk(step):
        at = pl.ds(pl.multiple_of(step * CHUNK, CHUNK), CHUNK)
        mine, other = kv_mine[at, :], kv_other[at, :]
        keys = jnp.where(is_key, mine, other)
        values = jnp.where(is_key, other, mine)
        scores = key_scores(query_all, keys, seg_col[at, :], seg_row[...], step * CHUNK, first_query)
        probs = [jnp.exp(scores[h] - lse_row[:, h * HEAD : (h + 1) * HEAD]) for h in range(3)]
        grad_probs = nt(values, grad_rows)
        return at, keys, probs, grad_probs

    acc[...] = jnp.zeros(acc.shape, F32)

    @pl.loop(0, SEQ // CHUNK)
    def _(step):
        at, keys, probs, grad_probs = chunk(step)
        low_probs = jnp.concatenate([p.astype(BF) for p in probs], axis=1)
        low_scores = jnp.concatenate(
            [
                (probs[h] * (grad_probs[:, h * HEAD : (h + 1) * HEAD] - sums[h])).astype(BF)
                for h in range(3)
            ],
            axis=1,
        )
        grad_value = nn(low_probs, grad_rows)
        grad_key = nn(low_scores, query_all) * SCALE
        acc[...] += tn(keys, low_scores)
        kept[at, :] = jnp.where(is_key, grad_key, grad_value)
        sent[at, :] = jnp.where(is_key, grad_value, grad_key).astype(BF)

    cos, sin = cosine[...], sine[...]
    for h in range(3):
        rows = acc[:, pl.ds(h * HEAD, HEAD)].T * SCALE
        grad_query[:, pl.ds(h * HEAD, HEAD)] = turned(rows, cos, -sin).astype(BF)


def attend_back(flag, query, kv_mine, kv_other, seg_col, seg_row, lse, wide, grad_att, cosine, sine, weight, first):
    return call(
        functools.partial(attend_back_kernel, first),
        (arr((HEAD, QCOLS)), arr((SEQ, HEAD), F32), arr((SEQ, HEAD))),
        [SMEM] + [VMEM] * 10 + [ANY],
        (flag, query, kv_mine, kv_other, seg_col, seg_row, lse, wide, grad_att, cosine, sine, weight),
        [pltpu.VMEM((3 * HEAD, HEAD), BF), pltpu.VMEM((HEAD, QCOLS), F32), *fetched(QCOLS)],
        flops=10 * 384 * 2048 * 128 + 2 * 128 * 384 * 1536,
        size=5_000_000,
        exps=2 * 384 * 2048,
    )


def qkv_back_kernel(
    flag, pieces, grad_query, weight, xin, cosine, sine, grad_qkv, grad_bias, grad_gain, part, whole, sem
):
    copy = fetch(weight, 0, whole, sem)
    total = jnp.sum(pieces[...].astype(F32), axis=0)
    total = jnp.where(flag[0] == 1, turned(total, cosine[...], -sine[...]), total).astype(BF)
    grad_qkv[:, pl.ds(0, QCOLS)] = grad_query[...]
    grad_qkv[:, pl.ds(QCOLS, HEAD)] = total
    grads = grad_qkv[...]
    grad_bias[...] = jnp.sum(grads.astype(F32), axis=0, keepdims=True)
    copy.wait()
    out = nt(grads, whole[...])
    rows = xin[...].astype(F32)
    grad_gain[...] = jnp.sum(out * rows * inverse_rms(rows), axis=0, keepdims=True)
    low = out.astype(BF)
    for t in range(4):
        part[t] = low[t * 32 : (t + 1) * 32]


def qkv_back(flag, pieces, grad_query, weight, xin, cosine, sine):
    return call(
        qkv_back_kernel,
        (arr((HEAD, 512)), arr((1, 512), F32), arr((1, WIDTH), F32), arr((4, 32, WIDTH))),
        [SMEM, VMEM, VMEM, ANY, VMEM, VMEM, VMEM],
        (flag, pieces, grad_query, weight, xin, cosine, sine),
        fetched(512),
        flops=2 * 128 * 1536 * 512,
        size=3_000_000,
    )


def weight_copies(own, other, gate_up, down, sems, order):
    copies = {}
    for i, ref in enumerate((own, other)):
        for name in order:
            start, size, buffer = (0, GU, gate_up) if name == "gate_up" else (GU, DOWN, down)
            copies[i, name] = pltpu.make_async_copy(
                ref.at[:, pl.ds(start, size)], buffer.at[i], sems.at[2 * i + (name == "down")]
            )
    for i in range(2):
        for name in order:
            copies[i, name].start()
    return copies


def gate_and_up(both):
    tail = both[:, 2 * MAIN :]
    gate = jnp.concatenate([both[:, :MAIN], tail], axis=1)
    return gate, jnp.concatenate([both[:, MAIN : 2 * MAIN], pltpu.roll(tail, PART, 1)], axis=1)


def known(hidden):
    lane = lax.broadcasted_iota(jnp.int32, hidden.shape, 1)
    return jnp.where(lane < MAIN + PART, hidden, 0.0)


def feed_kernel(tokens, own, other, part, gate_up_out, gate_up, down, acc, sems):
    copies = weight_copies(own, other, gate_up, down, sems, ("gate_up", "down"))
    rows = tokens[...]
    for i in range(2):
        copies[i, "gate_up"].wait()
        both = nn(rows, gate_up[i])
        gate_up_out[i] = both.astype(BF)
        gate, up = gate_and_up(both)
        hidden = known(gate * jax.nn.sigmoid(gate) * up).astype(BF)
        copies[i, "down"].wait()
        out = nt(hidden, down[i])
        if i == 0:
            acc[...] = out
        else:
            part[...] = (acc[...] + out).astype(BF)


FEED_SCRATCH = [
    pltpu.VMEM((2, WIDTH, GU), BF),
    pltpu.VMEM((2, WIDTH, DOWN), BF),
    pltpu.VMEM((256, WIDTH), F32),
    pltpu.SemaphoreType.DMA((4,)),
]


def feed(tokens, own, other):
    return call(
        feed_kernel,
        (arr((256, WIDTH)), arr((2, 256, GU))),
        [VMEM, ANY, ANY],
        (tokens, own, other),
        FEED_SCRATCH,
        flops=2 * 256 * 1536 * 3840,
        size=15_000_000,
        exps=256 * 1280,
    )


def feed_grads(gate, up, grad_hidden, result):
    sig = jax.nn.sigmoid(gate)
    silu = gate * sig
    grad_gate = grad_hidden * up * sig * (1.0 + gate * (1.0 - sig))
    grad_up = grad_hidden * silu
    tail = grad_gate[:, MAIN:] + pltpu.roll(grad_up[:, MAIN:], PART, 1)
    hidden = known(silu * up).astype(BF)
    result[:, pl.ds(0, MAIN)] = grad_gate[:, :MAIN].astype(BF)
    result[:, pl.ds(MAIN, MAIN)] = grad_up[:, :MAIN].astype(BF)
    result[:, pl.ds(2 * MAIN, 2 * PART)] = tail.astype(BF)
    result[:, pl.ds(GU, DOWN)] = hidden
    return hidden


def feed_back_kernel(grads, own, other, gate_up_in, part, for_own, for_other, gate_up, down, acc, sems):
    copies = weight_copies(own, other, gate_up, down, sems, ("down", "gate_up"))
    rows = grads[...]
    for i, result in enumerate((for_own, for_other)):
        copies[i, "down"].wait()
        grad_hidden = nn(rows, down[i])
        gate, up = gate_and_up(gate_up_in[i].astype(F32))
        feed_grads(gate, up, grad_hidden, result)
        copies[i, "gate_up"].wait()
        out = nt(result[:, pl.ds(0, GU)], gate_up[i])
        if i == 0:
            acc[...] = out
        else:
            part[...] = (acc[...] + out).astype(BF)


def feed_back(grads, own, other, gate_up):
    return call(
        feed_back_kernel,
        (arr((256, WIDTH)), arr((256, FW)), arr((256, FW))),
        [VMEM, ANY, ANY, VMEM],
        (grads, own, other, gate_up),
        FEED_SCRATCH,
        flops=2 * 256 * 1536 * 3840,
        size=17_000_000,
        exps=256 * 1280,
    )


def feed_both_kernel(
    tokens, grads, own, other, part, for_own, for_other, gate_up, down, acc, acc_back, sems
):
    copies = weight_copies(own, other, gate_up, down, sems, ("gate_up", "down"))
    rows, grad_rows = tokens[...], grads[...]
    for i, result in enumerate((for_own, for_other)):
        copies[i, "gate_up"].wait()
        gate, up = gate_and_up(nn(rows, gate_up[i]))
        copies[i, "down"].wait()
        grad_hidden = nn(grad_rows, down[i])
        hidden = feed_grads(gate, up, grad_hidden, result)
        out, back = nt(hidden, down[i]), nt(result[:, pl.ds(0, GU)], gate_up[i])
        if i == 0:
            acc[...] = out
            acc_back[...] = back
        else:
            part[:, pl.ds(0, 32), :] = (acc_back[...] + back).astype(BF).reshape(8, 32, WIDTH)
            part[:, pl.ds(32, 32), :] = (acc[...] + out).astype(BF).reshape(8, 32, WIDTH)


def feed_both(tokens, grads, own, other):
    return call(
        feed_both_kernel,
        (arr((8, 64, WIDTH)), arr((256, FW)), arr((256, FW))),
        [VMEM, VMEM, ANY, ANY],
        (tokens, grads, own, other),
        FEED_SCRATCH[:3] + [pltpu.VMEM((256, WIDTH), F32)] + FEED_SCRATCH[3:],
        flops=4 * 256 * 1536 * 3840,
        size=17_000_000,
        exps=256 * 1280,
    )


def feed_grad_kernel(tokens, tokens_other, grads, grads_other, own, given, out):
    gate_up, hidden = pl.ds(0, GU), pl.ds(GU, DOWN)
    out[:, gate_up] = (tn(tokens[...], own[:, gate_up]) + tn(tokens_other[...], given[:, gate_up])).astype(BF)
    out[:, hidden] = (tn(grads[...], own[:, hidden]) + tn(grads_other[...], given[:, hidden])).astype(BF)


def feed_grad(tokens, tokens_other, grads, grads_other, own, given):
    rows = 256
    columns = pl.BlockSpec((256, rows), lambda i: (0, i))
    fixed = pl.BlockSpec((256, FW), lambda i: (0, 0))
    return call(
        feed_grad_kernel,
        arr((WIDTH, FW)),
        [columns] * 4 + [fixed] * 2,
        (tokens, tokens_other, grads, grads_other, own, given),
        flops=2 * 512 * 1536 * 1920,
        size=12_000_000,
        grid=(WIDTH // rows,),
        out_specs=pl.BlockSpec((rows, FW), lambda i: (i, 0)),
    )


def shifted(value, axis, steps):
    return lax.ppermute(value, axis, [(i, (i + steps) % 4) for i in range(4)])


def ring_first(piece, axis):
    return jnp.stack([piece] + [shifted(piece, axis, j) for j in (1, 2, 3)])


def ring_second(blocks, axis):
    return [blocks] + [shifted(blocks, axis, k) for k in (1, 2, 3)]


def ring_block(place, j, k):
    return lax.rem(place[0] + 4 - j, 4) * place[1] + lax.rem(place[2] + 4 - k, 4) * place[3]


def assemble_kernel(place, *refs):
    pieces, out, tail = refs[:4], refs[4], refs[5] if len(refs) > 5 else None
    for k in range(4):
        for j in range(4):
            block = ring_block(place, j, k)
            out[pl.ds(pl.multiple_of(block * 96, 32), 96), :] = pieces[k][j, pl.ds(0, 96), :]
            if tail is not None:
                tail[block] = pieces[k][j, pl.ds(96, 16), :]


def assemble(place, pieces):
    _, rows, columns = pieces[0].shape
    whole, tail = arr((WIDTH, columns)), arr((16, 16, columns))
    return call(
        assemble_kernel,
        whole if rows == 96 else (whole, tail),
        [SMEM] + [VMEM] * 4,
        (place, *pieces),
        size=4_000_000,
    )


def weight_grad_kernel(normed, grad_qkv, grad_att, attended, out, scratch):
    scratch[:, pl.ds(0, 512)] = tn(normed[...], grad_qkv[...]).astype(BF)
    scratch[:, pl.ds(512, QCOLS)] = tn(grad_att[...], attended[...]).astype(BF)
    for b in range(16):
        out[b // 4, b % 4] = scratch[pl.ds(b * 96, 96), :]


def weight_grad(*args):
    return call(
        weight_grad_kernel,
        arr((4, 4, 96, 896)),
        [VMEM] * 4,
        args,
        [pltpu.VMEM((WIDTH, 896), BF)],
        flops=2 * 128 * 1536 * 896,
        size=6_000_000,
    )


def apart_kernel(place, normed, grad_qkv, grad_att, attended, *rest):
    smalls, outs, scratch, scratch_out = rest[:-10], rest[-10:-2], rest[-2], rest[-1]
    scratch[...] = tn(normed[...], grad_qkv[...]).astype(BF)
    scratch_out[...] = tn(grad_att[...], attended[...]).astype(BF)
    row_index = lax.broadcasted_iota(jnp.int32, (16, 512), 0)
    for b in range(16):
        y, z = b // 4, b % 4
        rows = jnp.zeros((16, 512), F32)
        for layer in range(2):
            bias, *gains = (ref[...] for ref in smalls[3 * layer : 3 * layer + 3])
            moved = [(pltpu.roll(g, (WIDTH - 96 * b) % WIDTH, 1) if b else g)[:, :HEAD] for g in gains]
            gain_row = jnp.concatenate([*moved, jnp.zeros((1, 2 * HEAD), F32)], axis=1)
            for at, row in ((2 * layer, bias), (2 * layer + 1, gain_row)):
                rows = jnp.where(row_index == at, jnp.broadcast_to(row, (16, 512)), rows)
        rows = rows.astype(BF)
        for k in range(4):

            @pl.when(lax.rem(place[2] + k, 4) == z)
            def _(k=k):
                outs[k][y, pl.ds(0, 96), :] = scratch[pl.ds(b * 96, 96), :]
                outs[k][y, pl.ds(96, 16), :] = rows

            @pl.when(lax.rem(place[0] + k, 4) == y)
            def _(k=k):
                outs[4 + k][z] = scratch_out[pl.ds(b * 96, 96), :]


def apart(place, factors, smalls):
    parts = call(
        apart_kernel,
        (arr((4, 112, 512)),) * 4 + (arr((4, 96, QCOLS)),) * 4,
        [SMEM] + [VMEM] * 10,
        (place, *factors, *smalls),
        [pltpu.VMEM((WIDTH, 512), BF), pltpu.VMEM((WIDTH, QCOLS), BF)],
        flops=2 * 128 * 1536 * 896,
        size=6_000_000,
    )
    return parts[:4], parts[4:]


def sent(parts, axis):
    return [parts[0]] + [shifted(parts[k], axis, k) for k in (1, 2, 3)]


def summed(parts):
    return sum(part.astype(F32) for part in parts).astype(BF)


def scatter_blocks(blocks, axis, last):
    here = lax.axis_index(axis)
    own, *others = (lax.dynamic_index_in_dim(blocks, lax.rem(here + j, 4), 0, keepdims=False) for j in range(4))
    moved = [shifted(other, axis, j + 1) for j, other in enumerate(others)]
    return summed([own] + (moved if last is None else after(moved, last)))


def after_heads_kernel(pieces, xin, gain, mixed, second):
    total = xin[...].astype(F32) + jnp.sum(pieces[...].astype(F32), axis=0)
    mixed[...] = total
    low = (total * inverse_rms(total) * gain[...]).astype(BF)
    for t in range(8):
        second[t] = low


def after_heads(pieces, xin, gain):
    return call(
        after_heads_kernel,
        (arr((32, WIDTH), F32), arr((8, 32, WIDTH))),
        [VMEM] * 3,
        (pieces, xin, gain),
        size=1_500_000,
    )


def after_feed_kernel(pieces, mixed, out):
    last = pl.ds(pieces.shape[1] - 32, 32)
    out[...] = (mixed[...] + jnp.sum(pieces[:, last, :].astype(F32), axis=0)).astype(BF)


def after_feed(pieces, mixed):
    return call(after_feed_kernel, arr((32, WIDTH)), [VMEM] * 2, (pieces, mixed), size=1_500_000)


def norm_back(grad, values, gain, grad_out):
    inverse = inverse_rms(values)
    norm = values * inverse
    scaled = grad * gain
    grad_gain = jnp.sum(grad * norm, axis=0, keepdims=True)
    return grad_out + inverse * (scaled - norm * jnp.mean(scaled * norm, axis=-1, keepdims=True)), grad_gain


def before_heads_kernel(pieces, mixed, gain, grad_out, grad_mixed, low, grad_gain):
    grad = jnp.sum(pieces[:, pl.ds(0, 32), :].astype(F32), axis=0)
    result, sums = norm_back(grad, mixed[...], gain[...], grad_out[...].astype(F32))
    grad_mixed[...] = result
    low[...] = result.astype(BF)
    grad_gain[...] = sums


def before_heads(pieces, mixed, gain, grad_out):
    return call(
        before_heads_kernel,
        (arr((32, WIDTH), F32), arr((32, WIDTH)), arr((1, WIDTH), F32)),
        [VMEM] * 4,
        (pieces, mixed, gain, grad_out),
        size=1_500_000,
    )


def layer_start_kernel(pieces, xin, gain, grad_mixed, grad_in, spread):
    grad = jnp.sum(pieces[...].astype(F32), axis=0)
    result, _ = norm_back(grad, xin[...].astype(F32), gain[...], grad_mixed[...])
    low = result.astype(BF)
    grad_in[...] = low
    for t in range(8):
        spread[t] = low


def layer_start(pieces, xin, gain, grad_mixed):
    return call(
        layer_start_kernel,
        (arr((32, WIDTH)), arr((8, 32, WIDTH))),
        [VMEM] * 4,
        (pieces, xin, gain, grad_mixed),
        size=1_500_000,
    )


def pack_kernel(gate, up, down, tails, out):
    for z in range(4):
        main = pl.ds(z * MAIN, MAIN)
        pieces = (
            (0, gate[:, main]),
            (MAIN, up[:, main]),
            (2 * MAIN, tails[z, :, pl.ds(0, 2 * PART)]),
            (GU, down[main, :].astype(F32).T.astype(BF)),
            (GU + MAIN, tails[z, :, pl.ds(2 * PART, 2 * PART)]),
        )
        for s in range(2):
            for at, piece in pieces:
                out[4 * s + z, :, pl.ds(at, piece.shape[1])] = piece


def pack(gate, up, down):
    rest = [jnp.pad(w, ((0, 0), (0, PART))).reshape(96, 4, PART) for w in (gate[:, TAIL:], up[:, TAIL:], down[TAIL:].T)]
    tails = jnp.concatenate([*rest, jnp.zeros((96, 4, PART), BF)], axis=2).transpose(1, 0, 2)
    return call(pack_kernel, arr((8, 96, FW)), [VMEM] * 4, (gate, up, down, tails), size=4_500_000)


def halves_kernel(pieces, first, second):
    first[...] = pieces[:4].reshape(384, FW)
    second[...] = pieces[4:].reshape(384, FW)


def halves(pieces):
    return call(halves_kernel, (arr((384, FW)), arr((384, FW))), [VMEM], (pieces,), size=6_000_000)


def unpack_kernel(pieces, gate, up, down):
    low = lax.broadcasted_iota(jnp.int32, (96, 2 * PART), 1) < PART
    tails = []
    for z in range(4):
        main = pl.ds(z * MAIN, MAIN)
        total = pieces[z].astype(F32) + pieces[4 + z].astype(F32)
        gate[:, main] = total[:, :MAIN]
        up[:, main] = total[:, MAIN : 2 * MAIN]
        down[main, :] = total[:, GU : GU + MAIN].T
        if z < 3:
            tails.append(total[:, 2 * MAIN : GU])
            down[pl.ds(TAIL + z * PART, PART), :] = total[:, GU + MAIN :].T[:PART]
    turned_tails = [pltpu.roll(tail, PART, 1) for tail in tails]
    gate[:, pl.ds(TAIL, 2 * PART)] = jnp.where(low, tails[0], turned_tails[1])
    gate[:, pl.ds(TAIL + 2 * PART, PART)] = tails[2][:, :PART]
    up[:, pl.ds(TAIL, 2 * PART)] = jnp.where(low, turned_tails[0], tails[1])
    up[:, pl.ds(TAIL + 2 * PART, PART)] = turned_tails[2][:, :PART]


def unpack(pieces):
    wide = TAIL + 3 * PART
    return call(
        unpack_kernel,
        (arr((96, wide), F32), arr((96, wide), F32), arr((wide, 96), F32)),
        [VMEM],
        (pieces,),
        size=7_000_000,
    )


def local(
    inputs, cotangent, segments, gain_one, w_query, b_query, w_keyval, b_keyval, w_out, gain_two, w_gate, w_up, w_down
):
    on_first = lax.axis_index("s") == 0
    core, chip = lax.axis_index("c"), lax.axis_index("x")
    block = lax.axis_index("y") * 4 + lax.axis_index("z")
    member = chip * 2 + core
    flag = jnp.stack([(core == 0).astype(jnp.int32), block.astype(jnp.int32)])

    def pick(first, second):
        return jnp.where(on_first, first, second)

    def gathered(piece, axes):
        return lax.all_gather(piece, axes, axis=0, tiled=True)

    def pair_gather(rows, axis):
        given = swap(rows, axis)
        is_low = lax.axis_index(axis) == 0
        return jnp.concatenate([jnp.where(is_low, rows, given), jnp.where(is_low, given, rows)], axis=0)

    def spread(rows, count, axes):
        return exchange(jnp.broadcast_to(rows[None], (count,) + rows.shape), axes)

    small = jnp.concatenate([gain_one[0], gain_two[0], b_keyval[0], jnp.zeros((72,), BF)])
    kv_blocks = w_keyval[0].reshape(24, 4, HEAD).transpose(1, 0, 2)
    kv_blocks = jnp.stack([kv_blocks[b] for b in BLOCK_ORDER])
    payload = jnp.concatenate(
        [kv_blocks, jnp.broadcast_to(small[None, None], (4, 1, HEAD)), jnp.zeros((4, 7, HEAD), BF)], axis=1
    )
    bias_rows = jnp.pad(b_query, ((0, 15), (0, QCOLS)))
    own = jnp.concatenate([jnp.concatenate([w_query[0], w_out[0].T], axis=1), bias_rows], axis=0)
    payload = after(payload, own)
    payload = exchange(jnp.concatenate([payload, payload], axis=0), ("s", "x", "c")).reshape(2, 4, 32, HEAD)
    other = swap(own, "s")

    def attention_rows(layer, matrices):
        return jnp.concatenate([matrices[:96, :QCOLS], payload[layer, :, :24].reshape(96, HEAD)], axis=1)

    def small_rows(layer, matrices):
        return jnp.concatenate([matrices[96:100, :QCOLS], payload[layer, :, 24]], axis=1)

    xin = pick(inputs[0], inputs[1])
    cot = pick(cotangent[0], cotangent[1])
    place_y, place_z = lax.axis_index("y").astype(jnp.int32), lax.axis_index("z").astype(jnp.int32)
    y_then_z = jnp.stack([place_y, jnp.int32(4), place_z, jnp.int32(1)])
    first, second = pick(own, other), pick(other, own)
    rows_first, out_rows = attention_rows(0, first), first[:96, QCOLS:]
    tails = [small_rows(0, first), small_rows(1, second), jnp.zeros((8, 512), BF)]
    rows_first = jnp.concatenate([rows_first, *tails], axis=0)
    rows_second = jnp.concatenate([attention_rows(1, second), second[:96, QCOLS:]], axis=1)
    ffn_packed = after(pack(w_gate[0], w_up[0], w_down[0]), (rows_first, rows_second))
    ffn_pieces = exchange(ffn_packed, ("s", "z"))
    blocks, out_blocks = ring_first(rows_first, "y"), ring_first(out_rows, "y")
    blocks, out_blocks, ffn_pieces = lax.optimization_barrier((blocks, out_blocks, ffn_pieces))
    ffn_halves = halves(ffn_pieces)
    x_block1 = pair_gather(pair_gather(after(xin, ffn_pieces), "c"), "x")
    ring = ring_second(blocks, "z")
    qkv_first, tail_first = assemble(y_then_z, ring)
    out_ring = ring_second(after(out_blocks, (ring[1], ring[3])), "z")

    seg = pick(segments[0], segments[1])
    local_pos = block * HEAD + jnp.arange(HEAD, dtype=jnp.int32)
    inverse_freq = THETA ** (-(jnp.arange(HEAD // 2, dtype=F32) * 2.0) / HEAD)
    angles = local_pos.astype(F32)[:, None] * inverse_freq[None, :]
    cosine = jnp.cos(angles)
    sine = jnp.sin(angles)
    cosine = jnp.concatenate([cosine, cosine], axis=1)
    sine = jnp.concatenate([-sine, sine], axis=1)
    seg_row = lax.dynamic_slice_in_dim(seg, block * HEAD, HEAD, 0)[None]
    seg_col = seg[:, None]

    def smalls(tail):
        bits = tail[:, :, QCOLS : QCOLS + 56].reshape(64, 56)
        gain_a = bits[:, :24].reshape(1, WIDTH).astype(F32)
        gain_b = bits[:, 24:48].reshape(1, WIDTH).astype(F32)
        kv_bias = lax.dynamic_slice_in_dim(bits[:, 48:].reshape(1, 512), (core * 2 + chip) * HEAD, HEAD, 1)
        bias = jnp.concatenate([tail[:1, 0, :QCOLS], kv_bias], axis=1).astype(F32)
        return gain_a, gain_b, bias

    gain_a1, gain_b1, bias1 = smalls(tail_first[:, :4])
    normed1, query1, kv = qkv_columns(flag, x_block1, gain_a1, qkv_first, bias1, cosine, sine)
    own1 = gathered(ffn_halves[0], "y")
    all_second = gathered(after(rows_second, kv), ("y", "z"))
    kv_mine1 = exchange(after(kv, (out_ring[1], out_ring[3])), ("y", "z")).reshape(SEQ, HEAD)
    kv_mine1, out_ring = lax.optimization_barrier((kv_mine1, out_ring))
    out_first = assemble(y_then_z, out_ring)
    kv_other1 = swap(kv_mine1, "c")
    attended1, wide1, lse1, part = attend(flag, query1, kv_mine1, kv_other1, seg_col, seg_row, out_first, 0)
    other1 = swap(after(own1, part), "c")
    mixed1, low = after_heads(after(exchange(part, ("x", "c")), other1), xin, gain_b1)
    second1 = exchange(low, ("z", "x")).reshape(256, WIDTH)
    own2 = gathered(after(ffn_halves[1], second1), "y")
    part, gate_up1 = feed(second1, own1, other1)
    pieces = exchange(part.reshape(8, 32, WIDTH), ("z", "x"))
    out_one = after_feed(pieces, mixed1)

    x_block2 = gathered(out_one, ("x", "c"))
    gain_a2, gain_b2, bias2 = smalls(tail_first[:, 4:8])
    normed2, query2, kv = qkv_columns(flag, x_block2, gain_a2, all_second, bias2, cosine, sine)
    kv_mine2 = exchange(kv, ("y", "z")).reshape(SEQ, HEAD)
    kv_other2 = swap(kv_mine2, "c")
    attended2, wide2, lse2, part = attend(flag, query2, kv_mine2, kv_other2, seg_col, seg_row, all_second, 512)
    mixed2, low = after_heads(exchange(part, ("x", "c")), out_one, gain_b2)
    second2 = exchange(low, ("z", "x")).reshape(256, WIDTH)
    other2 = swap(after(own2, second2), "c")
    cot_low = spread(after(cot, (second2, own2)), 8, ("z", "x")).reshape(256, WIDTH)
    second2 = after(second2, cot_low)
    fed2 = feed_both(second2, cot_low, own2, other2)

    def backward(grad_out, grad_low, fed, second, mixed, gain_b, xin, x_block, gain_a, normed, query, attended, wide,
                 kv_mine, kv_other, lse, weight, out_t, first, earlier=None):
        part, for_own, for_other = fed
        pieces = fed_pieces = exchange(part.reshape(8, -1, WIDTH), ("z", "x"))
        given = swap(for_other, "c")
        second_other, grad_other = swap(second, "c"), swap(grad_low, "c")
        grad_ffn = feed_grad(second, second_other, grad_low, grad_other, for_own, given)
        pieces, grad_ffn = lax.optimization_barrier((pieces, grad_ffn))
        grad_mixed, low, grad_gain_b = before_heads(pieces, mixed, gain_b, grad_out)
        grad_att = gathered(low, ("x", "c"))
        if earlier is not None:
            grad_ffn = after(grad_ffn, (earlier, grad_att))
        grad_ffn = lax.psum_scatter(grad_ffn, "y", scatter_dimension=0, tiled=True)
        grad_query, kept_half, sent_half = attend_back(
            flag, query, kv_mine, kv_other, seg_col, seg_row, lse, wide, grad_att, cosine, sine, out_t, first
        )
        grad_kv = (kept_half + swap(sent_half, "c").astype(F32)).astype(BF)
        grad_kv = exchange(grad_kv.reshape(16, HEAD, HEAD), ("y", "z"))
        grad_qkv, grad_bias, grad_gain_a, part = qkv_back(flag, grad_kv, grad_query, weight, x_block, cosine, sine)
        smalls = (grad_bias, grad_gain_a, grad_gain_b)
        factors = (normed, grad_qkv, grad_att, attended)
        if earlier is None:
            parts = smalls, weight_grad(*factors)
        else:
            parts = apart(y_then_z, factors, smalls + small_two)
            part = after(part, parts)
        pieces = exchange(part, ("x", "c"))
        grad_in, low = layer_start(pieces, xin, gain_a, grad_mixed)
        return grad_in, low, grad_ffn, parts, fed_pieces

    grad_two, low, ffn_two, attn_two, out_pieces = backward(
        cot, cot_low, fed2, second2, mixed2, gain_b2, out_one, x_block2, gain_a2, normed2, query2, attended2, wide2,
        kv_mine2, kv_other2, lse2, all_second, all_second, 512
    )
    out_two = after_feed(out_pieces, mixed2)
    grad_low = exchange(low, ("z", "x")).reshape(256, WIDTH)
    small_two, attn_two = attn_two
    grad_low = after(grad_low, attn_two)
    attn_two = after(attn_two, (ffn_two, grad_low))
    attn_two = lax.psum_scatter(attn_two.reshape(16 * 96, 896), "y", scatter_dimension=0, tiled=True)
    fed1 = feed_back(grad_low, own1, other1, gate_up1)
    grad_one, _, ffn_one, parts, _ = backward(
        grad_two, grad_low, fed1, second1, mixed1, gain_b1, xin, x_block1, gain_a1, normed1, query1, attended1, wide1,
        kv_mine1, kv_other1, lse1, qkv_first, out_first, 0, earlier=attn_two
    )
    ffn_payload = jnp.concatenate([ffn_one, ffn_two], axis=0).reshape(8, 96, FW)
    qkv_parts = sent(parts[0], "z")
    ffn_sum = exchange(after(ffn_payload, qkv_parts), ("s", "z"))
    halfway = summed(qkv_parts)
    out_parts = sent(after(parts[1], ffn_payload), "y")
    qkv_one = scatter_blocks(halfway, "y", None)
    out_one_grad = scatter_blocks(summed(out_parts), "z", ffn_sum)
    attn_one = jnp.concatenate([qkv_one, jnp.pad(out_one_grad, ((0, 16), (0, 0)))], axis=1)
    attn_two = lax.psum_scatter(after(attn_two, (ffn_one, grad_one, halfway)), "z", scatter_dimension=0, tiled=True)

    grad_gate, grad_up, grad_down = unpack(ffn_sum)
    leaving = jnp.concatenate([pick(attn_two, attn_one[:96]), attn_one[96:]], axis=0)
    given = swap(leaving, "s").astype(F32)
    main = pick(attn_one[:96], attn_two).astype(F32) + given[:96]
    row = pick(attn_one[96], attn_one[98]).astype(F32) + pick(given[96], given[98])
    gains = pick(attn_one[97], attn_one[99]).astype(F32) + pick(given[97], given[99])
    gains = jnp.concatenate([gains[:96].reshape(4, 24), gains[128:224].reshape(4, 24)], axis=1)
    payload = jnp.concatenate(
        [
            main[:, QCOLS:512].reshape(4, 24, HEAD),
            jnp.pad(gains, ((0, 0), (0, HEAD - 48)))[:, None],
            jnp.broadcast_to(row[None, None, QCOLS:512], (4, 1, HEAD)),
            jnp.zeros((4, 6, HEAD), F32),
        ],
        axis=1,
    )
    arrived = [lax.dynamic_index_in_dim(payload, member, 0, keepdims=False)]
    for step in (1, 2, 3):
        given = lax.dynamic_index_in_dim(payload, member ^ step, 0, keepdims=False)
        arrived.append(lax.ppermute(given, ("x", "c"), [(m, m ^ step) for m in range(4)]))
    arrived = jnp.stack(arrived)
    payload = jnp.stack([lax.dynamic_index_in_dim(arrived, member ^ b, 0, keepdims=False) for b in BLOCK_ORDER])
    grad_keyval = payload[:, :24].transpose(1, 0, 2).reshape(24, 512)
    gains = jnp.sum(payload[:, 24], axis=0)
    kv_bias_row = lax.dynamic_index_in_dim(payload[:, 25], lax.axis_index("y"), 0, keepdims=False)
    grad_b_keyval = lax.dynamic_slice_in_dim(kv_bias_row, (lax.axis_index("z") * 4 + member) * 8, 8, 0)

    firsts, seconds = jnp.stack([out_one, grad_one]), jnp.stack([out_two, grad_two])
    given = swap(after(pick(seconds, firsts), leaving), "s")
    rows = jnp.stack([pick(firsts, given), pick(given, seconds)], axis=1)[:, None]
    section_out, input_grad = rows[0], rows[1]

    return (
        section_out,
        input_grad,
        gains[None, :24],
        main[None, :, :QCOLS],
        row[None, :QCOLS],
        grad_keyval[None],
        grad_b_keyval[None],
        main[:, 512:].T[None],
        gains[None, 24:48],
        grad_gate[None],
        grad_up[None],
        grad_down[None],
    )


def solution(mesh):
    fine = Mesh(np.asarray(mesh.devices).reshape(2, 4, 4, 2, 2), AXES)
    block, member = ("y", "z"), ("x", "c")
    every = block + member
    tokens = P(None, every, None)
    split = P("s", every)
    columns = P("s", block, member)
    rows = P("s", member, block)
    keyval = P("s", every, None)
    outs = P("s", None, every, None)
    return jax.shard_map(
        local,
        mesh=fine,
        in_specs=(
            tokens, tokens, P(), split, columns, P("s", member), keyval, split, rows, split, columns, columns, rows,
        ),
        out_specs=(
            outs, outs, split, columns, P("s", member), keyval, split, rows, split, columns, columns, rows,
        ),
        check_vma=False,
    )
```
